32 devices in a mesh: dp: 32 (over z, y, x, core).
Axes of the slice: x: 2, y: 2, z: 4, core: 2. Of those that a mesh axis runs over, the one named last changes fastest.
Arguments:
- short_input: bfloat16 [96, 128, 1024], P('dp'), may hold values from -6 to 6
- short_lengths: int32 [96], P('dp'), may hold values from 32 to 128
- short_cotangent: bfloat16 [96, 128, 1024], P('dp'), may hold values from -6 to 6
- long_input: bfloat16 [32, 512, 1024], P('dp'), may hold values from -6 to 6
- long_lengths: int32 [32], P('dp'), may hold values from 128 to 512
- long_cotangent: bfloat16 [32, 512, 1024], P('dp'), may hold values from -6 to 6
- packed_weight: bfloat16 [1024, 3072], P('dp'), may hold values from -0.1875 to 0.1875
- output_weight: bfloat16 [1024, 1024], P('dp'), may hold values from -0.75 to 0.75
- inner_weight: bfloat16 [1024, 4096], P('dp'), may hold values from -0.1875 to 0.1875
- down_weight: bfloat16 [4096, 1024], P('dp'), may hold values from -0.09375 to 0.09375
- first_gain: float32 [1024], replicated, may hold values from 0.1 to 1.9
- second_gain: float32 [1024], replicated, may hold values from 0.1 to 1.9
- query_bias: float32 [1024], replicated, may hold values from -3 to 3
- value_bias: float32 [1024], replicated, may hold values from -3 to 3
- output_bias: float32 [1024], replicated, may hold values from -3 to 3
- inner_bias: float32 [4096], replicated, may hold values from -3 to 3
- down_bias: float32 [1024], replicated, may hold values from -3 to 3
- first_beta: float32 [1024], replicated, may hold values from -3 to 3
- second_beta: float32 [1024], replicated, may hold values from -3 to 3
Outputs:
- short_output: bfloat16 [96, 128, 1024], P('dp')
- short_input_grad: bfloat16 [96, 128, 1024], P('dp')
- long_output: bfloat16 [32, 512, 1024], P('dp')
- long_input_grad: bfloat16 [32, 512, 1024], P('dp')
- query_bias_grad: float32 [1024], replicated
- value_bias_grad: float32 [1024], replicated
- output_bias_grad: float32 [1024], replicated
- inner_bias_grad: float32 [4096], replicated
- down_bias_grad: float32 [1024], replicated
- first_beta_grad: float32 [1024], replicated
- second_beta_grad: float32 [1024], replicated
The draws below stay inside these ranges and needn't reach their ends.
All inputs are finite; a program needn't handle non-finite values.
Results may differ from the reference program's by a relative error of at most 0.014.
Values may be sent and summed in bfloat16 or wider, within the bound.
No kernel may reach another device: no remote copies, remote signals or barrier semaphores. Data moves between devices by JAX's collectives and lax.ppermute only.
A program may use at most 192 MiB of HBM per device.

```python
import math
import jax
import jax.numpy as jnp
from jax import lax

D = 1024
HEADS = 16
HEAD_DIM = 64
FF = 4096
SHORT_LEN = 128
LONG_LEN = 512
SHORT_SEQS = 96
LONG_SEQS = 32


def with_ends(drawn, stream_key, least, top_value):
    dims = drawn.shape
    index_at = [jax.random.randint(jax.random.fold_in(stream_key, axis), (), 0, dims[axis]) for axis in range(len(dims))]
    drawn = drawn.at[tuple(index_at)].set(least)
    longest = dims.index(max(dims))
    index_at[longest] = (index_at[longest] + 1) % dims[longest]
    return drawn.at[tuple(index_at)].set(top_value)


def steps_of(key, extent, split, least, top_value):
    factor_of, own = 1.0, jax.random.fold_in(key, 6)
    for position, parts in split:
        heights = jnp.exp(jax.random.uniform(jax.random.fold_in(own, position), (parts,), jnp.float32, least / len(split), top_value / len(split)))
        factor_of = factor_of * jnp.repeat(heights, extent[position] // parts).reshape([-1 if axis == position else 1 for axis in range(len(extent))])
    return factor_of


def noise(rng, dims, deviation, bound, split=(), kind=jnp.bfloat16):
    drawn = jax.random.normal(rng, dims, jnp.float32) * deviation
    if len(split) > 0:
        drawn = steps_of(rng, dims, split, -0.22, 0.18) * drawn
    return jnp.clip(drawn, min=-bound, max=bound).astype(kind)


def setup_inputs(seed: int = 0) -> dict:
    streams_of = jax.random.split(jax.random.key(seed), 20)
    short_input = noise(streams_of[0], (SHORT_SEQS, SHORT_LEN, D), 1.0, 6.0, ((0, 32),))
    short_lengths = with_ends(jax.random.randint(streams_of[1], (SHORT_SEQS,), SHORT_LEN // 4, SHORT_LEN + 1), jax.random.fold_in(streams_of[1], 1), SHORT_LEN // 4, SHORT_LEN).astype(jnp.int32)
    short_cotangent = noise(streams_of[2], (SHORT_SEQS, SHORT_LEN, D), 1.0, 6.0, ((0, 32),))
    long_input = noise(streams_of[3], (LONG_SEQS, LONG_LEN, D), 1.0, 6.0, ((0, 32),))
    long_lengths = with_ends(jax.random.randint(streams_of[4], (LONG_SEQS,), LONG_LEN // 4, LONG_LEN + 1), jax.random.fold_in(streams_of[4], 1), LONG_LEN // 4, LONG_LEN).astype(jnp.int32)
    long_cotangent = noise(streams_of[5], (LONG_SEQS, LONG_LEN, D), 1.0, 6.0, ((0, 32),))
    packed_weight = noise(streams_of[6], (D, 3 * D), D ** -0.5, 0.1875, ((0, 32),))
    output_weight = noise(streams_of[7], (D, D), (D // 16) ** -0.5, 0.75, ((0, 32),))
    inner_weight = noise(streams_of[8], (D, FF), D ** -0.5, 0.1875, ((0, 32),))
    down_weight = noise(streams_of[9], (FF, D), FF ** -0.5, 0.09375, ((0, 32),))
    first_gain = jnp.clip(1.0 + 0.18 * jax.random.normal(streams_of[10], (D,), jnp.float32), 0.1, 1.9)
    second_gain = jnp.clip(1.0 + 0.18 * jax.random.normal(streams_of[11], (D,), jnp.float32), 0.1, 1.9)
    query_bias = noise(streams_of[12], (D,), 0.5, 3.0, (), jnp.float32)
    value_bias = noise(streams_of[13], (D,), 0.5, 3.0, (), jnp.float32)
    output_bias = noise(streams_of[14], (D,), 0.5, 3.0, (), jnp.float32)
    inner_bias = noise(streams_of[15], (FF,), 0.5, 3.0, (), jnp.float32)
    down_bias = noise(streams_of[16], (D,), 0.5, 3.0, (), jnp.float32)
    first_beta = noise(streams_of[17], (D,), 0.5, 3.0, (), jnp.float32)
    second_beta = noise(streams_of[18], (D,), 0.5, 3.0, (), jnp.float32)
    return {"short_input": short_input, "short_lengths": short_lengths, "short_cotangent": short_cotangent, "long_input": long_input, "long_lengths": long_lengths, "long_cotangent": long_cotangent, "packed_weight": packed_weight, "output_weight": output_weight, "inner_weight": inner_weight, "down_weight": down_weight, "first_gain": first_gain, "second_gain": second_gain, "query_bias": query_bias, "value_bias": value_bias, "output_bias": output_bias, "inner_bias": inner_bias, "down_bias": down_bias, "first_beta": first_beta, "second_beta": second_beta}


@jax.custom_vjp
def low(v):
    return lax.optimization_barrier(v.astype(jnp.bfloat16)).astype(jnp.float32)

@jax.custom_vjp
def low_back(v):
    return v

def low_keep(v):
    return (low(v), None)

def low_pass(kept, grad):
    return (grad,)

def back_keep(v):
    return (v, None)

def back_low(kept, grad):
    return (low(grad),)
low.defvjp(low_keep, low_pass)
low_back.defvjp(back_keep, back_low)

def rounded_both(value_block):
    return low_back(low(value_block))

def norm_rows(summed, gain, beta):
    center = summed - lax.optimization_barrier(jnp.mean(summed, axis=-1, keepdims=True))
    spread = lax.optimization_barrier(jnp.mean(center * center, axis=-1, keepdims=True))
    return center * lax.rsqrt(spread + 1e-06) * gain + beta

def layer(inputs, lengths, matrices, gains, vectors):
    packed_w, output_w, inner_w, down_w = matrices
    first_gain, second_gain = gains
    query_bias, value_bias, output_bias, inner_bias, down_bias, first_beta, second_beta = vectors
    high = lax.Precision.HIGHEST
    seq_count, length, model_width = inputs.shape
    usable = jnp.arange(length)[None, :] < lengths[:, None]
    row_keep = usable.astype(jnp.float32)[..., None]
    tokens = inputs * row_keep
    packed = jnp.einsum('bld,de->ble', tokens, packed_w, precision=high)
    shape4 = (seq_count, length, HEADS, HEAD_DIM)
    queries = rounded_both(packed[..., :model_width] + query_bias).reshape(shape4)
    keys_all = rounded_both(packed[..., model_width:2 * model_width]).reshape(shape4)
    values = rounded_both(packed[..., 2 * model_width:] + value_bias).reshape(shape4)
    scores = low_back(jnp.einsum('bqhe,bkhe->bhqk', queries, keys_all, precision=high) * HEAD_DIM ** (-0.5))
    scores = jnp.where(usable[:, None, None, :], scores, -1e+30)
    attention_probs = low(jax.nn.softmax(scores, axis=-1))
    attention_mixture = jnp.einsum('bhqk,bkhe->bqhe', attention_probs, values, precision=high)
    attention_mixture = rounded_both(attention_mixture.reshape(seq_count, length, model_width))
    branch = low_back(jnp.einsum('bld,de->ble', attention_mixture, output_w, precision=high) + output_bias)
    first_out = norm_rows(tokens + branch, first_gain, first_beta)
    inner_sum = low_back(jnp.einsum('bld,df->blf', low(first_out), inner_w, precision=high) + inner_bias)
    active = low(jax.nn.gelu(inner_sum, approximate=False))
    second = low_back(jnp.einsum('blf,fd->bld', active, down_w, precision=high) + down_bias)
    result = norm_rows(first_out + second, second_gain, second_beta)
    return result * row_keep

def run_bucket(inputs, lengths, cotangent, matrices, gains, vectors):
    seq_count, length, model_width = inputs.shape
    group = math.gcd(seq_count, max(1, 4096 // length))
    blocks = seq_count // group
    inputs_f = inputs.astype(jnp.float32).reshape(blocks, group, length, model_width)
    cot_f = cotangent.astype(jnp.float32).reshape(blocks, group, length, model_width)
    lens = lengths.reshape(blocks, group)

    def one_block(totals, block):
        block_in, block_len, block_cot = block

        def forward(tokens, bias_set):
            return layer(tokens, block_len, matrices, gains, bias_set)
        result, pull = jax.vjp(forward, block_in, vectors)
        grad_in, grad_bias = pull(block_cot)
        totals = jax.tree.map(lambda left, right: left + right, totals, grad_bias)
        return (totals, (result.astype(jnp.bfloat16), grad_in.astype(jnp.bfloat16)))
    zeros = jax.tree.map(jnp.zeros_like, vectors)
    totals, (results, grads) = lax.scan(one_block, zeros, (inputs_f, lens, cot_f))
    shape3 = (seq_count, length, model_width)
    return (results.reshape(shape3), grads.reshape(shape3), totals)

def reference(short_input, short_lengths, short_cotangent, long_input, long_lengths, long_cotangent, packed_weight, output_weight, inner_weight, down_weight, first_gain, second_gain, query_bias, value_bias, output_bias, inner_bias, down_bias, first_beta, second_beta):
    matrices = tuple((item.astype(jnp.float32) for item in (packed_weight, output_weight, inner_weight, down_weight)))
    gains = (first_gain.astype(jnp.float32), second_gain.astype(jnp.float32))
    vectors = tuple((item.astype(jnp.float32) for item in (query_bias, value_bias, output_bias, inner_bias, down_bias, first_beta, second_beta)))
    short_out, short_grad, short_sums = run_bucket(short_input, short_lengths, short_cotangent, matrices, gains, vectors)
    long_out, long_grad, long_sums = run_bucket(long_input, long_lengths, long_cotangent, matrices, gains, vectors)
    sums = [left + right for left, right in zip(short_sums, long_sums)]
    return (short_out, short_grad, long_out, long_grad, sums[0], sums[1], sums[2], sums[3], sums[4], sums[5], sums[6])
```

```python
from functools import partial

import jax
import jax.numpy as jnp
from jax import lax
from jax.experimental import pallas as pl
from jax.experimental.pallas import tpu as pltpu
from jax.sharding import PartitionSpec as P

HEADS = 16
HEAD_DIM = 64
BF = jnp.bfloat16
F32 = jnp.float32
VMEM_BYTES = 60 * 1024 * 1024


def dot(left, right):
    return lax.dot_general(left, right, (((1,), (0,)), ((), ())), preferred_element_type=F32)


def dot_t(left, right):
    return lax.dot_general(left, right, (((1,), (1,)), ((), ())), preferred_element_type=F32)


def sequences(short_seqs, short_len, long_seqs, long_len):
    spans = [(i * short_len, short_len) for i in range(short_seqs)]
    base = short_seqs * short_len
    return spans, [(base + i * long_len, long_len) for i in range(long_seqs)]


def row_mask(short_lengths, long_lengths, shape):
    short_seqs, short_len, long_seqs, long_len = shape
    pieces = []
    for count, length, refs in (
        (short_seqs, short_len, short_lengths),
        (long_seqs, long_len, long_lengths),
    ):
        for i in range(count):
            rows = lax.broadcasted_iota(jnp.int32, (length, 1), 0)
            pieces.append(jnp.where(rows < refs[i], 1.0, 0.0).astype(F32))
    return jnp.concatenate(pieces, axis=0)


def head_lanes(block, half):
    lanes = lax.broadcasted_iota(jnp.int32, block.shape, 1)
    keep = lanes < HEAD_DIM if half == 0 else lanes >= HEAD_DIM
    return jnp.where(keep, block, jnp.zeros_like(block))


def flip(block):
    return jnp.transpose(block, (1, 0))


def attention_forward_kernel(
    shape, short_lengths, long_lengths, short_x, long_x, wq, wk, wv, wo, qb, vb, ob,
    q_out, k_out, v_out, short_p, long_p, mixed_t, xhat_out, rstd_out, x_all, mixed,
):
    step = pl.program_id(0)
    steps = pl.num_programs(0)
    short_seqs, short_len, long_seqs, long_len = shape
    base = short_seqs * short_len
    width = wq.shape[1]
    short_spans, long_spans = sequences(*shape)

    @pl.when(step == 0)
    def _():
        x_all[:base, :] = short_x[...]
        x_all[base:, :] = long_x[...]

    x = x_all[...]
    q_out[...] = ((dot(x, wq[...]) + qb[...]).astype(BF).astype(F32) * HEAD_DIM ** (-0.5)).astype(BF)
    k_out[...] = dot(x, wk[...]).astype(BF)
    v_out[...] = (dot(x, wv[...]) + vb[...]).astype(BF)
    for pair in range(width // 128):
        lanes = slice(128 * pair, 128 * pair + 128)
        v_t = flip(v_out[:, lanes])
        for which, spans, refs, probs in (
            (0, short_spans, short_lengths, short_p),
            (1, long_spans, long_lengths, long_p),
        ):
            for seq, (start, length) in enumerate(spans):
                k2 = k_out[start : start + length, lanes]
                rows = lax.broadcasted_iota(jnp.int32, (length, 1), 0)
                usable = rows < refs[seq]
                block = min(length, 256)
                for half in range(2):
                    k_head = head_lanes(k2, half)
                    v_head = v_t[HEAD_DIM * half : HEAD_DIM * half + HEAD_DIM, start : start + length]
                    for at in range(0, length, block):
                        scores = dot_t(k_head, q_out[start + at : start + at + block, lanes])
                        scores = jnp.where(usable, scores, -1e30)
                        top = jnp.max(scores, axis=0, keepdims=True)
                        powers = jnp.exp(scores - top)
                        total = jnp.sum(powers, axis=0, keepdims=True)
                        prob = (powers * (1.0 / total)).astype(BF)
                        probs[seq, 2 * pair + half, :, at : at + block] = prob
                        feature = 128 * pair + HEAD_DIM * half
                        mixed_t[feature : feature + HEAD_DIM, start + at : start + at + block] = dot(v_head, prob)
        offset = pl.multiple_of(step * width + 128 * pair, 128)
        mixed[:, pl.ds(offset, 128)] = flip(mixed_t[lanes, :]).astype(BF)

    @pl.when(step == steps - 1)
    def _():
        first_sum = x_all[...].astype(F32) + (dot(mixed[...], wo[...]) + ob[...])
        center = first_sum - jnp.mean(first_sum, axis=-1, keepdims=True)
        spread = jnp.mean(center * center, axis=-1, keepdims=True)
        rstd = lax.rsqrt(spread + 1e-06)
        xhat_out[...] = center * rstd
        rstd_out[...] = rstd


def attention_forward(shape, lengths, xs, packed_w, output_w, vectors):
    short_seqs, short_len, long_seqs, long_len = shape
    rows = short_seqs * short_len + long_seqs * long_len
    width = xs[0].shape[1]
    block = 256
    heads = block // HEAD_DIM
    steps = width // block
    whole = lambda shp: pl.BlockSpec(shp, lambda j: (0,) * len(shp))
    smem = pl.BlockSpec(memory_space=pltpu.SMEM)
    column = lambda off: pl.BlockSpec((width, block), lambda j: (0, j + off * steps))
    row_block = pl.BlockSpec((1, block), lambda j: (0, j))
    out_col = pl.BlockSpec((rows, block), lambda j: (0, j))
    return pl.pallas_call(
        partial(attention_forward_kernel, shape),
        grid=(steps,),
        in_specs=[
            smem, smem, whole(xs[0].shape), whole(xs[1].shape),
            column(0), column(1), column(2), whole((width, width)),
            row_block, row_block, whole((1, width)),
        ],
        out_specs=[
            out_col, out_col, out_col,
            pl.BlockSpec((short_seqs, heads, short_len, short_len), lambda j: (0, j, 0, 0)),
            pl.BlockSpec((long_seqs, heads, long_len, long_len), lambda j: (0, j, 0, 0)),
            pl.BlockSpec((block, rows), lambda j: (j, 0)),
            whole((rows, width)), whole((rows, 1)),
        ],
        out_shape=[
            jax.ShapeDtypeStruct((rows, width), BF),
            jax.ShapeDtypeStruct((rows, width), BF),
            jax.ShapeDtypeStruct((rows, width), BF),
            jax.ShapeDtypeStruct((short_seqs, HEADS, short_len, short_len), BF),
            jax.ShapeDtypeStruct((long_seqs, HEADS, long_len, long_len), BF),
            jax.ShapeDtypeStruct((width, rows), F32),
            jax.ShapeDtypeStruct((rows, width), F32),
            jax.ShapeDtypeStruct((rows, 1), F32),
        ],
        scratch_shapes=[pltpu.VMEM((rows, width), BF), pltpu.VMEM((rows, width), BF)],
        compiler_params=pltpu.CompilerParams(vmem_limit_bytes=VMEM_BYTES),
        name="attention_forward",
    )(*lengths, *xs, packed_w, packed_w, packed_w, output_w, vectors["query_bias"], vectors["value_bias"], vectors["output_bias"])


def gelu_and_slope(value):
    density = jnp.exp(value * value * -0.5)
    t = 1.0 / (1.0 + (0.3275911 * 0.5 ** 0.5) * jnp.abs(value))
    poly = t * (0.254829592 + t * (-0.284496736 + t * (1.421413741 + t * (-1.453152027 + t * 1.061405429))))
    tail = 0.5 * poly * density
    share = jnp.where(value < 0.0, tail, 1.0 - tail)
    return value * share, share + value * (density * 0.3989422804014327)


def inner_kernel(xhat, gain, beta, wi, bi, active, slope, first):
    @pl.when(pl.program_id(0) == 0)
    def _():
        first[...] = (xhat[...] * gain[...] + beta[...]).astype(BF)

    value = dot(first[...], wi[...]) + bi[...]
    act, slp = gelu_and_slope(value)
    active[...] = act.astype(BF)
    slope[...] = slp.astype(BF)


def inner_forward(xhat, gain, beta, inner_w, inner_bias, block=512):
    rows, width = xhat.shape
    units = inner_w.shape[1]
    whole = lambda shp: pl.BlockSpec(shp, lambda j: (0,) * len(shp))
    col = pl.BlockSpec((rows, block), lambda j: (0, j))
    return pl.pallas_call(
        inner_kernel,
        grid=(units // block,),
        in_specs=[
            whole((rows, width)), whole((1, width)), whole((1, width)),
            pl.BlockSpec((width, block), lambda j: (0, j)), pl.BlockSpec((1, block), lambda j: (0, j)),
        ],
        out_specs=[col, col],
        out_shape=[jax.ShapeDtypeStruct((rows, units), BF)] * 2,
        scratch_shapes=[pltpu.VMEM((rows, width), BF)],
        compiler_params=pltpu.CompilerParams(vmem_limit_bytes=VMEM_BYTES),
        name="inner_forward",
    )(xhat, gain, beta, inner_w, inner_bias)


def norm_gradient(grad, xhat, rstd, gain):
    scaled = grad * gain
    mean = jnp.mean(scaled, axis=-1, keepdims=True)
    along = jnp.mean(scaled * xhat, axis=-1, keepdims=True)
    return rstd * (scaled - mean - xhat * along)


def feed_kernel(
    shape, steps, short_lengths, long_lengths, xhat, rstd, short_ct, long_ct, active, slope, wd, wi, wo,
    gain1, beta1, gain2, beta2, down_bias,
    short_out, long_out, grad_mixed, grad_first_sum, second_beta_sum, down_sum, inner_sum, first_beta_sum, output_sum,
    total, grad_down,
):
    step = pl.program_id(0)
    short_seqs, short_len, long_seqs, long_len = shape
    base = short_seqs * short_len

    @pl.when(step == 0)
    def _():
        total[...] = xhat[...] * gain1[...] + beta1[...] + down_bias[...]

    @pl.when(step < steps)
    def _():
        total[...] += dot(active[...], wd[...])

    @pl.when(step == steps - 1)
    def _():
        keep = row_mask(short_lengths, long_lengths, shape)
        second = total[...]
        center = second - jnp.mean(second, axis=-1, keepdims=True)
        spread = jnp.mean(center * center, axis=-1, keepdims=True)
        rstd2 = lax.rsqrt(spread + 1e-06)
        xhat2 = center * rstd2
        output = ((xhat2 * gain2[...] + beta2[...]) * keep).astype(BF)
        short_out[...] = output[:base]
        long_out[...] = output[base:]
        grad_out = jnp.concatenate([short_ct[...], long_ct[...]], axis=0).astype(F32) * keep
        second_beta_sum[...] = jnp.sum(grad_out, axis=0, keepdims=True)
        grad_second = norm_gradient(grad_out, xhat2, rstd2, gain2[...])
        low = grad_second.astype(BF)
        grad_down[...] = low
        down_sum[...] = jnp.sum(low.astype(F32), axis=0, keepdims=True)
        total[...] = grad_second

    @pl.when(step >= steps)
    def _():
        grad_inner = (dot_t(grad_down[...], wd[...]) * slope[...].astype(F32)).astype(BF)
        inner_sum[...] = jnp.sum(grad_inner.astype(F32), axis=0, keepdims=True)
        total[...] += dot_t(grad_inner, wi[...])

    @pl.when(step == 2 * steps - 1)
    def _():
        grad_first = total[...]
        first_beta_sum[...] = jnp.sum(grad_first, axis=0, keepdims=True)
        result = norm_gradient(grad_first, xhat[...], rstd[...], gain1[...])
        grad_first_sum[...] = result
        branch = result.astype(BF)
        output_sum[...] = jnp.sum(branch.astype(F32), axis=0, keepdims=True)
        grad_mixed[...] = dot_t(branch, wo[...]).astype(BF)


def feed_back(shape, lengths, xhat, rstd, cts, active, slope, down_w, inner_w, output_w, vectors, block=512):
    rows, width = xhat.shape
    units = down_w.shape[0]
    steps = units // block
    whole = lambda shp: pl.BlockSpec(shp, lambda j: (0,) * len(shp))
    smem = pl.BlockSpec(memory_space=pltpu.SMEM)
    vec = whole((1, width))
    late = lambda j: jnp.maximum(j - steps, 0)
    vector_out = jax.ShapeDtypeStruct((1, width), F32)
    return pl.pallas_call(
        partial(feed_kernel, shape, steps),
        grid=(2 * steps,),
        in_specs=[
            smem, smem, whole((rows, width)), whole((rows, 1)), whole(cts[0].shape), whole(cts[1].shape),
            pl.BlockSpec((rows, block), lambda j: (0, jnp.minimum(j, steps - 1))),
            pl.BlockSpec((rows, block), lambda j: (0, late(j))),
            pl.BlockSpec((block, width), lambda j: (lax.rem(j, steps), 0)),
            pl.BlockSpec((width, block), lambda j: (0, late(j))),
            whole((width, width)), vec, vec, vec, vec, vec,
        ],
        out_specs=[
            whole(cts[0].shape), whole(cts[1].shape), whole((rows, width)), whole((rows, width)),
            vec, vec, pl.BlockSpec((1, block), lambda j: (0, late(j))), vec, vec,
        ],
        out_shape=[
            jax.ShapeDtypeStruct(cts[0].shape, BF), jax.ShapeDtypeStruct(cts[1].shape, BF),
            jax.ShapeDtypeStruct((rows, width), BF), jax.ShapeDtypeStruct((rows, width), F32),
            vector_out, vector_out, jax.ShapeDtypeStruct((1, units), F32), vector_out, vector_out,
        ],
        scratch_shapes=[pltpu.VMEM((rows, width), F32), pltpu.VMEM((rows, width), BF)],
        compiler_params=pltpu.CompilerParams(vmem_limit_bytes=VMEM_BYTES),
        name="feed_back",
    )(
        *lengths, xhat, rstd, *cts, active, slope, down_w, inner_w, output_w,
        vectors["first_gain"], vectors["first_beta"], vectors["second_gain"], vectors["second_beta"], vectors["down_bias"],
    )


def attention_backward_kernel(
    shape, short_lengths, long_lengths, q, k, v, gm, short_p, long_p, mixed_t, wq, wk, wv, grad_first_sum,
    short_grad, long_grad, query_sum, value_sum, grad_packed, total,
):
    step = pl.program_id(0)
    steps = pl.num_programs(0)
    short_seqs, short_len, long_seqs, long_len = shape
    base = short_seqs * short_len
    width = q.shape[1]
    short_spans, long_spans = sequences(*shape)
    scale = HEAD_DIM ** (-0.5)
    for pair in range(width // 128):
        lanes = slice(128 * pair, 128 * pair + 128)
        gm_t = flip(gm[:, lanes]).astype(F32)
        k_t = flip(k[:, lanes])
        product = gm_t * mixed_t[lanes, :]
        delta = [jnp.sum(product[HEAD_DIM * h : HEAD_DIM * h + HEAD_DIM], axis=0, keepdims=True) for h in range(2)]
        for spans, probs in ((short_spans, short_p), (long_spans, long_p)):
            for seq, (start, length) in enumerate(spans):
                here = slice(start, start + length)
                gm2, v2, q2 = gm[here, lanes], v[here, lanes], q[here, lanes]
                grad_value = grad_key = None
                grad_query_t = []
                for half in range(2):
                    prob = probs[seq, 2 * pair + half]
                    grad_p = dot_t(head_lanes(v2, half), gm2)
                    grad_s = (prob.astype(F32) * (grad_p - delta[half][:, here])).astype(BF)
                    dv = dot(prob, head_lanes(gm2, half))
                    dk = dot(grad_s, head_lanes(q2, half))
                    grad_value = dv if half == 0 else grad_value + dv
                    grad_key = dk if half == 0 else grad_key + dk
                    grad_query_t.append(dot(k_t[HEAD_DIM * half : HEAD_DIM * half + HEAD_DIM, here], grad_s))
                grad_packed[here, 128 * pair : 128 * pair + 128] = (
                    flip(jnp.concatenate(grad_query_t, axis=0)) * scale
                ).astype(BF)
                grad_packed[here, width + 128 * pair : width + 128 * pair + 128] = grad_key.astype(BF)
                grad_packed[here, 2 * width + 128 * pair : 2 * width + 128 * pair + 128] = grad_value.astype(BF)
    query_sum[...] = jnp.sum(grad_packed[:, :width].astype(F32), axis=0, keepdims=True)
    value_sum[...] = jnp.sum(grad_packed[:, 2 * width :].astype(F32), axis=0, keepdims=True)
    part = (
        dot_t(grad_packed[:, :width], wq[...])
        + dot_t(grad_packed[:, width : 2 * width], wk[...])
        + dot_t(grad_packed[:, 2 * width :], wv[...])
    )

    @pl.when(step == 0)
    def _():
        total[...] = grad_first_sum[...] + part

    @pl.when(step > 0)
    def _():
        total[...] += part

    @pl.when(step == steps - 1)
    def _():
        keep = row_mask(short_lengths, long_lengths, shape)
        result = (total[...] * keep).astype(BF)
        short_grad[...] = result[:base]
        long_grad[...] = result[base:]


def attention_backward(shape, lengths, q, k, v, gm, short_p, long_p, mixed_t, packed_w, grad_first_sum):
    short_seqs, short_len, long_seqs, long_len = shape
    rows, width = q.shape
    block = 256
    heads = block // HEAD_DIM
    steps = width // block
    base = short_seqs * short_len
    whole = lambda shp: pl.BlockSpec(shp, lambda j: (0,) * len(shp))
    smem = pl.BlockSpec(memory_space=pltpu.SMEM)
    column = lambda off: pl.BlockSpec((width, block), lambda j: (0, j + off * steps))
    col = pl.BlockSpec((rows, block), lambda j: (0, j))
    vec = pl.BlockSpec((1, block), lambda j: (0, j))
    return pl.pallas_call(
        partial(attention_backward_kernel, shape),
        grid=(steps,),
        in_specs=[
            smem, smem, col, col, col, col,
            pl.BlockSpec((short_seqs, heads, short_len, short_len), lambda j: (0, j, 0, 0)),
            pl.BlockSpec((long_seqs, heads, long_len, long_len), lambda j: (0, j, 0, 0)),
            pl.BlockSpec((block, rows), lambda j: (j, 0)),
            column(0), column(1), column(2), whole((rows, width)),
        ],
        out_specs=[whole((base, width)), whole((rows - base, width)), vec, vec],
        out_shape=[
            jax.ShapeDtypeStruct((base, width), BF), jax.ShapeDtypeStruct((rows - base, width), BF),
            jax.ShapeDtypeStruct((1, width), F32), jax.ShapeDtypeStruct((1, width), F32),
        ],
        scratch_shapes=[pltpu.VMEM((rows, 3 * block), BF), pltpu.VMEM((rows, width), F32)],
        compiler_params=pltpu.CompilerParams(vmem_limit_bytes=VMEM_BYTES),
        name="attention_backward",
    )(*lengths, q, k, v, gm, short_p, long_p, mixed_t, packed_w, packed_w, packed_w, grad_first_sum)


def local(
    short_input, short_lengths, short_cotangent, long_input, long_lengths, long_cotangent,
    packed_weight, output_weight, inner_weight, down_weight,
    first_gain, second_gain, query_bias, value_bias, output_bias, inner_bias, down_bias, first_beta, second_beta,
):
    short_seqs, short_len, width = short_input.shape
    long_seqs, long_len, _ = long_input.shape
    shape = (short_seqs, short_len, long_seqs, long_len)
    lengths = (short_lengths, long_lengths)
    vectors = dict(
        first_gain=first_gain, second_gain=second_gain, query_bias=query_bias, value_bias=value_bias,
        output_bias=output_bias, inner_bias=inner_bias, down_bias=down_bias, first_beta=first_beta, second_beta=second_beta,
    )
    vectors = {name: item.reshape(1, -1) for name, item in vectors.items()}
    xs = (short_input.reshape(-1, width), long_input.reshape(-1, width))
    cts = (short_cotangent.reshape(-1, width), long_cotangent.reshape(-1, width))
    packed_w, output_w, inner_w, down_w = gather_all(packed_weight, output_weight, inner_weight, down_weight)
    q, k, v, short_p, long_p, mixed_t, xhat, rstd = attention_forward(shape, lengths, xs, packed_w, output_w, vectors)
    active, slope = inner_forward(xhat, vectors["first_gain"], vectors["first_beta"], inner_w, vectors["inner_bias"])
    (
        short_out, long_out, gm, grad_first_sum, second_beta_sum, down_sum, inner_sum, first_beta_sum, output_sum,
    ) = feed_back(shape, lengths, xhat, rstd, cts, active, slope, down_w, inner_w, output_w, vectors)
    short_grad, long_grad, query_sum, value_sum = attention_backward(
        shape, lengths, q, k, v, gm, short_p, long_p, mixed_t, packed_w, grad_first_sum
    )
    sums = sum_all(jnp.concatenate(
        [query_sum, value_sum, output_sum, inner_sum, down_sum, first_beta_sum, second_beta_sum], axis=1
    ).reshape(-1))
    outs = []
    at = 0
    for size in (width, width, width, inner_bias.shape[0], width, width, width):
        outs.append(lax.slice_in_dim(sums, at, at + size))
        at += size
    return (
        short_out.reshape(short_input.shape), short_grad.reshape(short_input.shape),
        long_out.reshape(long_input.shape), long_grad.reshape(long_input.shape), *outs,
    )


def gather_all(*shards):
    return [lax.all_gather(shard, "dp", axis=0, tiled=True) for shard in shards]


def sum_all(vector):
    return lax.psum(vector, "dp")


def solution(mesh):
    rows = P("dp", None, None)
    in_specs = (rows, P("dp"), rows, rows, P("dp"), rows) + (P("dp", None),) * 4 + (P(),) * 9
    out_specs = (rows,) * 4 + (P(),) * 7
    return jax.shard_map(local, mesh=mesh, in_specs=in_specs, out_specs=out_specs, check_vma=False)
```

```python
from functools import partial

import jax
import jax.numpy as jnp
from jax import lax
from jax.experimental import pallas as pl
from jax.experimental.pallas import tpu as pltpu
from jax.sharding import PartitionSpec as P

HEADS = 16
HEAD_DIM = 64
BF = jnp.bfloat16
F32 = jnp.float32
VMEM_BYTES = 60 * 1024 * 1024


def dot(left, right):
    return lax.dot_general(left, right, (((1,), (0,)), ((), ())), preferred_element_type=F32)


def dot_t(left, right):
    return lax.dot_general(left, right, (((1,), (1,)), ((), ())), preferred_element_type=F32)


def sequences(short_seqs, short_len, long_seqs, long_len):
    spans = [(i * short_len, short_len) for i in range(short_seqs)]
    base = short_seqs * short_len
    return spans, [(base + i * long_len, long_len) for i in range(long_seqs)]


def row_mask(short_lengths, long_lengths, shape):
    short_seqs, short_len, long_seqs, long_len = shape
    pieces = []
    for count, length, refs in (
        (short_seqs, short_len, short_lengths),
        (long_seqs, long_len, long_lengths),
    ):
        for i in range(count):
            rows = lax.broadcasted_iota(jnp.int32, (length, 1), 0)
            pieces.append(jnp.where(rows < refs[i], 1.0, 0.0).astype(F32))
    return jnp.concatenate(pieces, axis=0)


def head_lanes(block, half):
    lanes = lax.broadcasted_iota(jnp.int32, block.shape, 1)
    keep = lanes < HEAD_DIM if half == 0 else lanes >= HEAD_DIM
    return jnp.where(keep, block, jnp.zeros_like(block))


def flip(block):
    return jnp.transpose(block, (1, 0))


def attention_forward_kernel(
    shape, slots, me, short_lengths, long_lengths, short_x, long_x, *refs,
):
    pieces, refs = refs[: 3 * len(slots)], refs[3 * len(slots) :]
    (
        qb, vb, ob, q_out, k_out, v_out, short_p, long_p, mixed_t, xhat_out, rstd_out, packed_out, output_out,
        x_all, mixed, packed, wo, in_sems, out_sems,
    ) = refs
    step = pl.program_id(0)
    steps = pl.num_programs(0)
    short_seqs, short_len, long_seqs, long_len = shape
    base = short_seqs * short_len
    width = q_out.shape[1]
    half_width = packed.shape[2]
    short_spans, long_spans = sequences(*shape)
    targets = (packed.at[0], packed.at[1], wo)

    @pl.when(step == 0)
    def _():
        for part in range(3):
            for ref, masks in zip(pieces[part::3], slots):
                tall = ref.shape[0] // len(masks)
                for slot, mask in enumerate(masks):
                    mask = jnp.where(jnp.bitwise_and(me[0], 1) == 0, mask[0], mask[1])
                    place = pl.multiple_of(jnp.bitwise_xor(me[0], mask) * tall, tall)
                    pltpu.make_async_copy(
                        ref.at[pl.ds(slot * tall, tall)], targets[part].at[pl.ds(place, tall)], in_sems.at[part]
                    ).start()
        x_all[:base, :] = short_x[...]
        x_all[base:, :] = long_x[...]

    keeps = [
        pltpu.make_async_copy(packed.at[0], packed_out.at[0], out_sems.at[0]),
        pltpu.make_async_copy(packed.at[1], packed_out.at[1], out_sems.at[1]),
        pltpu.make_async_copy(wo, output_out, out_sems.at[2]),
    ]
    for part, first_step in enumerate((0, steps // 2, steps - 1)):
        @pl.when(step == first_step)
        def _():
            pltpu.make_async_copy(targets[part], targets[part], in_sems.at[part]).wait()
            keeps[part].start()

    x = x_all[...]
    side = step // (steps // 2)
    turn = lax.rem(step, steps // 2)
    third = half_width // 3
    weight = lambda which: packed[side, :, pl.ds(pl.multiple_of(which * third + turn * width, width), width)]
    q_out[...] = ((dot(x, weight(0)) + qb[...]).astype(BF).astype(F32) * HEAD_DIM ** (-0.5)).astype(BF)
    k_out[...] = dot(x, weight(1)).astype(BF)
    v_out[...] = (dot(x, weight(2)) + vb[...]).astype(BF)
    for pair in range(width // 128):
        lanes = slice(128 * pair, 128 * pair + 128)
        v_t = flip(v_out[:, lanes])
        for which, spans, refs, probs in (
            (0, short_spans, short_lengths, short_p),
            (1, long_spans, long_lengths, long_p),
        ):
            for seq, (start, length) in enumerate(spans):
                k2 = k_out[start : start + length, lanes]
                rows = lax.broadcasted_iota(jnp.int32, (length, 1), 0)
                usable = rows < refs[seq]
                block = min(length, 256)
                for half in range(2):
                    k_head = head_lanes(k2, half)
                    v_head = v_t[HEAD_DIM * half : HEAD_DIM * half + HEAD_DIM, start : start + length]
                    for at in range(0, length, block):
                        scores = dot_t(k_head, q_out[start + at : start + at + block, lanes])
                        scores = jnp.where(usable, scores, -1e30)
                        top = jnp.max(scores, axis=0, keepdims=True)
                        powers = jnp.exp(scores - top)
                        total = jnp.sum(powers, axis=0, keepdims=True)
                        prob = (powers * (1.0 / total)).astype(BF)
                        probs[seq, 2 * pair + half, :, at : at + block] = prob
                        feature = 128 * pair + HEAD_DIM * half
                        mixed_t[feature : feature + HEAD_DIM, start + at : start + at + block] = dot(v_head, prob)
        offset = pl.multiple_of(step * width + 128 * pair, 128)
        mixed[:, pl.ds(offset, 128)] = flip(mixed_t[lanes, :]).astype(BF)

    @pl.when(step == steps - 1)
    def _():
        first_sum = x_all[...].astype(F32) + (dot(mixed[...], wo[...]) + ob[...])
        center = first_sum - jnp.mean(first_sum, axis=-1, keepdims=True)
        spread = jnp.mean(center * center, axis=-1, keepdims=True)
        rstd = lax.rsqrt(spread + 1e-06)
        xhat_out[...] = center * rstd
        rstd_out[...] = rstd
        for keep in keeps:
            keep.wait()


def attention_forward(shape, lengths, xs, weights, vectors):
    short_seqs, short_len, long_seqs, long_len = shape
    rows = short_seqs * short_len + long_seqs * long_len
    width = xs[0].shape[1]
    block = 256
    heads = block // HEAD_DIM
    steps = width // block
    whole = lambda shp: pl.BlockSpec(shp, lambda j: (0,) * len(shp))
    smem = pl.BlockSpec(memory_space=pltpu.SMEM)
    anywhere = pl.BlockSpec(memory_space=pl.ANY)
    row_block = pl.BlockSpec((1, block), lambda j: (0, j))
    out_col = pl.BlockSpec((rows, block), lambda j: (0, j))
    half_width = 3 * width // 2
    return pl.pallas_call(
        partial(attention_forward_kernel, shape, weights["slots"]),
        grid=(steps,),
        in_specs=[
            smem, smem, smem, whole(xs[0].shape), whole(xs[1].shape),
            *[anywhere] * len(weights["pieces"]), row_block, row_block, whole((1, width)),
        ],
        out_specs=[
            out_col, out_col, out_col,
            pl.BlockSpec((short_seqs, heads, short_len, short_len), lambda j: (0, j, 0, 0)),
            pl.BlockSpec((long_seqs, heads, long_len, long_len), lambda j: (0, j, 0, 0)),
            pl.BlockSpec((block, rows), lambda j: (j, 0)),
            whole((rows, width)), whole((rows, 1)), anywhere, anywhere,
        ],
        out_shape=[
            jax.ShapeDtypeStruct((rows, width), BF),
            jax.ShapeDtypeStruct((rows, width), BF),
            jax.ShapeDtypeStruct((rows, width), BF),
            jax.ShapeDtypeStruct((short_seqs, HEADS, short_len, short_len), BF),
            jax.ShapeDtypeStruct((long_seqs, HEADS, long_len, long_len), BF),
            jax.ShapeDtypeStruct((width, rows), F32),
            jax.ShapeDtypeStruct((rows, width), F32),
            jax.ShapeDtypeStruct((rows, 1), F32),
            jax.ShapeDtypeStruct((2, width, half_width), BF),
            jax.ShapeDtypeStruct((width, width), BF),
        ],
        scratch_shapes=[
            pltpu.VMEM((rows, width), BF), pltpu.VMEM((rows, width), BF),
            pltpu.VMEM((2, width, half_width), BF), pltpu.VMEM((width, width), BF),
            pltpu.SemaphoreType.DMA((3,)), pltpu.SemaphoreType.DMA((3,)),
        ],
        compiler_params=pltpu.CompilerParams(vmem_limit_bytes=VMEM_BYTES),
        cost_estimate=pl.CostEstimate(flops=36 * 10**9, bytes_accessed=40 * 10**6, transcendentals=5 * 10**6),
        name="attention_forward",
    )(
        weights["me"], *lengths, *xs, *weights["pieces"],
        vectors["query_bias"], vectors["value_bias"], vectors["output_bias"],
    )


def gelu_and_slope(value):
    density = jnp.exp(value * value * -0.5)
    t = 1.0 / (1.0 + (0.3275911 * 0.5 ** 0.5) * jnp.abs(value))
    poly = t * (0.254829592 + t * (-0.284496736 + t * (1.421413741 + t * (-1.453152027 + t * 1.061405429))))
    tail = 0.5 * poly * density
    share = jnp.where(value < 0.0, tail, 1.0 - tail)
    return value * share, share + value * (density * 0.3989422804014327)


def inner_kernel(xhat, gain, beta, wi, bi, active, slope, first):
    @pl.when(pl.program_id(0) == 0)
    def _():
        first[...] = (xhat[...] * gain[...] + beta[...]).astype(BF)

    value = dot(first[...], wi[...].reshape(first.shape[1], -1)) + bi[...]
    act, slp = gelu_and_slope(value)
    active[...] = act.astype(BF)
    slope[...] = slp.astype(BF)


def inner_block(feed_w, block, turn):
    shards, _, width = feed_w.shape
    per = width // block
    return pl.BlockSpec((shards, width // shards, block), lambda j: (0, turn(j) // per, lax.rem(turn(j), per)))


def down_block(feed_w, block, turn):
    shards, tall, width = feed_w.shape
    tall = tall // 2
    return pl.BlockSpec((block // tall, tall, width), lambda j: (turn(j), 1, 0))


def inner_forward(xhat, gain, beta, feed_w, inner_bias, block=512):
    rows, width = xhat.shape
    units = inner_bias.shape[1]
    whole = lambda shp: pl.BlockSpec(shp, lambda j: (0,) * len(shp))
    col = pl.BlockSpec((rows, block), lambda j: (0, j))
    return pl.pallas_call(
        inner_kernel,
        grid=(units // block,),
        in_specs=[
            whole((rows, width)), whole((1, width)), whole((1, width)),
            inner_block(feed_w, block, lambda j: j), pl.BlockSpec((1, block), lambda j: (0, j)),
        ],
        out_specs=[col, col],
        out_shape=[jax.ShapeDtypeStruct((rows, units), BF)] * 2,
        scratch_shapes=[pltpu.VMEM((rows, width), BF)],
        compiler_params=pltpu.CompilerParams(vmem_limit_bytes=VMEM_BYTES),
        name="inner_forward",
    )(xhat, gain, beta, feed_w, inner_bias)


def norm_gradient(grad, xhat, rstd, gain):
    scaled = grad * gain
    mean = jnp.mean(scaled, axis=-1, keepdims=True)
    along = jnp.mean(scaled * xhat, axis=-1, keepdims=True)
    return rstd * (scaled - mean - xhat * along)


def feed_kernel(
    shape, steps, short_lengths, long_lengths, xhat, rstd, short_ct, long_ct, active, slope, wd, wi, wo,
    gain1, beta1, gain2, beta2, down_bias,
    short_out, long_out, grad_mixed, grad_first_sum, second_beta_sum, down_sum, inner_sum, first_beta_sum, output_sum,
    total, grad_down,
):
    step = pl.program_id(0)
    short_seqs, short_len, long_seqs, long_len = shape
    base = short_seqs * short_len

    @pl.when(step == 0)
    def _():
        total[...] = xhat[...] * gain1[...] + beta1[...] + down_bias[...]

    @pl.when(step < steps)
    def _():
        total[...] += dot(active[...], wd[...].reshape(-1, wd.shape[2]))

    @pl.when(step == steps - 1)
    def _():
        keep = row_mask(short_lengths, long_lengths, shape)
        second = total[...]
        center = second - jnp.mean(second, axis=-1, keepdims=True)
        spread = jnp.mean(center * center, axis=-1, keepdims=True)
        rstd2 = lax.rsqrt(spread + 1e-06)
        xhat2 = center * rstd2
        output = ((xhat2 * gain2[...] + beta2[...]) * keep).astype(BF)
        short_out[...] = output[:base]
        long_out[...] = output[base:]
        grad_out = jnp.concatenate([short_ct[...], long_ct[...]], axis=0).astype(F32) * keep
        second_beta_sum[...] = jnp.sum(grad_out, axis=0, keepdims=True)
        grad_second = norm_gradient(grad_out, xhat2, rstd2, gain2[...])
        low = grad_second.astype(BF)
        grad_down[...] = low
        down_sum[...] = jnp.sum(low.astype(F32), axis=0, keepdims=True)
        total[...] = grad_second

    @pl.when(step >= steps)
    def _():
        grad_inner = (dot_t(grad_down[...], wd[...].reshape(-1, wd.shape[2])) * slope[...].astype(F32)).astype(BF)
        inner_sum[...] = jnp.sum(grad_inner.astype(F32), axis=0, keepdims=True)
        total[...] += dot_t(grad_inner, wi[...].reshape(total.shape[1], -1))

    @pl.when(step == 2 * steps - 1)
    def _():
        grad_first = total[...]
        first_beta_sum[...] = jnp.sum(grad_first, axis=0, keepdims=True)
        result = norm_gradient(grad_first, xhat[...], rstd[...], gain1[...])
        grad_first_sum[...] = result
        branch = result.astype(BF)
        output_sum[...] = jnp.sum(branch.astype(F32), axis=0, keepdims=True)
        grad_mixed[...] = dot_t(branch, wo[...]).astype(BF)


def feed_back(shape, lengths, xhat, rstd, cts, active, slope, feed_w, output_w, vectors, block=512):
    rows, width = xhat.shape
    units = active.shape[1]
    steps = units // block
    whole = lambda shp: pl.BlockSpec(shp, lambda j: (0,) * len(shp))
    smem = pl.BlockSpec(memory_space=pltpu.SMEM)
    vec = whole((1, width))
    late = lambda j: jnp.maximum(j - steps, 0)
    vector_out = jax.ShapeDtypeStruct((1, width), F32)
    return pl.pallas_call(
        partial(feed_kernel, shape, steps),
        grid=(2 * steps,),
        in_specs=[
            smem, smem, whole((rows, width)), whole((rows, 1)), whole(cts[0].shape), whole(cts[1].shape),
            pl.BlockSpec((rows, block), lambda j: (0, jnp.minimum(j, steps - 1))),
            pl.BlockSpec((rows, block), lambda j: (0, late(j))),
            down_block(feed_w, block, lambda j: lax.rem(j, steps)),
            inner_block(feed_w, block, late),
            whole((width, width)), vec, vec, vec, vec, vec,
        ],
        out_specs=[
            whole(cts[0].shape), whole(cts[1].shape), whole((rows, width)), whole((rows, width)),
            vec, vec, pl.BlockSpec((1, block), lambda j: (0, late(j))), vec, vec,
        ],
        out_shape=[
            jax.ShapeDtypeStruct(cts[0].shape, BF), jax.ShapeDtypeStruct(cts[1].shape, BF),
            jax.ShapeDtypeStruct((rows, width), BF), jax.ShapeDtypeStruct((rows, width), F32),
            vector_out, vector_out, jax.ShapeDtypeStruct((1, units), F32), vector_out, vector_out,
        ],
        scratch_shapes=[pltpu.VMEM((rows, width), F32), pltpu.VMEM((rows, width), BF)],
        compiler_params=pltpu.CompilerParams(vmem_limit_bytes=VMEM_BYTES),
        name="feed_back",
    )(
        *lengths, xhat, rstd, *cts, active, slope, feed_w, feed_w, output_w,
        vectors["first_gain"], vectors["first_beta"], vectors["second_gain"], vectors["second_beta"], vectors["down_bias"],
    )


def attention_backward_kernel(
    shape, short_lengths, long_lengths, q, k, v, gm, short_p, long_p, mixed_t, wq, wk, wv, grad_first_sum,
    short_grad, long_grad, query_sum, value_sum, grad_packed, total,
):
    step = pl.program_id(0)
    steps = pl.num_programs(0)
    short_seqs, short_len, long_seqs, long_len = shape
    base = short_seqs * short_len
    width = q.shape[1]
    short_spans, long_spans = sequences(*shape)
    scale = HEAD_DIM ** (-0.5)
    for pair in range(width // 128):
        lanes = slice(128 * pair, 128 * pair + 128)
        gm_t = flip(gm[:, lanes]).astype(F32)
        k_t = flip(k[:, lanes])
        product = gm_t * mixed_t[lanes, :]
        delta = [jnp.sum(product[HEAD_DIM * h : HEAD_DIM * h + HEAD_DIM], axis=0, keepdims=True) for h in range(2)]
        for spans, probs in ((short_spans, short_p), (long_spans, long_p)):
            for seq, (start, length) in enumerate(spans):
                here = slice(start, start + length)
                gm2, v2, q2 = gm[here, lanes], v[here, lanes], q[here, lanes]
                grad_value = grad_key = None
                grad_query_t = []
                for half in range(2):
                    prob = probs[seq, 2 * pair + half]
                    grad_p = dot_t(head_lanes(v2, half), gm2)
                    grad_s = (prob.astype(F32) * (grad_p - delta[half][:, here])).astype(BF)
                    dv = dot(prob, head_lanes(gm2, half))
                    dk = dot(grad_s, head_lanes(q2, half))
                    grad_value = dv if half == 0 else grad_value + dv
                    grad_key = dk if half == 0 else grad_key + dk
                    grad_query_t.append(dot(k_t[HEAD_DIM * half : HEAD_DIM * half + HEAD_DIM, here], grad_s))
                grad_packed[here, 128 * pair : 128 * pair + 128] = (
                    flip(jnp.concatenate(grad_query_t, axis=0)) * scale
                ).astype(BF)
                grad_packed[here, width + 128 * pair : width + 128 * pair + 128] = grad_key.astype(BF)
                grad_packed[here, 2 * width + 128 * pair : 2 * width + 128 * pair + 128] = grad_value.astype(BF)
    query_sum[...] = jnp.sum(grad_packed[:, :width].astype(F32), axis=0, keepdims=True)
    value_sum[...] = jnp.sum(grad_packed[:, 2 * width :].astype(F32), axis=0, keepdims=True)
    part = (
        dot_t(grad_packed[:, :width], wq[0])
        + dot_t(grad_packed[:, width : 2 * width], wk[0])
        + dot_t(grad_packed[:, 2 * width :], wv[0])
    )

    @pl.when(step == 0)
    def _():
        total[...] = grad_first_sum[...] + part

    @pl.when(step > 0)
    def _():
        total[...] += part

    @pl.when(step == steps - 1)
    def _():
        keep = row_mask(short_lengths, long_lengths, shape)
        result = (total[...] * keep).astype(BF)
        short_grad[...] = result[:base]
        long_grad[...] = result[base:]


def attention_backward(shape, lengths, q, k, v, gm, short_p, long_p, mixed_t, packed_w, grad_first_sum):
    short_seqs, short_len, long_seqs, long_len = shape
    rows, width = q.shape
    block = 256
    heads = block // HEAD_DIM
    steps = width // block
    base = short_seqs * short_len
    whole = lambda shp: pl.BlockSpec(shp, lambda j: (0,) * len(shp))
    smem = pl.BlockSpec(memory_space=pltpu.SMEM)
    half = steps // 2
    column = lambda off: pl.BlockSpec((1, width, block), lambda j: (j // half, 0, lax.rem(j, half) + off * half))
    col = pl.BlockSpec((rows, block), lambda j: (0, j))
    vec = pl.BlockSpec((1, block), lambda j: (0, j))
    return pl.pallas_call(
        partial(attention_backward_kernel, shape),
        grid=(steps,),
        in_specs=[
            smem, smem, col, col, col, col,
            pl.BlockSpec((short_seqs, heads, short_len, short_len), lambda j: (0, j, 0, 0)),
            pl.BlockSpec((long_seqs, heads, long_len, long_len), lambda j: (0, j, 0, 0)),
            pl.BlockSpec((block, rows), lambda j: (j, 0)),
            column(0), column(1), column(2), whole((rows, width)),
        ],
        out_specs=[whole((base, width)), whole((rows - base, width)), vec, vec],
        out_shape=[
            jax.ShapeDtypeStruct((base, width), BF), jax.ShapeDtypeStruct((rows - base, width), BF),
            jax.ShapeDtypeStruct((1, width), F32), jax.ShapeDtypeStruct((1, width), F32),
        ],
        scratch_shapes=[pltpu.VMEM((rows, 3 * block), BF), pltpu.VMEM((rows, width), F32)],
        compiler_params=pltpu.CompilerParams(vmem_limit_bytes=VMEM_BYTES),
        name="attention_backward",
    )(*lengths, q, k, v, gm, short_p, long_p, mixed_t, packed_w, packed_w, packed_w, grad_first_sum)


def local(
    short_input, short_lengths, short_cotangent, long_input, long_lengths, long_cotangent,
    packed_weight, output_weight, inner_weight, down_weight,
    first_gain, second_gain, query_bias, value_bias, output_bias, inner_bias, down_bias, first_beta, second_beta,
):
    short_seqs, short_len, width = short_input.shape
    long_seqs, long_len, _ = long_input.shape
    shape = (short_seqs, short_len, long_seqs, long_len)
    lengths = (short_lengths, long_lengths)
    vectors = dict(
        first_gain=first_gain, second_gain=second_gain, query_bias=query_bias, value_bias=value_bias,
        output_bias=output_bias, inner_bias=inner_bias, down_bias=down_bias, first_beta=first_beta, second_beta=second_beta,
    )
    vectors = {name: item.reshape(1, -1) for name, item in vectors.items()}
    xs = (short_input.reshape(-1, width), long_input.reshape(-1, width))
    cts = (short_cotangent.reshape(-1, width), long_cotangent.reshape(-1, width))
    weights = gather_weights(packed_weight, output_weight, inner_weight, down_weight)
    q, k, v, short_p, long_p, mixed_t, xhat, rstd, packed_w, output_w = attention_forward(shape, lengths, xs, weights, vectors)
    active, slope = inner_forward(xhat, vectors["first_gain"], vectors["first_beta"], weights["feed"], vectors["inner_bias"])
    (
        short_out, long_out, gm, grad_first_sum, second_beta_sum, down_sum, inner_sum, first_beta_sum, output_sum,
    ) = feed_back(shape, lengths, xhat, rstd, cts, active, slope, weights["feed"], output_w, vectors)
    short_grad, long_grad, query_sum, value_sum = attention_backward(
        shape, lengths, q, k, v, gm, short_p, long_p, mixed_t, packed_w, grad_first_sum
    )
    sums = sum_all(jnp.concatenate(
        [query_sum, value_sum, output_sum, inner_sum, down_sum, first_beta_sum, second_beta_sum], axis=1
    ).reshape(-1))
    outs = []
    at = 0
    for size in (width, width, width, inner_bias.shape[0], width, width, width):
        outs.append(lax.slice_in_dim(sums, at, at + size))
        at += size
    return (
        short_out.reshape(short_input.shape), short_grad.reshape(short_input.shape),
        long_out.reshape(long_input.shape), long_grad.reshape(long_input.shape), *outs,
    )


def exchange(block, mask):
    count = lax.axis_size("dp")
    return lax.ppermute(block, "dp", [(i, i ^ mask(i)) for i in range(count)])


CORE, X, Y, Z_NEAR, Z_FAR = 1, 2, 4, 8, 16


def side_first(index):
    return X if index & CORE == 0 else Y


def side_second(index):
    return Y if index & CORE == 0 else X


def gather_by_exchange(shard):
    held = jnp.concatenate([shard, exchange(shard, lambda i: Z_FAR)])
    held = jnp.concatenate([held, exchange(held, side_first)])
    held = jnp.concatenate([held, exchange(held, lambda i: Z_NEAR)])
    other = exchange(held, side_second)
    return [held, other, exchange(held, lambda i: CORE), exchange(other, lambda i: CORE)]


def exchange_slots():
    def mask(core, swap, far, slot):
        owner = core ^ swap
        return (
            swap * CORE + far * side_second(owner) + Z_FAR * (slot & 1)
            + side_first(owner) * (slot >> 1 & 1) + Z_NEAR * (slot >> 2)
        )

    return [
        [(mask(0, swap, far, slot), mask(1, swap, far, slot)) for slot in range(8)]
        for swap in (0, 1) for far in (0, 1)
    ]


def gather_weights(packed, output, inner, down):
    count = lax.axis_size("dp")
    width = output.shape[1]
    half = width // 2
    sides = [
        jnp.concatenate([packed[:, i * width + at : i * width + at + half] for i in range(3)], axis=1) for at in (0, half)
    ]
    parts = [*sides, output]
    tall = inner.shape[0]
    blocks = inner.shape[1] // width
    if count == 32:
        feed = jnp.concatenate(
            [inner.reshape(tall, blocks, width).transpose(1, 0, 2).reshape(blocks * tall, width), down], axis=0
        )
        feed = lax.all_gather(feed, "dp", axis=0, tiled=False)
        gathered = [gather_by_exchange(part) for part in parts]
        return dict(
            me=lax.axis_index("dp").reshape(1).astype(jnp.int32), slots=exchange_slots(),
            pieces=[gathered[part][piece] for piece in range(4) for part in range(3)], feed=feed,
        )
    whole = [lax.all_gather(part, "dp", axis=0, tiled=True) for part in (*parts, inner, down)]
    shards = 32
    feed = jnp.concatenate(
        [
            whole[3].reshape(shards, -1, blocks, width).transpose(0, 2, 1, 3).reshape(shards, -1, width),
            whole[4].reshape(shards, -1, width),
        ],
        axis=1,
    )
    return dict(me=jnp.zeros((1,), jnp.int32), slots=[[(i, i) for i in range(shards)]], pieces=whole[:3], feed=feed)


def sum_all(vector):
    count = lax.axis_size("dp")
    if count & (count - 1):
        return lax.psum(vector, "dp")
    bit = 1
    while bit < count:
        vector = vector + exchange(vector, lambda i: bit)
        bit *= 2
    return vector


def solution(mesh):
    rows = P("dp", None, None)
    in_specs = (rows, P("dp"), rows, rows, P("dp"), rows) + (P("dp", None),) * 4 + (P(),) * 9
    out_specs = (rows,) * 4 + (P(),) * 7
    return jax.shard_map(local, mesh=mesh, in_specs=in_specs, out_specs=out_specs, check_vma=False)
```

```python
from functools import partial

import jax
import jax.numpy as jnp
from jax import lax
from jax.experimental import pallas as pl
from jax.experimental.pallas import tpu as pltpu
from jax.sharding import PartitionSpec as P

HEADS = 16
HEAD_DIM = 64
BF = jnp.bfloat16
F32 = jnp.float32
VMEM_BYTES = 60 * 1024 * 1024
FEED_BLOCK = 1024


def dot(left, right):
    return lax.dot_general(left, right, (((1,), (0,)), ((), ())), preferred_element_type=F32)


def dot_t(left, right):
    return lax.dot_general(left, right, (((1,), (1,)), ((), ())), preferred_element_type=F32)


def sequences(short_seqs, short_len, long_seqs, long_len):
    spans = [(i * short_len, short_len) for i in range(short_seqs)]
    base = short_seqs * short_len
    return spans, [(base + i * long_len, long_len) for i in range(long_seqs)]


def row_mask(short_lengths, long_lengths, shape):
    short_seqs, short_len, long_seqs, long_len = shape
    pieces = []
    for count, length, refs in (
        (short_seqs, short_len, short_lengths),
        (long_seqs, long_len, long_lengths),
    ):
        for i in range(count):
            rows = lax.broadcasted_iota(jnp.int32, (length, 1), 0)
            pieces.append(jnp.where(rows < refs[i], 1.0, 0.0).astype(F32))
    return jnp.concatenate(pieces, axis=0)


def head_lanes(block, half):
    lanes = lax.broadcasted_iota(jnp.int32, block.shape, 1)
    keep = lanes < HEAD_DIM if half == 0 else lanes >= HEAD_DIM
    return jnp.where(keep, block, jnp.zeros_like(block))


def flip(block):
    return jnp.transpose(block, (1, 0))


def attention_forward_kernel(
    shape, slots, me, short_lengths, long_lengths, short_x, long_x, *refs,
):
    pieces, refs = refs[: 3 * len(slots)], refs[3 * len(slots) :]
    (
        qb, vb, ob, q_out, k_out, v_out, short_p, long_p, mixed_t, xhat_out, rstd_out, packed_out, output_out,
        x_all, mixed, packed, wo, in_sems, out_sems,
    ) = refs
    step = pl.program_id(0)
    steps = pl.num_programs(0)
    short_seqs, short_len, long_seqs, long_len = shape
    base = short_seqs * short_len
    width = q_out.shape[1]
    half_width = packed.shape[2]
    short_spans, long_spans = sequences(*shape)
    targets = (packed.at[0], packed.at[1], wo)

    @pl.when(step == 0)
    def _():
        for part in range(3):
            for ref, masks in zip(pieces[part::3], slots):
                tall = ref.shape[0] // len(masks)
                for slot, mask in enumerate(masks):
                    mask = jnp.where(jnp.bitwise_and(me[0], 1) == 0, mask[0], mask[1])
                    place = pl.multiple_of(jnp.bitwise_xor(me[0], mask) * tall, tall)
                    pltpu.make_async_copy(
                        ref.at[pl.ds(slot * tall, tall)], targets[part].at[pl.ds(place, tall)], in_sems.at[part]
                    ).start()
        x_all[:base, :] = short_x[...]
        x_all[base:, :] = long_x[...]

    keeps = [
        pltpu.make_async_copy(packed.at[0], packed_out.at[0], out_sems.at[0]),
        pltpu.make_async_copy(packed.at[1], packed_out.at[1], out_sems.at[1]),
        pltpu.make_async_copy(wo, output_out, out_sems.at[2]),
    ]
    for part, first_step in enumerate((0, steps // 2, steps - 1)):
        @pl.when(step == first_step)
        def _():
            pltpu.make_async_copy(targets[part], targets[part], in_sems.at[part]).wait()
            keeps[part].start()

    x = x_all[...]
    side = step // (steps // 2)
    turn = lax.rem(step, steps // 2)
    third = half_width // 3
    weight = lambda which: packed[side, :, pl.ds(pl.multiple_of(which * third + turn * width, width), width)]
    q_out[...] = ((dot(x, weight(0)) + qb[...]).astype(BF).astype(F32) * HEAD_DIM ** (-0.5)).astype(BF)
    k_out[...] = dot(x, weight(1)).astype(BF)
    v_out[...] = (dot(x, weight(2)) + vb[...]).astype(BF)
    for pair in range(width // 128):
        lanes = slice(128 * pair, 128 * pair + 128)
        v_t = flip(v_out[:, lanes])
        for which, spans, refs, probs in (
            (0, short_spans, short_lengths, short_p),
            (1, long_spans, long_lengths, long_p),
        ):
            for seq, (start, length) in enumerate(spans):
                k2 = k_out[start : start + length, lanes]
                rows = lax.broadcasted_iota(jnp.int32, (length, 1), 0)
                usable = rows < refs[seq]
                block = min(length, 256)
                for half in range(2):
                    k_head = head_lanes(k2, half)
                    v_head = v_t[HEAD_DIM * half : HEAD_DIM * half + HEAD_DIM, start : start + length]
                    for at in range(0, length, block):
                        scores = dot_t(k_head, q_out[start + at : start + at + block, lanes])
                        scores = jnp.where(usable, scores, -1e30)
                        top = jnp.max(scores, axis=0, keepdims=True)
                        powers = jnp.exp(scores - top)
                        total = jnp.sum(powers, axis=0, keepdims=True)
                        prob = (powers * (1.0 / total)).astype(BF)
                        probs[seq, 2 * pair + half, :, at : at + block] = prob
                        feature = 128 * pair + HEAD_DIM * half
                        mixed_t[feature : feature + HEAD_DIM, start + at : start + at + block] = dot(v_head, prob)
        offset = pl.multiple_of(step * width + 128 * pair, 128)
        mixed[:, pl.ds(offset, 128)] = flip(mixed_t[lanes, :]).astype(BF)

    @pl.when(step == steps - 1)
    def _():
        first_sum = x_all[...].astype(F32) + (dot(mixed[...], wo[...]) + ob[...])
        center = first_sum - jnp.mean(first_sum, axis=-1, keepdims=True)
        spread = jnp.mean(center * center, axis=-1, keepdims=True)
        rstd = lax.rsqrt(spread + 1e-06)
        xhat_out[...] = center * rstd
        rstd_out[...] = rstd
        for keep in keeps:
            keep.wait()


def attention_forward(shape, lengths, xs, weights, vectors):
    short_seqs, short_len, long_seqs, long_len = shape
    rows = short_seqs * short_len + long_seqs * long_len
    width = xs[0].shape[1]
    block = 256
    heads = block // HEAD_DIM
    steps = width // block
    whole = lambda shp: pl.BlockSpec(shp, lambda j: (0,) * len(shp))
    smem = pl.BlockSpec(memory_space=pltpu.SMEM)
    anywhere = pl.BlockSpec(memory_space=pl.ANY)
    row_block = pl.BlockSpec((1, block), lambda j: (0, j))
    out_col = pl.BlockSpec((rows, block), lambda j: (0, j))
    half_width = 3 * width // 2
    return pl.pallas_call(
        partial(attention_forward_kernel, shape, weights["slots"]),
        grid=(steps,),
        in_specs=[
            smem, smem, smem, whole(xs[0].shape), whole(xs[1].shape),
            *[anywhere] * len(weights["pieces"]), row_block, row_block, whole((1, width)),
        ],
        out_specs=[
            out_col, out_col, out_col,
            pl.BlockSpec((short_seqs, heads, short_len, short_len), lambda j: (0, j, 0, 0)),
            pl.BlockSpec((long_seqs, heads, long_len, long_len), lambda j: (0, j, 0, 0)),
            pl.BlockSpec((block, rows), lambda j: (j, 0)),
            whole((rows, width)), whole((rows, 1)), anywhere, anywhere,
        ],
        out_shape=[
            jax.ShapeDtypeStruct((rows, width), BF),
            jax.ShapeDtypeStruct((rows, width), BF),
            jax.ShapeDtypeStruct((rows, width), BF),
            jax.ShapeDtypeStruct((short_seqs, HEADS, short_len, short_len), BF),
            jax.ShapeDtypeStruct((long_seqs, HEADS, long_len, long_len), BF),
            jax.ShapeDtypeStruct((width, rows), F32),
            jax.ShapeDtypeStruct((rows, width), F32),
            jax.ShapeDtypeStruct((rows, 1), F32),
            jax.ShapeDtypeStruct((2, width, half_width), BF),
            jax.ShapeDtypeStruct((width, width), BF),
        ],
        scratch_shapes=[
            pltpu.VMEM((rows, width), BF), pltpu.VMEM((rows, width), BF),
            pltpu.VMEM((2, width, half_width), BF), pltpu.VMEM((width, width), BF),
            pltpu.SemaphoreType.DMA((3,)), pltpu.SemaphoreType.DMA((3,)),
        ],
        compiler_params=pltpu.CompilerParams(vmem_limit_bytes=VMEM_BYTES),
        cost_estimate=pl.CostEstimate(flops=36 * 10**9, bytes_accessed=40 * 10**6, transcendentals=5 * 10**6),
        name="attention_forward",
    )(
        weights["me"], *lengths, *xs, *weights["pieces"],
        vectors["query_bias"], vectors["value_bias"], vectors["output_bias"],
    )


def gelu_and_slope(value):
    share = 0.5 + 0.5 * lax.erf(value * 0.5 ** 0.5)
    density = jnp.exp2(value * (value * -0.7213475204444817)) * 0.3989422804014327
    return value * share, share + value * density


def inner_block(feed_w, block, turn):
    shards, _, width = feed_w.shape
    per = width // block
    return pl.BlockSpec((shards, width // shards, block), lambda j: (0, turn(j) // per, lax.rem(turn(j), per)))


def down_block(feed_w, block, turn):
    shards, tall, width = feed_w.shape
    tall = tall // 2
    return pl.BlockSpec((block // tall, tall, width), lambda j: (turn(j), 1, 0))


def norm_gradient(grad, xhat, rstd, gain):
    scaled = grad * gain
    mean = jnp.mean(scaled, axis=-1, keepdims=True)
    along = jnp.mean(scaled * xhat, axis=-1, keepdims=True)
    return rstd * (scaled - mean - xhat * along)


def fold(block):
    return jnp.sum(block.reshape(block.shape[0] // 8, 8, block.shape[1]), axis=0)


def feed_kernel(
    shape, steps, keep, xhat, rstd, short_ct, long_ct, wi, wd, wo, inner_bias,
    gain1, beta1, gain2, beta2, down_bias,
    short_out, long_out, grad_mixed, grad_first_sum, second_beta_sum, down_sum, inner_sum, first_beta_sum, output_sum,
    total, low, value, slope, sums,
):
    step = pl.program_id(0)
    short_seqs, short_len, long_seqs, long_len = shape
    base = short_seqs * short_len
    rows, width = xhat.shape
    chunk = 128
    wide = lambda ref: ref[...].reshape(width, -1)
    tall = lambda ref: ref[...].reshape(-1, width)

    def first_part():
        value[lax.rem(step, 2)] = dot(low[...], wide(wi)) + inner_bias[...]

    def second_part():
        act, slp = gelu_and_slope(value[lax.rem(step + 1, 2)])
        slope[step - 1] = slp.astype(BF)
        total[...] += dot(act.astype(BF), tall(wd))

    @pl.when(step == 0)
    def _():
        def body(i, _):
            here = pl.ds(pl.multiple_of(i * chunk, chunk), chunk)
            first = xhat[here, :] * gain1[...] + beta1[...]
            low[here, :] = first.astype(BF)
            total[here, :] = first + down_bias[...]
            return 0

        lax.fori_loop(0, rows // chunk, body, 0)
        first_part()

    @pl.when((step > 0) & (step < steps))
    def _():
        first_part()
        second_part()

    @pl.when(step == steps)
    def _():
        second_part()
        sums[...] = jnp.zeros_like(sums)

        def rows_of(source, out, start):
            def body(i, _):
                there = pl.ds(pl.multiple_of(i * chunk, chunk), chunk)
                here = pl.ds(pl.multiple_of(start + i * chunk, chunk), chunk)
                second = total[here, :]
                center = second - jnp.mean(second, axis=-1, keepdims=True)
                spread = jnp.mean(center * center, axis=-1, keepdims=True)
                rstd2 = lax.rsqrt(spread + 1e-06)
                xhat2 = center * rstd2
                usable = keep[here, :]
                out[there, :] = ((xhat2 * gain2[...] + beta2[...]) * usable).astype(BF)
                grad_out = source[there, :].astype(F32) * usable
                grad_second = norm_gradient(grad_out, xhat2, rstd2, gain2[...])
                rounded = grad_second.astype(BF)
                low[here, :] = rounded
                total[here, :] = grad_second
                sums[0] += fold(grad_out)
                sums[1] += fold(rounded.astype(F32))
                return 0

            lax.fori_loop(0, source.shape[0] // chunk, body, 0)

        rows_of(short_ct, short_out, 0)
        rows_of(long_ct, long_out, base)
        second_beta_sum[...] = jnp.sum(sums[0], axis=0, keepdims=True)
        down_sum[...] = jnp.sum(sums[1], axis=0, keepdims=True)

    @pl.when(step > steps)
    def _():
        grad_inner = (dot_t(low[...], tall(wd)) * slope[2 * steps - step].astype(F32)).astype(BF)
        inner_sum[...] = jnp.sum(grad_inner.astype(F32), axis=0, keepdims=True)
        total[...] += dot_t(grad_inner, wide(wi))

    @pl.when(step == 2 * steps)
    def _():
        sums[...] = jnp.zeros_like(sums)

        def body(i, _):
            here = pl.ds(pl.multiple_of(i * chunk, chunk), chunk)
            grad_first = total[here, :]
            result = norm_gradient(grad_first, xhat[here, :], rstd[here, :], gain1[...])
            grad_first_sum[here, :] = result
            branch = result.astype(BF)
            low[here, :] = branch
            sums[0] += fold(grad_first)
            sums[1] += fold(branch.astype(F32))
            return 0

        lax.fori_loop(0, rows // chunk, body, 0)
        first_beta_sum[...] = jnp.sum(sums[0], axis=0, keepdims=True)
        output_sum[...] = jnp.sum(sums[1], axis=0, keepdims=True)
        grad_mixed[...] = dot_t(low[...], wo[...]).astype(BF)


def feed_forward_and_back(shape, keep, xhat, rstd, cts, feed_w, output_w, vectors, block=FEED_BLOCK):
    rows, width = xhat.shape
    units = vectors["inner_bias"].shape[1]
    steps = units // block
    whole = lambda shp: pl.BlockSpec(shp, lambda j: (0,) * len(shp))
    vec = whole((1, width))
    back = lambda j: 2 * steps - j
    inner_turn = lambda j: jnp.where(j <= steps, jnp.minimum(j, steps - 1), back(j))
    down_turn = lambda j: jnp.where(j <= steps, jnp.maximum(j - 1, 0), back(j))
    vector_out = jax.ShapeDtypeStruct((1, width), F32)
    return pl.pallas_call(
        partial(feed_kernel, shape, steps),
        grid=(2 * steps + 1,),
        in_specs=[
            whole((rows, 1)), whole((rows, width)), whole((rows, 1)), whole(cts[0].shape), whole(cts[1].shape),
            inner_block(feed_w, block, inner_turn), down_block(feed_w, block, down_turn), whole((width, width)),
            pl.BlockSpec((1, block), lambda j: (0, jnp.minimum(j, steps - 1))), vec, vec, vec, vec, vec,
        ],
        out_specs=[
            whole(cts[0].shape), whole(cts[1].shape), whole((rows, width)), whole((rows, width)),
            vec, vec, pl.BlockSpec((1, block), lambda j: (0, jnp.minimum(back(j), steps - 1))), vec, vec,
        ],
        out_shape=[
            jax.ShapeDtypeStruct(cts[0].shape, BF), jax.ShapeDtypeStruct(cts[1].shape, BF),
            jax.ShapeDtypeStruct((rows, width), BF), jax.ShapeDtypeStruct((rows, width), F32),
            vector_out, vector_out, jax.ShapeDtypeStruct((1, units), F32), vector_out, vector_out,
        ],
        scratch_shapes=[
            pltpu.VMEM((rows, width), F32), pltpu.VMEM((rows, width), BF), pltpu.VMEM((2, rows, block), F32),
            pltpu.VMEM((steps, rows, block), BF), pltpu.VMEM((2, 8, width), F32),
        ],
        compiler_params=pltpu.CompilerParams(vmem_limit_bytes=VMEM_BYTES),
        cost_estimate=pl.CostEstimate(flops=65 * 10**9, bytes_accessed=60 * 10**6, transcendentals=4 * 10**6),
        name="feed_forward_and_back",
    )(
        keep, xhat, rstd, *cts, feed_w, feed_w, output_w, vectors["inner_bias"],
        vectors["first_gain"], vectors["first_beta"], vectors["second_gain"], vectors["second_beta"], vectors["down_bias"],
    )


def attention_backward_kernel(
    shape, short_lengths, long_lengths, q, k, v, gm, short_p, long_p, mixed_t, wq, wk, wv, grad_first_sum,
    short_grad, long_grad, query_sum, value_sum, grad_packed, total,
):
    step = pl.program_id(0)
    steps = pl.num_programs(0)
    short_seqs, short_len, long_seqs, long_len = shape
    base = short_seqs * short_len
    width = q.shape[1]
    short_spans, long_spans = sequences(*shape)
    scale = HEAD_DIM ** (-0.5)
    for pair in range(width // 128):
        lanes = slice(128 * pair, 128 * pair + 128)
        gm_t = flip(gm[:, lanes]).astype(F32)
        k_t = flip(k[:, lanes])
        product = gm_t * mixed_t[lanes, :]
        delta = [jnp.sum(product[HEAD_DIM * h : HEAD_DIM * h + HEAD_DIM], axis=0, keepdims=True) for h in range(2)]
        for spans, probs in ((short_spans, short_p), (long_spans, long_p)):
            for seq, (start, length) in enumerate(spans):
                here = slice(start, start + length)
                gm2, v2, q2 = gm[here, lanes], v[here, lanes], q[here, lanes]
                grad_value = grad_key = None
                grad_query_t = []
                for half in range(2):
                    prob = probs[seq, 2 * pair + half]
                    grad_p = dot_t(head_lanes(v2, half), gm2)
                    grad_s = (prob.astype(F32) * (grad_p - delta[half][:, here])).astype(BF)
                    dv = dot(prob, head_lanes(gm2, half))
                    dk = dot(grad_s, head_lanes(q2, half))
                    grad_value = dv if half == 0 else grad_value + dv
                    grad_key = dk if half == 0 else grad_key + dk
                    grad_query_t.append(dot(k_t[HEAD_DIM * half : HEAD_DIM * half + HEAD_DIM, here], grad_s))
                grad_packed[here, 128 * pair : 128 * pair + 128] = (
                    flip(jnp.concatenate(grad_query_t, axis=0)) * scale
                ).astype(BF)
                grad_packed[here, width + 128 * pair : width + 128 * pair + 128] = grad_key.astype(BF)
                grad_packed[here, 2 * width + 128 * pair : 2 * width + 128 * pair + 128] = grad_value.astype(BF)
    query_sum[...] = jnp.sum(grad_packed[:, :width].astype(F32), axis=0, keepdims=True)
    value_sum[...] = jnp.sum(grad_packed[:, 2 * width :].astype(F32), axis=0, keepdims=True)
    part = (
        dot_t(grad_packed[:, :width], wq[0])
        + dot_t(grad_packed[:, width : 2 * width], wk[0])
        + dot_t(grad_packed[:, 2 * width :], wv[0])
    )

    @pl.when(step == 0)
    def _():
        total[...] = grad_first_sum[...] + part

    @pl.when(step > 0)
    def _():
        total[...] += part

    @pl.when(step == steps - 1)
    def _():
        keep = row_mask(short_lengths, long_lengths, shape)
        result = (total[...] * keep).astype(BF)
        short_grad[...] = result[:base]
        long_grad[...] = result[base:]


def attention_backward(shape, lengths, q, k, v, gm, short_p, long_p, mixed_t, packed_w, grad_first_sum):
    short_seqs, short_len, long_seqs, long_len = shape
    rows, width = q.shape
    block = 256
    heads = block // HEAD_DIM
    steps = width // block
    base = short_seqs * short_len
    whole = lambda shp: pl.BlockSpec(shp, lambda j: (0,) * len(shp))
    smem = pl.BlockSpec(memory_space=pltpu.SMEM)
    half = steps // 2
    column = lambda off: pl.BlockSpec((1, width, block), lambda j: (j // half, 0, lax.rem(j, half) + off * half))
    col = pl.BlockSpec((rows, block), lambda j: (0, j))
    vec = pl.BlockSpec((1, block), lambda j: (0, j))
    return pl.pallas_call(
        partial(attention_backward_kernel, shape),
        grid=(steps,),
        in_specs=[
            smem, smem, col, col, col, col,
            pl.BlockSpec((short_seqs, heads, short_len, short_len), lambda j: (0, j, 0, 0)),
            pl.BlockSpec((long_seqs, heads, long_len, long_len), lambda j: (0, j, 0, 0)),
            pl.BlockSpec((block, rows), lambda j: (j, 0)),
            column(0), column(1), column(2), whole((rows, width)),
        ],
        out_specs=[whole((base, width)), whole((rows - base, width)), vec, vec],
        out_shape=[
            jax.ShapeDtypeStruct((base, width), BF), jax.ShapeDtypeStruct((rows - base, width), BF),
            jax.ShapeDtypeStruct((1, width), F32), jax.ShapeDtypeStruct((1, width), F32),
        ],
        scratch_shapes=[pltpu.VMEM((rows, 3 * block), BF), pltpu.VMEM((rows, width), F32)],
        compiler_params=pltpu.CompilerParams(vmem_limit_bytes=VMEM_BYTES),
        name="attention_backward",
    )(*lengths, q, k, v, gm, short_p, long_p, mixed_t, packed_w, packed_w, packed_w, grad_first_sum)


def local(
    short_input, short_lengths, short_cotangent, long_input, long_lengths, long_cotangent,
    packed_weight, output_weight, inner_weight, down_weight,
    first_gain, second_gain, query_bias, value_bias, output_bias, inner_bias, down_bias, first_beta, second_beta,
):
    short_seqs, short_len, width = short_input.shape
    long_seqs, long_len, _ = long_input.shape
    shape = (short_seqs, short_len, long_seqs, long_len)
    lengths = (short_lengths, long_lengths)
    vectors = dict(
        first_gain=first_gain, second_gain=second_gain, query_bias=query_bias, value_bias=value_bias,
        output_bias=output_bias, inner_bias=inner_bias, down_bias=down_bias, first_beta=first_beta, second_beta=second_beta,
    )
    vectors = {name: item.reshape(1, -1) for name, item in vectors.items()}
    xs = (short_input.reshape(-1, width), long_input.reshape(-1, width))
    cts = (short_cotangent.reshape(-1, width), long_cotangent.reshape(-1, width))
    weights = gather_weights(packed_weight, output_weight, inner_weight, down_weight)
    q, k, v, short_p, long_p, mixed_t, xhat, rstd, packed_w, output_w = attention_forward(shape, lengths, xs, weights, vectors)
    keep = jnp.concatenate([
        (jnp.arange(item.shape[1])[None, :] < length[:, None]).reshape(-1, 1)
        for item, length in ((short_input, short_lengths), (long_input, long_lengths))
    ], axis=0).astype(F32)
    (
        short_out, long_out, gm, grad_first_sum, second_beta_sum, down_sum, inner_sum, first_beta_sum, output_sum,
    ) = feed_forward_and_back(shape, keep, xhat, rstd, cts, weights["feed"], output_w, vectors)
    short_grad, long_grad, query_sum, value_sum = attention_backward(
        shape, lengths, q, k, v, gm, short_p, long_p, mixed_t, packed_w, grad_first_sum
    )
    sums = sum_all(jnp.concatenate(
        [query_sum, value_sum, output_sum, inner_sum, down_sum, first_beta_sum, second_beta_sum], axis=1
    ).reshape(-1))
    outs = []
    at = 0
    for size in (width, width, width, inner_bias.shape[0], width, width, width):
        outs.append(lax.slice_in_dim(sums, at, at + size))
        at += size
    return (
        short_out.reshape(short_input.shape), short_grad.reshape(short_input.shape),
        long_out.reshape(long_input.shape), long_grad.reshape(long_input.shape), *outs,
    )


def exchange(block, mask):
    count = lax.axis_size("dp")
    return lax.ppermute(block, "dp", [(i, i ^ mask(i)) for i in range(count)])


CORE, X, Y, Z_NEAR, Z_FAR = 1, 2, 4, 8, 16


def side_first(index):
    return X if index & CORE == 0 else Y


def side_second(index):
    return Y if index & CORE == 0 else X


def gather_by_exchange(shard):
    held = jnp.concatenate([shard, exchange(shard, lambda i: Z_FAR)])
    held = jnp.concatenate([held, exchange(held, side_first)])
    held = jnp.concatenate([held, exchange(held, lambda i: Z_NEAR)])
    other = exchange(held, side_second)
    return [held, other, exchange(held, lambda i: CORE), exchange(other, lambda i: CORE)]


def exchange_slots():
    def mask(core, swap, far, slot):
        owner = core ^ swap
        return (
            swap * CORE + far * side_second(owner) + Z_FAR * (slot & 1)
            + side_first(owner) * (slot >> 1 & 1) + Z_NEAR * (slot >> 2)
        )

    return [
        [(mask(0, swap, far, slot), mask(1, swap, far, slot)) for slot in range(8)]
        for swap in (0, 1) for far in (0, 1)
    ]


def gather_weights(packed, output, inner, down):
    count = lax.axis_size("dp")
    width = output.shape[1]
    half = width // 2
    sides = [
        jnp.concatenate([packed[:, i * width + at : i * width + at + half] for i in range(3)], axis=1) for at in (0, half)
    ]
    parts = [*sides, output]
    tall = inner.shape[0]
    blocks = inner.shape[1] // width
    if count == 32:
        feed = jnp.concatenate(
            [inner.reshape(tall, blocks, width).transpose(1, 0, 2).reshape(blocks * tall, width), down], axis=0
        )
        feed = lax.all_gather(feed, "dp", axis=0, tiled=False)
        gathered = [gather_by_exchange(part) for part in parts]
        return dict(
            me=lax.axis_index("dp").reshape(1).astype(jnp.int32), slots=exchange_slots(),
            pieces=[gathered[part][piece] for piece in range(4) for part in range(3)], feed=feed,
        )
    whole = [lax.all_gather(part, "dp", axis=0, tiled=True) for part in (*parts, inner, down)]
    shards = 32
    feed = jnp.concatenate(
        [
            whole[3].reshape(shards, -1, blocks, width).transpose(0, 2, 1, 3).reshape(shards, -1, width),
            whole[4].reshape(shards, -1, width),
        ],
        axis=1,
    )
    return dict(me=jnp.zeros((1,), jnp.int32), slots=[[(i, i) for i in range(shards)]], pieces=whole[:3], feed=feed)


def sum_all(vector):
    count = lax.axis_size("dp")
    if count & (count - 1):
        return lax.psum(vector, "dp")
    bit = 1
    while bit < count:
        vector = vector + exchange(vector, lambda i: bit)
        bit *= 2
    return vector


def solution(mesh):
    rows = P("dp", None, None)
    in_specs = (rows, P("dp"), rows, rows, P("dp"), rows) + (P("dp", None),) * 4 + (P(),) * 9
    out_specs = (rows,) * 4 + (P(),) * 7
    return jax.shard_map(local, mesh=mesh, in_specs=in_specs, out_specs=out_specs, check_vma=False)
```

```python
from functools import partial

import jax
import jax.numpy as jnp
from jax import lax
from jax.experimental import pallas as pl
from jax.experimental.pallas import tpu as pltpu
from jax.sharding import PartitionSpec as P

HEADS = 16
HEAD_DIM = 64
BF = jnp.bfloat16
F32 = jnp.float32
VMEM_BYTES = 60 * 1024 * 1024
FEED_BLOCK = 1024


def dot(left, right):
    return lax.dot_general(left, right, (((1,), (0,)), ((), ())), preferred_element_type=F32)


def dot_t(left, right):
    return lax.dot_general(left, right, (((1,), (1,)), ((), ())), preferred_element_type=F32)


def sequences(short_seqs, short_len, long_seqs, long_len):
    spans = [(i * short_len, short_len) for i in range(short_seqs)]
    base = short_seqs * short_len
    return spans, [(base + i * long_len, long_len) for i in range(long_seqs)]


def row_mask(short_lengths, long_lengths, shape):
    short_seqs, short_len, long_seqs, long_len = shape
    pieces = []
    for count, length, refs in (
        (short_seqs, short_len, short_lengths),
        (long_seqs, long_len, long_lengths),
    ):
        for i in range(count):
            rows = lax.broadcasted_iota(jnp.int32, (length, 1), 0)
            pieces.append(jnp.where(rows < refs[i], 1.0, 0.0).astype(F32))
    return jnp.concatenate(pieces, axis=0)


def head_lanes(block, half):
    lanes = lax.broadcasted_iota(jnp.int32, block.shape, 1)
    keep = lanes < HEAD_DIM if half == 0 else lanes >= HEAD_DIM
    return jnp.where(keep, block, jnp.zeros_like(block))


def flip(block):
    return jnp.transpose(block, (1, 0))


def attention_forward_kernel(
    shape, slots, me, short_lengths, long_lengths, short_x, long_x, *refs,
):
    pieces, refs = refs[: 3 * len(slots)], refs[3 * len(slots) :]
    (
        qb, vb, ob, q_out, k_out, v_out, short_p, long_p, mixed_t, xhat_out, rstd_out, packed_out, output_out,
        x_all, mixed, packed, wo, in_sems, out_sems,
    ) = refs
    step = pl.program_id(0)
    steps = pl.num_programs(0)
    short_seqs, short_len, long_seqs, long_len = shape
    base = short_seqs * short_len
    width = q_out.shape[1]
    half_width = packed.shape[2]
    short_spans, long_spans = sequences(*shape)
    targets = (packed.at[0], packed.at[1], wo)

    @pl.when(step == 0)
    def _():
        for part in range(3):
            for ref, masks in zip(pieces[part::3], slots):
                tall = ref.shape[0] // len(masks)
                for slot, mask in enumerate(masks):
                    mask = jnp.where(jnp.bitwise_and(me[0], 1) == 0, mask[0], mask[1])
                    place = pl.multiple_of(jnp.bitwise_xor(me[0], mask) * tall, tall)
                    pltpu.make_async_copy(
                        ref.at[pl.ds(slot * tall, tall)], targets[part].at[pl.ds(place, tall)], in_sems.at[part]
                    ).start()
        x_all[:base, :] = short_x[...]
        x_all[base:, :] = long_x[...]

    keeps = [
        pltpu.make_async_copy(packed.at[0], packed_out.at[0], out_sems.at[0]),
        pltpu.make_async_copy(packed.at[1], packed_out.at[1], out_sems.at[1]),
        pltpu.make_async_copy(wo, output_out, out_sems.at[2]),
    ]
    for part, first_step in enumerate((0, steps // 2, steps - 1)):
        @pl.when(step == first_step)
        def _():
            pltpu.make_async_copy(targets[part], targets[part], in_sems.at[part]).wait()
            keeps[part].start()

    x = x_all[...]
    side = step // (steps // 2)
    turn = lax.rem(step, steps // 2)
    third = half_width // 3
    weight = lambda which: packed[side, :, pl.ds(pl.multiple_of(which * third + turn * width, width), width)]
    q_out[...] = ((dot(x, weight(0)) + qb[...]).astype(BF).astype(F32) * HEAD_DIM ** (-0.5)).astype(BF)
    k_out[...] = dot(x, weight(1)).astype(BF)
    v_out[...] = (dot(x, weight(2)) + vb[...]).astype(BF)
    groups = ((short_spans, short_lengths, short_p), (long_spans, long_lengths, long_p))
    pairs = range(width // 128)
    jobs = []
    for pair in pairs:
        lanes = slice(128 * pair, 128 * pair + 128)
        for spans, refs, probs in groups:
            for seq, (start, length) in enumerate(spans):
                k2 = k_out[start : start + length, lanes]
                usable = lax.broadcasted_iota(jnp.int32, (length, 1), 0) < refs[seq]
                block = min(length, 512)
                for half in range(2):
                    for at in range(0, length, block):
                        jobs.append(dict(pair=pair, probs=probs, seq=seq, start=start, length=length, usable=usable, half=half, at=at, block=block, lanes=lanes,
                            scores=dot_t(head_lanes(k2, half), q_out[start + at : start + at + block, lanes])))
    for job in jobs:
        scores = jnp.where(job["usable"], job["scores"], -1e30)
        top = jnp.max(scores, axis=0, keepdims=True)
        powers = jnp.exp(scores - top)
        total = jnp.sum(powers, axis=0, keepdims=True)
        job["prob"] = (powers * (1.0 / total)).astype(BF)
        job["probs"][job["seq"], 2 * job["pair"] + job["half"], :, job["at"] : job["at"] + job["block"]] = job["prob"]

    flipped = {pair: flip(v_out[:, 128 * pair : 128 * pair + 128]) for pair in pairs}
    for job in jobs:
        feature = 128 * job["pair"] + HEAD_DIM * job["half"]
        v_head = flipped[job["pair"]][HEAD_DIM * job["half"] : HEAD_DIM * job["half"] + HEAD_DIM, job["start"] : job["start"] + job["length"]]
        mixed_t[feature : feature + HEAD_DIM, job["start"] + job["at"] : job["start"] + job["at"] + job["block"]] = dot(v_head, job["prob"])
    for pair in pairs:
        offset = pl.multiple_of(step * width + 128 * pair, 128)
        mixed[:, pl.ds(offset, 128)] = flip(mixed_t[128 * pair : 128 * pair + 128, :]).astype(BF)

    @pl.when(step == steps - 1)
    def _():
        first_sum = x_all[...].astype(F32) + (dot(mixed[...], wo[...]) + ob[...])
        center = first_sum - jnp.mean(first_sum, axis=-1, keepdims=True)
        spread = jnp.mean(center * center, axis=-1, keepdims=True)
        rstd = lax.rsqrt(spread + 1e-06)
        xhat_out[...] = center * rstd
        rstd_out[...] = rstd
        for keep in keeps:
            keep.wait()


def attention_forward(shape, lengths, xs, weights, vectors):
    short_seqs, short_len, long_seqs, long_len = shape
    rows = short_seqs * short_len + long_seqs * long_len
    width = xs[0].shape[1]
    block = 256
    heads = block // HEAD_DIM
    steps = width // block
    whole = lambda shp: pl.BlockSpec(shp, lambda j: (0,) * len(shp))
    smem = pl.BlockSpec(memory_space=pltpu.SMEM)
    anywhere = pl.BlockSpec(memory_space=pl.ANY)
    row_block = pl.BlockSpec((1, block), lambda j: (0, j))
    out_col = pl.BlockSpec((rows, block), lambda j: (0, j))
    half_width = 3 * width // 2
    return pl.pallas_call(
        partial(attention_forward_kernel, shape, weights["slots"]),
        grid=(steps,),
        in_specs=[
            smem, smem, smem, whole(xs[0].shape), whole(xs[1].shape),
            *[anywhere] * len(weights["pieces"]), row_block, row_block, whole((1, width)),
        ],
        out_specs=[
            out_col, out_col, out_col,
            pl.BlockSpec((short_seqs, heads, short_len, short_len), lambda j: (0, j, 0, 0)),
            pl.BlockSpec((long_seqs, heads, long_len, long_len), lambda j: (0, j, 0, 0)),
            pl.BlockSpec((block, rows), lambda j: (j, 0)),
            whole((rows, width)), whole((rows, 1)), anywhere, anywhere,
        ],
        out_shape=[
            jax.ShapeDtypeStruct((rows, width), BF),
            jax.ShapeDtypeStruct((rows, width), BF),
            jax.ShapeDtypeStruct((rows, width), BF),
            jax.ShapeDtypeStruct((short_seqs, HEADS, short_len, short_len), BF),
            jax.ShapeDtypeStruct((long_seqs, HEADS, long_len, long_len), BF),
            jax.ShapeDtypeStruct((width, rows), F32),
            jax.ShapeDtypeStruct((rows, width), F32),
            jax.ShapeDtypeStruct((rows, 1), F32),
            jax.ShapeDtypeStruct((2, width, half_width), BF),
            jax.ShapeDtypeStruct((width, width), BF),
        ],
        scratch_shapes=[
            pltpu.VMEM((rows, width), BF), pltpu.VMEM((rows, width), BF),
            pltpu.VMEM((2, width, half_width), BF), pltpu.VMEM((width, width), BF),
            pltpu.SemaphoreType.DMA((3,)), pltpu.SemaphoreType.DMA((3,)),
        ],
        compiler_params=pltpu.CompilerParams(vmem_limit_bytes=VMEM_BYTES),
        cost_estimate=pl.CostEstimate(flops=36 * 10**9, bytes_accessed=40 * 10**6, transcendentals=5 * 10**6),
        name="attention_forward",
    )(
        weights["me"], *lengths, *xs, *weights["pieces"],
        vectors["query_bias"], vectors["value_bias"], vectors["output_bias"],
    )


def gelu_and_slope(value):
    share = 0.5 + 0.5 * lax.erf(value * 0.5 ** 0.5)
    density = jnp.exp2(value * (value * -0.7213475204444817)) * 0.3989422804014327
    return value * share, share + value * density


def inner_block(feed_w, block, turn):
    shards, _, width = feed_w.shape
    per = width // block
    return pl.BlockSpec((shards, width // shards, block), lambda j: (0, turn(j) // per, lax.rem(turn(j), per)))


def down_block(feed_w, block, turn):
    shards, tall, width = feed_w.shape
    tall = tall // 2
    return pl.BlockSpec((block // tall, tall, width), lambda j: (turn(j), 1, 0))


def norm_gradient(grad, xhat, rstd, gain):
    scaled = grad * gain
    mean = jnp.mean(scaled, axis=-1, keepdims=True)
    along = jnp.mean(scaled * xhat, axis=-1, keepdims=True)
    return rstd * (scaled - mean - xhat * along)


def fold(block):
    return jnp.sum(block.reshape(block.shape[0] // 8, 8, block.shape[1]), axis=0)


def feed_kernel(
    shape, steps, keep, xhat, rstd, short_ct, long_ct, wi, wd, wo, inner_bias,
    gain1, beta1, gain2, beta2, down_bias,
    short_out, long_out, grad_mixed, grad_first_sum, second_beta_sum, down_sum, inner_sum, first_beta_sum, output_sum,
    total, low, value, slope, sums,
):
    step = pl.program_id(0)
    short_seqs, short_len, long_seqs, long_len = shape
    base = short_seqs * short_len
    rows, width = xhat.shape
    chunk = 128
    wide = lambda ref: ref[...].reshape(width, -1)
    tall = lambda ref: ref[...].reshape(-1, width)

    def first_part():
        value[lax.rem(step, 2)] = dot(low[...], wide(wi)) + inner_bias[...]

    def second_part():
        act, slp = gelu_and_slope(value[lax.rem(step + 1, 2)])
        slope[step - 1] = slp.astype(BF)
        total[...] += dot(act.astype(BF), tall(wd))

    @pl.when(step == 0)
    def _():
        def body(i, _):
            here = pl.ds(pl.multiple_of(i * chunk, chunk), chunk)
            first = xhat[here, :] * gain1[...] + beta1[...]
            low[here, :] = first.astype(BF)
            total[here, :] = first + down_bias[...]
            return 0

        lax.fori_loop(0, rows // chunk, body, 0)
        first_part()

    @pl.when((step > 0) & (step < steps))
    def _():
        first_part()
        second_part()

    @pl.when(step == steps)
    def _():
        second_part()
        sums[...] = jnp.zeros_like(sums)

        def rows_of(source, out, start):
            def body(i, _):
                there = pl.ds(pl.multiple_of(i * chunk, chunk), chunk)
                here = pl.ds(pl.multiple_of(start + i * chunk, chunk), chunk)
                second = total[here, :]
                center = second - jnp.mean(second, axis=-1, keepdims=True)
                spread = jnp.mean(center * center, axis=-1, keepdims=True)
                rstd2 = lax.rsqrt(spread + 1e-06)
                xhat2 = center * rstd2
                usable = keep[here, :]
                out[there, :] = ((xhat2 * gain2[...] + beta2[...]) * usable).astype(BF)
                grad_out = source[there, :].astype(F32) * usable
                grad_second = norm_gradient(grad_out, xhat2, rstd2, gain2[...])
                rounded = grad_second.astype(BF)
                low[here, :] = rounded
                total[here, :] = grad_second
                sums[0] += fold(grad_out)
                sums[1] += fold(rounded.astype(F32))
                return 0

            lax.fori_loop(0, source.shape[0] // chunk, body, 0)

        rows_of(short_ct, short_out, 0)
        rows_of(long_ct, long_out, base)
        second_beta_sum[...] = jnp.sum(sums[0], axis=0, keepdims=True)
        down_sum[...] = jnp.sum(sums[1], axis=0, keepdims=True)

    @pl.when(step > steps)
    def _():
        grad_inner = (dot_t(low[...], tall(wd)) * slope[2 * steps - step].astype(F32)).astype(BF)
        inner_sum[...] = jnp.sum(grad_inner.astype(F32), axis=0, keepdims=True)
        total[...] += dot_t(grad_inner, wide(wi))

    @pl.when(step == 2 * steps)
    def _():
        sums[...] = jnp.zeros_like(sums)

        def body(i, _):
            here = pl.ds(pl.multiple_of(i * chunk, chunk), chunk)
            grad_first = total[here, :]
            result = norm_gradient(grad_first, xhat[here, :], rstd[here, :], gain1[...])
            grad_first_sum[here, :] = result
            branch = result.astype(BF)
            low[here, :] = branch
            sums[0] += fold(grad_first)
            sums[1] += fold(branch.astype(F32))
            return 0

        lax.fori_loop(0, rows // chunk, body, 0)
        first_beta_sum[...] = jnp.sum(sums[0], axis=0, keepdims=True)
        output_sum[...] = jnp.sum(sums[1], axis=0, keepdims=True)
        grad_mixed[...] = dot_t(low[...], wo[...]).astype(BF)


def feed_forward_and_back(shape, keep, xhat, rstd, cts, feed_w, output_w, vectors, block=FEED_BLOCK):
    rows, width = xhat.shape
    units = vectors["inner_bias"].shape[1]
    steps = units // block
    whole = lambda shp: pl.BlockSpec(shp, lambda j: (0,) * len(shp))
    vec = whole((1, width))
    back = lambda j: 2 * steps - j
    inner_turn = lambda j: jnp.where(j <= steps, jnp.minimum(j, steps - 1), back(j))
    down_turn = lambda j: jnp.where(j <= steps, jnp.maximum(j - 1, 0), back(j))
    vector_out = jax.ShapeDtypeStruct((1, width), F32)
    return pl.pallas_call(
        partial(feed_kernel, shape, steps),
        grid=(2 * steps + 1,),
        in_specs=[
            whole((rows, 1)), whole((rows, width)), whole((rows, 1)), whole(cts[0].shape), whole(cts[1].shape),
            inner_block(feed_w, block, inner_turn), down_block(feed_w, block, down_turn), whole((width, width)),
            pl.BlockSpec((1, block), lambda j: (0, jnp.minimum(j, steps - 1))), vec, vec, vec, vec, vec,
        ],
        out_specs=[
            whole(cts[0].shape), whole(cts[1].shape), whole((rows, width)), whole((rows, width)),
            vec, vec, pl.BlockSpec((1, block), lambda j: (0, jnp.minimum(back(j), steps - 1))), vec, vec,
        ],
        out_shape=[
            jax.ShapeDtypeStruct(cts[0].shape, BF), jax.ShapeDtypeStruct(cts[1].shape, BF),
            jax.ShapeDtypeStruct((rows, width), BF), jax.ShapeDtypeStruct((rows, width), F32),
            vector_out, vector_out, jax.ShapeDtypeStruct((1, units), F32), vector_out, vector_out,
        ],
        scratch_shapes=[
            pltpu.VMEM((rows, width), F32), pltpu.VMEM((rows, width), BF), pltpu.VMEM((2, rows, block), F32),
            pltpu.VMEM((steps, rows, block), BF), pltpu.VMEM((2, 8, width), F32),
        ],
        compiler_params=pltpu.CompilerParams(vmem_limit_bytes=VMEM_BYTES),
        cost_estimate=pl.CostEstimate(flops=65 * 10**9, bytes_accessed=60 * 10**6, transcendentals=4 * 10**6),
        name="feed_forward_and_back",
    )(
        keep, xhat, rstd, *cts, feed_w, feed_w, output_w, vectors["inner_bias"],
        vectors["first_gain"], vectors["first_beta"], vectors["second_gain"], vectors["second_beta"], vectors["down_bias"],
    )


def attention_backward_kernel(
    shape, short_lengths, long_lengths, q, k, v, gm, short_p, long_p, mixed_t, wq, wk, wv, grad_first_sum,
    short_grad, long_grad, query_sum, value_sum, grad_packed, total,
):
    step = pl.program_id(0)
    steps = pl.num_programs(0)
    short_seqs, short_len, long_seqs, long_len = shape
    base = short_seqs * short_len
    width = q.shape[1]
    short_spans, long_spans = sequences(*shape)
    scale = HEAD_DIM ** (-0.5)
    jobs = []
    for pair in range(width // 128):
        lanes = slice(128 * pair, 128 * pair + 128)
        for spans, probs in ((short_spans, short_p), (long_spans, long_p)):
            for seq, (start, length) in enumerate(spans):
                here = slice(start, start + length)
                for half in range(2):
                    jobs.append(dict(
                        pair=pair, here=here, lanes=lanes, half=half, probs=probs, seq=seq,
                        grad_p=dot_t(head_lanes(v[here, lanes], half), gm[here, lanes]),
                    ))
    flipped, delta = {}, {}
    for pair in range(width // 128):
        lanes = slice(128 * pair, 128 * pair + 128)
        flipped[pair] = flip(k[:, lanes])
        product = flip(gm[:, lanes]).astype(F32) * mixed_t[lanes, :]
        for half in range(2):
            delta[pair, half] = jnp.sum(product[HEAD_DIM * half : HEAD_DIM * half + HEAD_DIM], axis=0, keepdims=True)
    for job in jobs:
        pair, half = job["pair"], job["half"]
        prob = job["probs"][job["seq"], 2 * pair + half].astype(F32)
        job["grad_s"] = (prob * (job["grad_p"] - delta[pair, half][:, job["here"]])).astype(BF)
    for first, second in zip(jobs[0::2], jobs[1::2]):
        pair, here, lanes = first["pair"], first["here"], first["lanes"]
        grad_value = grad_key = None
        grad_query_t = []
        for job in (first, second):
            half = job["half"]
            prob = job["probs"][job["seq"], 2 * pair + half]
            dv = dot(prob, head_lanes(gm[here, lanes], half))
            dk = dot(job["grad_s"], head_lanes(q[here, lanes], half))
            grad_value = dv if half == 0 else grad_value + dv
            grad_key = dk if half == 0 else grad_key + dk
            grad_query_t.append(dot(flipped[pair][HEAD_DIM * half : HEAD_DIM * half + HEAD_DIM, here], job["grad_s"]))
        grad_packed[here, 128 * pair : 128 * pair + 128] = (
            flip(jnp.concatenate(grad_query_t, axis=0)) * scale
        ).astype(BF)
        grad_packed[here, width + 128 * pair : width + 128 * pair + 128] = grad_key.astype(BF)
        grad_packed[here, 2 * width + 128 * pair : 2 * width + 128 * pair + 128] = grad_value.astype(BF)
    query_sum[...] = jnp.sum(grad_packed[:, :width].astype(F32), axis=0, keepdims=True)
    value_sum[...] = jnp.sum(grad_packed[:, 2 * width :].astype(F32), axis=0, keepdims=True)
    part = (
        dot_t(grad_packed[:, :width], wq[0])
        + dot_t(grad_packed[:, width : 2 * width], wk[0])
        + dot_t(grad_packed[:, 2 * width :], wv[0])
    )

    @pl.when(step == 0)
    def _():
        total[...] = grad_first_sum[...] + part

    @pl.when(step > 0)
    def _():
        total[...] += part

    @pl.when(step == steps - 1)
    def _():
        keep = row_mask(short_lengths, long_lengths, shape)
        result = (total[...] * keep).astype(BF)
        short_grad[...] = result[:base]
        long_grad[...] = result[base:]


def attention_backward(shape, lengths, q, k, v, gm, short_p, long_p, mixed_t, packed_w, grad_first_sum):
    short_seqs, short_len, long_seqs, long_len = shape
    rows, width = q.shape
    block = 256
    heads = block // HEAD_DIM
    steps = width // block
    base = short_seqs * short_len
    whole = lambda shp: pl.BlockSpec(shp, lambda j: (0,) * len(shp))
    smem = pl.BlockSpec(memory_space=pltpu.SMEM)
    half = steps // 2
    column = lambda off: pl.BlockSpec((1, width, block), lambda j: (j // half, 0, lax.rem(j, half) + off * half))
    col = pl.BlockSpec((rows, block), lambda j: (0, j))
    vec = pl.BlockSpec((1, block), lambda j: (0, j))
    return pl.pallas_call(
        partial(attention_backward_kernel, shape),
        grid=(steps,),
        in_specs=[
            smem, smem, col, col, col, col,
            pl.BlockSpec((short_seqs, heads, short_len, short_len), lambda j: (0, j, 0, 0)),
            pl.BlockSpec((long_seqs, heads, long_len, long_len), lambda j: (0, j, 0, 0)),
            pl.BlockSpec((block, rows), lambda j: (j, 0)),
            column(0), column(1), column(2), whole((rows, width)),
        ],
        out_specs=[whole((base, width)), whole((rows - base, width)), vec, vec],
        out_shape=[
            jax.ShapeDtypeStruct((base, width), BF), jax.ShapeDtypeStruct((rows - base, width), BF),
            jax.ShapeDtypeStruct((1, width), F32), jax.ShapeDtypeStruct((1, width), F32),
        ],
        scratch_shapes=[pltpu.VMEM((rows, 3 * block), BF), pltpu.VMEM((rows, width), F32)],
        compiler_params=pltpu.CompilerParams(vmem_limit_bytes=VMEM_BYTES),
        name="attention_backward",
    )(*lengths, q, k, v, gm, short_p, long_p, mixed_t, packed_w, packed_w, packed_w, grad_first_sum)


def local(
    short_input, short_lengths, short_cotangent, long_input, long_lengths, long_cotangent,
    packed_weight, output_weight, inner_weight, down_weight,
    first_gain, second_gain, query_bias, value_bias, output_bias, inner_bias, down_bias, first_beta, second_beta,
):
    short_seqs, short_len, width = short_input.shape
    long_seqs, long_len, _ = long_input.shape
    shape = (short_seqs, short_len, long_seqs, long_len)
    lengths = (short_lengths, long_lengths)
    vectors = dict(
        first_gain=first_gain, second_gain=second_gain, query_bias=query_bias, value_bias=value_bias,
        output_bias=output_bias, inner_bias=inner_bias, down_bias=down_bias, first_beta=first_beta, second_beta=second_beta,
    )
    vectors = {name: item.reshape(1, -1) for name, item in vectors.items()}
    xs = (short_input.reshape(-1, width), long_input.reshape(-1, width))
    cts = (short_cotangent.reshape(-1, width), long_cotangent.reshape(-1, width))
    weights = gather_weights(packed_weight, output_weight, inner_weight, down_weight)
    q, k, v, short_p, long_p, mixed_t, xhat, rstd, packed_w, output_w = attention_forward(shape, lengths, xs, weights, vectors)
    keep = jnp.concatenate([
        (jnp.arange(item.shape[1])[None, :] < length[:, None]).reshape(-1, 1)
        for item, length in ((short_input, short_lengths), (long_input, long_lengths))
    ], axis=0).astype(F32)
    (
        short_out, long_out, gm, grad_first_sum, second_beta_sum, down_sum, inner_sum, first_beta_sum, output_sum,
    ) = feed_forward_and_back(shape, keep, xhat, rstd, cts, weights["feed"], output_w, vectors)
    short_grad, long_grad, query_sum, value_sum = attention_backward(
        shape, lengths, q, k, v, gm, short_p, long_p, mixed_t, packed_w, grad_first_sum
    )
    sums = sum_all(jnp.concatenate(
        [query_sum, value_sum, output_sum, inner_sum, down_sum, first_beta_sum, second_beta_sum], axis=1
    ).reshape(-1))
    outs = []
    at = 0
    for size in (width, width, width, inner_bias.shape[0], width, width, width):
        outs.append(lax.slice_in_dim(sums, at, at + size))
        at += size
    return (
        short_out.reshape(short_input.shape), short_grad.reshape(short_input.shape),
        long_out.reshape(long_input.shape), long_grad.reshape(long_input.shape), *outs,
    )


def exchange(block, mask):
    count = lax.axis_size("dp")
    return lax.ppermute(block, "dp", [(i, i ^ mask(i)) for i in range(count)])


CORE, X, Y, Z_NEAR, Z_FAR = 1, 2, 4, 8, 16


def side_first(index):
    return X if index & CORE == 0 else Y


def side_second(index):
    return Y if index & CORE == 0 else X


def gather_by_exchange(shard):
    held = jnp.concatenate([shard, exchange(shard, lambda i: Z_FAR)])
    held = jnp.concatenate([held, exchange(held, side_first)])
    held = jnp.concatenate([held, exchange(held, lambda i: Z_NEAR)])
    other = exchange(held, side_second)
    return [held, other, exchange(held, lambda i: CORE), exchange(other, lambda i: CORE)]


def exchange_slots():
    def mask(core, swap, far, slot):
        owner = core ^ swap
        return (
            swap * CORE + far * side_second(owner) + Z_FAR * (slot & 1)
            + side_first(owner) * (slot >> 1 & 1) + Z_NEAR * (slot >> 2)
        )

    return [
        [(mask(0, swap, far, slot), mask(1, swap, far, slot)) for slot in range(8)]
        for swap in (0, 1) for far in (0, 1)
    ]


def gather_weights(packed, output, inner, down):
    count = lax.axis_size("dp")
    width = output.shape[1]
    half = width // 2
    sides = [
        jnp.concatenate([packed[:, i * width + at : i * width + at + half] for i in range(3)], axis=1) for at in (0, half)
    ]
    parts = [*sides, output]
    tall = inner.shape[0]
    blocks = inner.shape[1] // width
    if count == 32:
        feed = jnp.concatenate(
            [inner.reshape(tall, blocks, width).transpose(1, 0, 2).reshape(blocks * tall, width), down], axis=0
        )
        feed = lax.all_gather(feed, "dp", axis=0, tiled=False)
        gathered = [gather_by_exchange(part) for part in parts]
        return dict(
            me=lax.axis_index("dp").reshape(1).astype(jnp.int32), slots=exchange_slots(),
            pieces=[gathered[part][piece] for piece in range(4) for part in range(3)], feed=feed,
        )
    whole = [lax.all_gather(part, "dp", axis=0, tiled=True) for part in (*parts, inner, down)]
    shards = 32
    feed = jnp.concatenate(
        [
            whole[3].reshape(shards, -1, blocks, width).transpose(0, 2, 1, 3).reshape(shards, -1, width),
            whole[4].reshape(shards, -1, width),
        ],
        axis=1,
    )
    return dict(me=jnp.zeros((1,), jnp.int32), slots=[[(i, i) for i in range(shards)]], pieces=whole[:3], feed=feed)


def sum_all(vector):
    count = lax.axis_size("dp")
    if count & (count - 1):
        return lax.psum(vector, "dp")
    bit = 1
    while bit < count:
        vector = vector + exchange(vector, lambda i: bit)
        bit *= 2
    return vector


def solution(mesh):
    rows = P("dp", None, None)
    in_specs = (rows, P("dp"), rows, rows, P("dp"), rows) + (P("dp", None),) * 4 + (P(),) * 9
    out_specs = (rows,) * 4 + (P(),) * 7
    return jax.shard_map(local, mesh=mesh, in_specs=in_specs, out_specs=out_specs, check_vma=False)
```

```python
from functools import partial

import jax
import jax.numpy as jnp
from jax import lax
from jax.experimental import pallas as pl
from jax.experimental.pallas import tpu as pltpu
from jax.sharding import PartitionSpec as P

HEADS = 16
HEAD_DIM = 64
BF = jnp.bfloat16
F32 = jnp.float32
VMEM_BYTES = 60 * 1024 * 1024
FEED_BLOCK = 1024
TAIL_VMEM_BYTES = 63 * 1024 * 1024


def dot(left, right):
    return lax.dot_general(left, right, (((1,), (0,)), ((), ())), preferred_element_type=F32)


def dot_t(left, right):
    return lax.dot_general(left, right, (((1,), (1,)), ((), ())), preferred_element_type=F32)


def sequences(short_seqs, short_len, long_seqs, long_len):
    spans = [(i * short_len, short_len) for i in range(short_seqs)]
    base = short_seqs * short_len
    return spans, [(base + i * long_len, long_len) for i in range(long_seqs)]


def row_mask(short_lengths, long_lengths, shape):
    short_seqs, short_len, long_seqs, long_len = shape
    pieces = []
    for count, length, refs in (
        (short_seqs, short_len, short_lengths),
        (long_seqs, long_len, long_lengths),
    ):
        for i in range(count):
            rows = lax.broadcasted_iota(jnp.int32, (length, 1), 0)
            pieces.append(jnp.where(rows < refs[i], 1.0, 0.0).astype(F32))
    return jnp.concatenate(pieces, axis=0)


def head_lanes(block, half):
    lanes = lax.broadcasted_iota(jnp.int32, block.shape, 1)
    keep = lanes < HEAD_DIM if half == 0 else lanes >= HEAD_DIM
    return jnp.where(keep, block, jnp.zeros_like(block))


def flip(block):
    return jnp.transpose(block, (1, 0))


def attention_forward_kernel(
    shape, slots, me, short_lengths, long_lengths, short_x, long_x, *refs,
):
    pieces, refs = refs[: 3 * len(slots)], refs[3 * len(slots) :]
    (
        qb, vb, ob, gain1, beta1, q_out, k_out, v_out, short_p, long_p, mixed_t, xhat_out, rstd_out, first_out,
        packed_out, output_out,
        x_all, mixed, packed, wo, in_sems, out_sems,
    ) = refs
    step = pl.program_id(0)
    steps = pl.num_programs(0)
    short_seqs, short_len, long_seqs, long_len = shape
    base = short_seqs * short_len
    width = q_out.shape[1]
    half_width = packed.shape[2]
    short_spans, long_spans = sequences(*shape)
    targets = (packed.at[0], packed.at[1], wo)

    @pl.when(step == 0)
    def _():
        for part in range(3):
            for ref, masks in zip(pieces[part::3], slots):
                tall = ref.shape[0] // len(masks)
                for slot, mask in enumerate(masks):
                    mask = jnp.where(jnp.bitwise_and(me[0], 1) == 0, mask[0], mask[1])
                    place = pl.multiple_of(jnp.bitwise_xor(me[0], mask) * tall, tall)
                    pltpu.make_async_copy(
                        ref.at[pl.ds(slot * tall, tall)], targets[part].at[pl.ds(place, tall)], in_sems.at[part]
                    ).start()
        x_all[:base, :] = short_x[...]
        x_all[base:, :] = long_x[...]

    keeps = [
        pltpu.make_async_copy(packed.at[0], packed_out.at[0], out_sems.at[0]),
        pltpu.make_async_copy(packed.at[1], packed_out.at[1], out_sems.at[1]),
        pltpu.make_async_copy(wo, output_out, out_sems.at[2]),
    ]
    for part, first_step in enumerate((0, steps // 2, steps - 1)):
        @pl.when(step == first_step)
        def _():
            pltpu.make_async_copy(targets[part], targets[part], in_sems.at[part]).wait()
            keeps[part].start()

    x = x_all[...]
    side = step // (steps // 2)
    turn = lax.rem(step, steps // 2)
    third = half_width // 3
    weight = lambda which: packed[side, :, pl.ds(pl.multiple_of(which * third + turn * width, width), width)]
    q_out[...] = ((dot(x, weight(0)) + qb[...]).astype(BF).astype(F32) * HEAD_DIM ** (-0.5)).astype(BF)
    k_out[...] = dot(x, weight(1)).astype(BF)
    v_out[...] = (dot(x, weight(2)) + vb[...]).astype(BF)
    groups = ((short_spans, short_lengths, short_p), (long_spans, long_lengths, long_p))
    pairs = range(width // 128)
    jobs = []
    for pair in pairs:
        lanes = slice(128 * pair, 128 * pair + 128)
        for spans, refs, probs in groups:
            for seq, (start, length) in enumerate(spans):
                k2 = k_out[start : start + length, lanes]
                usable = lax.broadcasted_iota(jnp.int32, (length, 1), 0) < refs[seq]
                block = min(length, 512)
                for half in range(2):
                    for at in range(0, length, block):
                        jobs.append(dict(pair=pair, probs=probs, seq=seq, start=start, length=length, usable=usable, half=half, at=at, block=block, lanes=lanes,
                            scores=dot_t(head_lanes(k2, half), q_out[start + at : start + at + block, lanes])))
    for job in jobs:
        scores = jnp.where(job["usable"], job["scores"], -1e30)
        top = jnp.max(scores, axis=0, keepdims=True)
        powers = jnp.exp(scores - top)
        total = jnp.sum(powers, axis=0, keepdims=True)
        job["prob"] = (powers * (1.0 / total)).astype(BF)
        job["probs"][job["seq"], 2 * job["pair"] + job["half"], :, job["at"] : job["at"] + job["block"]] = job["prob"]

    flipped = {pair: flip(v_out[:, 128 * pair : 128 * pair + 128]) for pair in pairs}
    for job in jobs:
        feature = 128 * job["pair"] + HEAD_DIM * job["half"]
        v_head = flipped[job["pair"]][HEAD_DIM * job["half"] : HEAD_DIM * job["half"] + HEAD_DIM, job["start"] : job["start"] + job["length"]]
        mixed_t[feature : feature + HEAD_DIM, job["start"] + job["at"] : job["start"] + job["at"] + job["block"]] = dot(v_head, job["prob"])
    for pair in pairs:
        offset = pl.multiple_of(step * width + 128 * pair, 128)
        mixed[:, pl.ds(offset, 128)] = flip(mixed_t[128 * pair : 128 * pair + 128, :]).astype(BF)

    @pl.when(step == steps - 1)
    def _():
        first_sum = x_all[...].astype(F32) + (dot(mixed[...], wo[...]) + ob[...])
        center = first_sum - jnp.mean(first_sum, axis=-1, keepdims=True)
        spread = jnp.mean(center * center, axis=-1, keepdims=True)
        rstd = lax.rsqrt(spread + 1e-06)
        xhat = center * rstd
        xhat_out[...] = xhat
        rstd_out[...] = rstd
        first_out[...] = (xhat * gain1[...] + beta1[...]).astype(BF)
        for keep in keeps:
            keep.wait()


def attention_forward(shape, lengths, xs, weights, vectors):
    short_seqs, short_len, long_seqs, long_len = shape
    rows = short_seqs * short_len + long_seqs * long_len
    width = xs[0].shape[1]
    block = 256
    heads = block // HEAD_DIM
    steps = width // block
    whole = lambda shp: pl.BlockSpec(shp, lambda j: (0,) * len(shp))
    smem = pl.BlockSpec(memory_space=pltpu.SMEM)
    anywhere = pl.BlockSpec(memory_space=pl.ANY)
    row_block = pl.BlockSpec((1, block), lambda j: (0, j))
    out_col = pl.BlockSpec((rows, block), lambda j: (0, j))
    half_width = 3 * width // 2
    return pl.pallas_call(
        partial(attention_forward_kernel, shape, weights["slots"]),
        grid=(steps,),
        in_specs=[
            smem, smem, smem, whole(xs[0].shape), whole(xs[1].shape),
            *[anywhere] * len(weights["pieces"]), row_block, row_block, *[whole((1, width))] * 3,
        ],
        out_specs=[
            out_col, out_col, out_col,
            pl.BlockSpec((short_seqs, heads, short_len, short_len), lambda j: (0, j, 0, 0)),
            pl.BlockSpec((long_seqs, heads, long_len, long_len), lambda j: (0, j, 0, 0)),
            pl.BlockSpec((block, rows), lambda j: (j, 0)),
            whole((rows, width)), whole((rows, 1)), whole((rows, width)), anywhere, anywhere,
        ],
        out_shape=[
            jax.ShapeDtypeStruct((rows, width), BF),
            jax.ShapeDtypeStruct((rows, width), BF),
            jax.ShapeDtypeStruct((rows, width), BF),
            jax.ShapeDtypeStruct((short_seqs, HEADS, short_len, short_len), BF),
            jax.ShapeDtypeStruct((long_seqs, HEADS, long_len, long_len), BF),
            jax.ShapeDtypeStruct((width, rows), F32),
            jax.ShapeDtypeStruct((rows, width), F32),
            jax.ShapeDtypeStruct((rows, 1), F32),
            jax.ShapeDtypeStruct((rows, width), BF),
            jax.ShapeDtypeStruct((2, width, half_width), BF),
            jax.ShapeDtypeStruct((width, width), BF),
        ],
        scratch_shapes=[
            pltpu.VMEM((rows, width), BF), pltpu.VMEM((rows, width), BF),
            pltpu.VMEM((2, width, half_width), BF), pltpu.VMEM((width, width), BF),
            pltpu.SemaphoreType.DMA((3,)), pltpu.SemaphoreType.DMA((3,)),
        ],
        compiler_params=pltpu.CompilerParams(vmem_limit_bytes=VMEM_BYTES),
        cost_estimate=pl.CostEstimate(flops=36 * 10**9, bytes_accessed=40 * 10**6, transcendentals=5 * 10**6),
        name="attention_forward",
    )(
        weights["me"], *lengths, *xs, *weights["pieces"],
        vectors["query_bias"], vectors["value_bias"], vectors["output_bias"],
        vectors["first_gain"], vectors["first_beta"],
    )


def gelu_and_slope(value):
    share = 0.5 + 0.5 * lax.erf(value * 0.5 ** 0.5)
    density = jnp.exp2(value * (value * -0.7213475204444817)) * 0.3989422804014327
    return value * share, share + value * density


def inner_block(feed_w, block, turn):
    shards, _, width = feed_w.shape
    per = width // block
    return pl.BlockSpec((shards, width // shards, block), lambda j: (0, turn(j) // per, lax.rem(turn(j), per)))


def down_block(feed_w, block, turn):
    shards, tall, width = feed_w.shape
    tall = tall // 2
    return pl.BlockSpec((block // tall, tall, width), lambda j: (turn(j), 1, 0))


def norm_gradient(grad, xhat, rstd, gain):
    scaled = grad * gain
    mean = jnp.mean(scaled, axis=-1, keepdims=True)
    along = jnp.mean(scaled * xhat, axis=-1, keepdims=True)
    return rstd * (scaled - mean - xhat * along)


def fold(block):
    return jnp.sum(block.reshape(block.shape[0] // 8, 8, block.shape[1]), axis=0)


def tail_kernel(
    shape, steps, keep, rstd, first, wi, wd, inner_bias, gain1, beta1, gain2, beta2, down_bias,
    xhat_in, short_ct, long_ct, wo_in, q_in, k_in, v_in, short_p_in, long_p_in, mixed_t_in, packed_in,
    short_out, long_out, short_grad, long_grad, sums_out,
    total, low, value, slope, sums, xhat, ct, wo, short_p, long_p, mixed_t, packed, gm, sems, load_sems,
):
    step = pl.program_id(0)
    short_seqs, short_len, long_seqs, long_len = shape
    base = short_seqs * short_len
    rows, width = total.shape
    units = steps * value.shape[2]
    part = packed.shape[3]
    attention_steps = width // part
    heads = part // HEAD_DIM
    first_attention = 2 * steps + 1
    turn = step - first_attention
    slot = lax.rem(jnp.maximum(turn, 0), 2)
    chunk = 128
    wide = lambda ref: ref[...].reshape(width, -1)
    tall = lambda ref: ref[...].reshape(-1, width)
    short_spans, long_spans = sequences(*shape)

    early = [
        pltpu.make_async_copy(short_ct, ct.at[:base], sems.at[0]),
        pltpu.make_async_copy(long_ct, ct.at[base:], sems.at[1]),
        pltpu.make_async_copy(xhat_in, xhat, sems.at[2]),
        pltpu.make_async_copy(wo_in, wo, sems.at[3]),
    ]
    outs = [
        pltpu.make_async_copy(ct.at[:base], short_out, sems.at[4]),
        pltpu.make_async_copy(ct.at[base:], long_out, sems.at[5]),
    ]
    grads = [
        pltpu.make_async_copy(low.at[:base], short_grad, sems.at[6]),
        pltpu.make_async_copy(low.at[base:], long_grad, sems.at[7]),
    ]

    def loads(at, into):
        columns = pl.ds(pl.multiple_of(at * part, part), part)
        side = at // (attention_steps // 2)
        within = lax.rem(at, attention_steps // 2)
        third = packed_in.shape[2] // 3
        pairs = [(ref.at[:, columns], slope.at[3 - into, :, part * i : part * i + part]) for i, ref in enumerate((q_in, k_in, v_in))]
        pairs += [
            (short_p_in.at[:, pl.ds(at * heads, heads)], short_p.at[into]),
            (long_p_in.at[:, pl.ds(at * heads, heads)], long_p.at[into]),
            (mixed_t_in.at[columns], mixed_t.at[into]),
        ]
        pairs += [
            (
                packed_in.at[side, :, pl.ds(pl.multiple_of(i * third + within * part, part), part)],
                packed.at[into, i],
            )
            for i in range(3)
        ]
        return [pltpu.make_async_copy(a, b, load_sems.at[into, i]) for i, (a, b) in enumerate(pairs)]

    def first_part():
        value[lax.rem(step, 2)] = dot(first[...], wide(wi)) + inner_bias[...]

    def second_part():
        act, slp = gelu_and_slope(value[lax.rem(step + 1, 2)])
        slope[step - 1] = slp.astype(BF)
        total[...] += dot(act.astype(BF), tall(wd))

    @pl.when(step == 0)
    def _():
        for copy in early:
            copy.start()
        first_part()
        total[...] = jnp.broadcast_to(down_bias[...], total.shape)

    @pl.when((step > 0) & (step < steps))
    def _():
        first_part()
        second_part()

    @pl.when(step == steps)
    def _():
        for copy in early[:3]:
            copy.wait()
        second_part()
        sums[...] = jnp.zeros_like(sums)

        def body(i, _):
            here = pl.ds(pl.multiple_of(i * chunk, chunk), chunk)
            second = total[here, :] + (xhat[here, :] * gain1[...] + beta1[...])
            center = second - jnp.mean(second, axis=-1, keepdims=True)
            spread = jnp.mean(center * center, axis=-1, keepdims=True)
            rstd2 = lax.rsqrt(spread + 1e-06)
            xhat2 = center * rstd2
            usable = keep[here, :]
            grad_out = ct[here, :].astype(F32) * usable
            ct[here, :] = ((xhat2 * gain2[...] + beta2[...]) * usable).astype(BF)
            grad_second = norm_gradient(grad_out, xhat2, rstd2, gain2[...])
            rounded = grad_second.astype(BF)
            low[here, :] = rounded
            total[here, :] = grad_second
            sums[0] += fold(grad_out)
            sums[1] += fold(rounded.astype(F32))
            return 0

        lax.fori_loop(0, rows // chunk, body, 0)
        for copy in outs:
            copy.start()
        sums_out[:, 5 * width + units : 6 * width + units] = jnp.sum(sums[0], axis=0, keepdims=True)
        sums_out[:, 3 * width + units : 4 * width + units] = jnp.sum(sums[1], axis=0, keepdims=True)

    @pl.when((step > steps) & (step <= 2 * steps))
    def _():
        grad_inner = (dot_t(low[...], tall(wd)) * slope[2 * steps - step].astype(F32)).astype(BF)
        place = pl.multiple_of(3 * width + (2 * steps - step) * wd.shape[0] * wd.shape[1], 128)
        sums_out[:, pl.ds(place, value.shape[2])] = jnp.sum(grad_inner.astype(F32), axis=0, keepdims=True)
        total[...] += dot_t(grad_inner, wide(wi))

    @pl.when(step == 2 * steps - 1)
    def _():
        for copy in loads(0, 0):
            copy.start()

    @pl.when(step == 2 * steps)
    def _():
        for copy in loads(1, 1):
            copy.start()
        sums[...] = jnp.zeros_like(sums)

        def body(i, _):
            here = pl.ds(pl.multiple_of(i * chunk, chunk), chunk)
            grad_first = total[here, :]
            result = norm_gradient(grad_first, xhat[here, :], rstd[here, :], gain1[...])
            total[here, :] = result
            branch = result.astype(BF)
            low[here, :] = branch
            sums[0] += fold(grad_first)
            sums[1] += fold(branch.astype(F32))
            return 0

        lax.fori_loop(0, rows // chunk, body, 0)
        sums_out[:, 4 * width + units : 5 * width + units] = jnp.sum(sums[0], axis=0, keepdims=True)
        sums_out[:, 2 * width : 3 * width] = jnp.sum(sums[1], axis=0, keepdims=True)
        early[3].wait()
        gm[...] = dot_t(low[...], wo[...]).astype(BF)

    @pl.when(turn >= 0)
    def _():
        for copy in loads(turn, slot):
            copy.wait()
        scale = HEAD_DIM ** (-0.5)
        own = 3 - slot
        q = lambda here, lanes: slope[own, here, lanes]
        k = lambda here, lanes: slope[own, here, slice(part + lanes.start, part + lanes.stop)]
        v = lambda here, lanes: slope[own, here, slice(2 * part + lanes.start, 2 * part + lanes.stop)]
        grad = lambda here, lanes: slope[1, here, slice(3 * part + lanes.start, 3 * part + lanes.stop)]
        slope[1, :, 3 * part : 4 * part] = gm[:, pl.ds(pl.multiple_of(turn * part, part), part)]
        everything = slice(0, rows)
        jobs = []
        for pair in range(part // 128):
            lanes = slice(128 * pair, 128 * pair + 128)
            for spans, probs in ((short_spans, short_p), (long_spans, long_p)):
                for seq, (start, length) in enumerate(spans):
                    here = slice(start, start + length)
                    for half in range(2):
                        jobs.append(dict(
                            pair=pair, here=here, lanes=lanes, half=half, probs=probs, seq=seq,
                            grad_p=dot_t(head_lanes(v(here, lanes), half), grad(here, lanes)),
                        ))
        flipped, delta = {}, {}
        for pair in range(part // 128):
            lanes = slice(128 * pair, 128 * pair + 128)
            flipped[pair] = flip(k(everything, lanes))
            product = flip(grad(everything, lanes)).astype(F32) * mixed_t[slot, lanes, :]
            for half in range(2):
                delta[pair, half] = jnp.sum(product[HEAD_DIM * half : HEAD_DIM * half + HEAD_DIM], axis=0, keepdims=True)
        for job in jobs:
            pair, half = job["pair"], job["half"]
            prob = job["probs"][slot, job["seq"], 2 * pair + half].astype(F32)
            job["grad_s"] = (prob * (job["grad_p"] - delta[pair, half][:, job["here"]])).astype(BF)
        for one, two in zip(jobs[0::2], jobs[1::2]):
            pair, here, lanes = one["pair"], one["here"], one["lanes"]
            grad_value = grad_key = None
            grad_query_t = []
            for job in (one, two):
                half = job["half"]
                prob = job["probs"][slot, job["seq"], 2 * pair + half]
                dv = dot(prob, head_lanes(grad(here, lanes), half))
                dk = dot(job["grad_s"], head_lanes(q(here, lanes), half))
                grad_value = dv if half == 0 else grad_value + dv
                grad_key = dk if half == 0 else grad_key + dk
                grad_query_t.append(dot(flipped[pair][HEAD_DIM * half : HEAD_DIM * half + HEAD_DIM, here], job["grad_s"]))
            slope[1, here, 128 * pair : 128 * pair + 128] = (flip(jnp.concatenate(grad_query_t, axis=0)) * scale).astype(BF)
            slope[1, here, part + 128 * pair : part + 128 * pair + 128] = grad_key.astype(BF)
            slope[1, here, 2 * part + 128 * pair : 2 * part + 128 * pair + 128] = grad_value.astype(BF)
        place = pl.multiple_of(turn * part, part)
        sums_out[:, pl.ds(place, part)] = jnp.sum(slope[1, :, :part].astype(F32), axis=0, keepdims=True)
        sums_out[:, pl.ds(width + place, part)] = jnp.sum(slope[1, :, 2 * part : 3 * part].astype(F32), axis=0, keepdims=True)
        total[...] += (
            dot_t(slope[1, :, :part], packed[slot, 0])
            + dot_t(slope[1, :, part : 2 * part], packed[slot, 1])
            + dot_t(slope[1, :, 2 * part : 3 * part], packed[slot, 2])
        )

    @pl.when((turn >= 0) & (turn < attention_steps - 2))
    def _():
        for copy in loads(turn + 2, slot):
            copy.start()

    @pl.when(turn == attention_steps - 1)
    def _():
        low[...] = (total[...] * keep[...]).astype(BF)
        for copy in grads:
            copy.start()
        for copy in outs + grads:
            copy.wait()


def feed_and_attention_backward(shape, keep, attention, cts, feed_w, vectors, block=FEED_BLOCK):
    q, k, v, short_p, long_p, mixed_t, xhat, rstd, first, packed_w, output_w = attention
    short_seqs, short_len, long_seqs, long_len = shape
    rows, width = xhat.shape
    base = short_seqs * short_len
    units = vectors["inner_bias"].shape[1]
    steps = units // block
    part = 256
    heads = part // HEAD_DIM
    once = pl.Buffered(1)
    whole = lambda shp: pl.BlockSpec(shp, lambda j: (0,) * len(shp), pipeline_mode=once)
    vec = whole((1, width))
    anywhere = pl.BlockSpec(memory_space=pl.ANY)
    back = lambda j: jnp.maximum(2 * steps - j, 0)
    inner_turn = lambda j: jnp.where(j <= steps, jnp.minimum(j, steps - 1), back(j))
    down_turn = lambda j: jnp.where(j <= steps, jnp.maximum(j - 1, 0), back(j))
    total_width = 6 * width + units
    return pl.pallas_call(
        partial(tail_kernel, shape, steps),
        grid=(2 * steps + 1 + width // part,),
        in_specs=[
            whole((rows, 1)), whole((rows, 1)), whole((rows, width)),
            inner_block(feed_w, block, inner_turn), down_block(feed_w, block, down_turn),
            pl.BlockSpec((1, block), lambda j: (0, jnp.minimum(j, steps - 1))), vec, vec, vec, vec, vec,
            *[anywhere] * 11,
        ],
        out_specs=[anywhere] * 4 + [pl.BlockSpec((1, total_width), lambda j: (0, 0))],
        out_shape=[
            jax.ShapeDtypeStruct(cts[0].shape, BF), jax.ShapeDtypeStruct(cts[1].shape, BF),
            jax.ShapeDtypeStruct(cts[0].shape, BF), jax.ShapeDtypeStruct(cts[1].shape, BF),
            jax.ShapeDtypeStruct((1, total_width), F32),
        ],
        scratch_shapes=[
            pltpu.VMEM((rows, width), F32), pltpu.VMEM((rows, width), BF), pltpu.VMEM((2, rows, block), F32),
            pltpu.VMEM((steps, rows, block), BF), pltpu.VMEM((2, 8, width), F32),
            pltpu.VMEM((rows, width), F32), pltpu.VMEM((rows, width), BF), pltpu.VMEM((width, width), BF),
            pltpu.VMEM((2, short_seqs, heads, short_len, short_len), BF),
            pltpu.VMEM((2, long_seqs, heads, long_len, long_len), BF),
            pltpu.VMEM((2, part, rows), F32), pltpu.VMEM((2, 3, width, part), BF), pltpu.VMEM((rows, width), BF),
            pltpu.SemaphoreType.DMA((8,)), pltpu.SemaphoreType.DMA((2, 9)),
        ],
        compiler_params=pltpu.CompilerParams(vmem_limit_bytes=TAIL_VMEM_BYTES),
        cost_estimate=pl.CostEstimate(flops=85 * 10**9, bytes_accessed=90 * 10**6, transcendentals=4 * 10**6),
        name="feed_and_attention_backward",
    )(
        keep, rstd, first, feed_w, feed_w, vectors["inner_bias"],
        vectors["first_gain"], vectors["first_beta"], vectors["second_gain"], vectors["second_beta"], vectors["down_bias"],
        xhat, *cts, output_w, q, k, v, short_p, long_p, mixed_t, packed_w,
    )


def local(
    short_input, short_lengths, short_cotangent, long_input, long_lengths, long_cotangent,
    packed_weight, output_weight, inner_weight, down_weight,
    first_gain, second_gain, query_bias, value_bias, output_bias, inner_bias, down_bias, first_beta, second_beta,
):
    short_seqs, short_len, width = short_input.shape
    long_seqs, long_len, _ = long_input.shape
    shape = (short_seqs, short_len, long_seqs, long_len)
    lengths = (short_lengths, long_lengths)
    vectors = dict(
        first_gain=first_gain, second_gain=second_gain, query_bias=query_bias, value_bias=value_bias,
        output_bias=output_bias, inner_bias=inner_bias, down_bias=down_bias, first_beta=first_beta, second_beta=second_beta,
    )
    vectors = {name: item.reshape(1, -1) for name, item in vectors.items()}
    xs = (short_input.reshape(-1, width), long_input.reshape(-1, width))
    cts = (short_cotangent.reshape(-1, width), long_cotangent.reshape(-1, width))
    weights = gather_weights(packed_weight, output_weight, inner_weight, down_weight)
    attention = attention_forward(shape, lengths, xs, weights, vectors)
    keep = jnp.concatenate([
        (jnp.arange(item.shape[1])[None, :] < length[:, None]).reshape(-1, 1)
        for item, length in ((short_input, short_lengths), (long_input, long_lengths))
    ], axis=0).astype(F32)
    short_out, long_out, short_grad, long_grad, sums = feed_and_attention_backward(
        shape, keep, attention, cts, weights["feed"], vectors
    )
    sums = sum_all(sums).reshape(-1)
    outs = []
    at = 0
    for size in (width, width, width, inner_bias.shape[0], width, width, width):
        outs.append(lax.slice_in_dim(sums, at, at + size))
        at += size
    return (
        short_out.reshape(short_input.shape), short_grad.reshape(short_input.shape),
        long_out.reshape(long_input.shape), long_grad.reshape(long_input.shape), *outs,
    )


def exchange(block, mask):
    count = lax.axis_size("dp")
    return lax.ppermute(block, "dp", [(i, i ^ mask(i)) for i in range(count)])


CORE, X, Y, Z_NEAR, Z_FAR = 1, 2, 4, 8, 16


def side_first(index):
    return X if index & CORE == 0 else Y


def side_second(index):
    return Y if index & CORE == 0 else X


def gather_by_exchange(shard):
    held = jnp.concatenate([shard, exchange(shard, lambda i: Z_FAR)])
    held = jnp.concatenate([held, exchange(held, side_first)])
    held = jnp.concatenate([held, exchange(held, lambda i: Z_NEAR)])
    other = exchange(held, side_second)
    return [held, other, exchange(held, lambda i: CORE), exchange(other, lambda i: CORE)]


def exchange_slots():
    def mask(core, swap, far, slot):
        owner = core ^ swap
        return (
            swap * CORE + far * side_second(owner) + Z_FAR * (slot & 1)
            + side_first(owner) * (slot >> 1 & 1) + Z_NEAR * (slot >> 2)
        )

    return [
        [(mask(0, swap, far, slot), mask(1, swap, far, slot)) for slot in range(8)]
        for swap in (0, 1) for far in (0, 1)
    ]


def gather_weights(packed, output, inner, down):
    count = lax.axis_size("dp")
    width = output.shape[1]
    half = width // 2
    sides = [
        jnp.concatenate([packed[:, i * width + at : i * width + at + half] for i in range(3)], axis=1) for at in (0, half)
    ]
    parts = [*sides, output]
    tall = inner.shape[0]
    blocks = inner.shape[1] // width
    if count == 32:
        feed = jnp.concatenate(
            [inner.reshape(tall, blocks, width).transpose(1, 0, 2).reshape(blocks * tall, width), down], axis=0
        )
        feed = lax.all_gather(feed, "dp", axis=0, tiled=False)
        gathered = [gather_by_exchange(part) for part in parts]
        return dict(
            me=lax.axis_index("dp").reshape(1).astype(jnp.int32), slots=exchange_slots(),
            pieces=[gathered[part][piece] for piece in range(4) for part in range(3)], feed=feed,
        )
    whole = [lax.all_gather(part, "dp", axis=0, tiled=True) for part in (*parts, inner, down)]
    shards = 32
    feed = jnp.concatenate(
        [
            whole[3].reshape(shards, -1, blocks, width).transpose(0, 2, 1, 3).reshape(shards, -1, width),
            whole[4].reshape(shards, -1, width),
        ],
        axis=1,
    )
    return dict(me=jnp.zeros((1,), jnp.int32), slots=[[(i, i) for i in range(shards)]], pieces=whole[:3], feed=feed)


def sum_all(vector):
    count = lax.axis_size("dp")
    if count & (count - 1):
        return lax.psum(vector, "dp")
    bit = 1
    while bit < count:
        vector = vector + exchange(vector, lambda i: bit)
        bit *= 2
    return vector


def solution(mesh):
    rows = P("dp", None, None)
    in_specs = (rows, P("dp"), rows, rows, P("dp"), rows) + (P("dp", None),) * 4 + (P(),) * 9
    out_specs = (rows,) * 4 + (P(),) * 7
    return jax.shard_map(local, mesh=mesh, in_specs=in_specs, out_specs=out_specs, check_vma=False)
```

```python
from functools import partial

import jax
import jax.numpy as jnp
from jax import lax
from jax.experimental import pallas as pl
from jax.experimental.pallas import tpu as pltpu
from jax.sharding import PartitionSpec as P

HEADS = 16
HEAD_DIM = 64
BF = jnp.bfloat16
F32 = jnp.float32
VMEM_BYTES = 60 * 1024 * 1024
FEED_BLOCK = 1024
TAIL_VMEM_BYTES = 63 * 1024 * 1024


def dot(left, right):
    return lax.dot_general(left, right, (((1,), (0,)), ((), ())), preferred_element_type=F32)


def dot_t(left, right):
    return lax.dot_general(left, right, (((1,), (1,)), ((), ())), preferred_element_type=F32)


def sequences(short_seqs, short_len, long_seqs, long_len):
    spans = [(i * short_len, short_len) for i in range(short_seqs)]
    base = short_seqs * short_len
    return spans, [(base + i * long_len, long_len) for i in range(long_seqs)]


def row_mask(short_lengths, long_lengths, shape):
    short_seqs, short_len, long_seqs, long_len = shape
    pieces = []
    for count, length, refs in (
        (short_seqs, short_len, short_lengths),
        (long_seqs, long_len, long_lengths),
    ):
        for i in range(count):
            rows = lax.broadcasted_iota(jnp.int32, (length, 1), 0)
            pieces.append(jnp.where(rows < refs[i], 1.0, 0.0).astype(F32))
    return jnp.concatenate(pieces, axis=0)


def head_lanes(block, half):
    lanes = lax.broadcasted_iota(jnp.int32, block.shape, 1)
    keep = lanes < HEAD_DIM if half == 0 else lanes >= HEAD_DIM
    return jnp.where(keep, block, jnp.zeros_like(block))


def flip(block):
    return jnp.transpose(block, (1, 0))


def attention_forward_kernel(
    shape, slots, me, short_lengths, long_lengths, short_x, long_x, *refs,
):
    pieces, refs = refs[: 3 * len(slots)], refs[3 * len(slots) :]
    (
        qb, vb, ob, gain1, beta1, q_out, k_out, v_out, short_p, long_p, mixed_t, xhat_out, rstd_out, first_out,
        packed_out, output_out,
        x_all, mixed, packed, wo, in_sems, out_sems,
    ) = refs
    step = pl.program_id(0)
    steps = pl.num_programs(0)
    short_seqs, short_len, long_seqs, long_len = shape
    base = short_seqs * short_len
    width = q_out.shape[1]
    half_width = packed.shape[2]
    short_spans, long_spans = sequences(*shape)
    targets = (packed.at[0], packed.at[1], wo)

    @pl.when(step == 0)
    def _():
        for part in range(3):
            for ref, masks in zip(pieces[part::3], slots):
                tall = ref.shape[0] // len(masks)
                for slot, mask in enumerate(masks):
                    mask = jnp.where(jnp.bitwise_and(me[0], 1) == 0, mask[0], mask[1])
                    place = pl.multiple_of(jnp.bitwise_xor(me[0], mask) * tall, tall)
                    pltpu.make_async_copy(
                        ref.at[pl.ds(slot * tall, tall)], targets[part].at[pl.ds(place, tall)], in_sems.at[part]
                    ).start()
        x_all[:base, :] = short_x[...]
        x_all[base:, :] = long_x[...]

    keeps = [
        pltpu.make_async_copy(packed.at[0], packed_out.at[0], out_sems.at[0]),
        pltpu.make_async_copy(packed.at[1], packed_out.at[1], out_sems.at[1]),
        pltpu.make_async_copy(wo, output_out, out_sems.at[2]),
    ]
    for part, first_step in enumerate((0, steps // 2, steps - 1)):
        @pl.when(step == first_step)
        def _():
            pltpu.make_async_copy(targets[part], targets[part], in_sems.at[part]).wait()
            keeps[part].start()

    x = x_all[...]
    side = step // (steps // 2)
    turn = lax.rem(step, steps // 2)
    third = half_width // 3
    weight = lambda which: packed[side, :, pl.ds(pl.multiple_of(which * third + turn * width, width), width)]
    q_out[...] = ((dot(x, weight(0)) + qb[...]).astype(BF).astype(F32) * HEAD_DIM ** (-0.5)).astype(BF)
    k_out[...] = dot(x, weight(1)).astype(BF)
    v_out[...] = (dot(x, weight(2)) + vb[...]).astype(BF)
    groups = ((short_spans, short_lengths, short_p), (long_spans, long_lengths, long_p))
    pairs = range(width // 128)
    jobs = []
    for pair in pairs:
        lanes = slice(128 * pair, 128 * pair + 128)
        for spans, refs, probs in groups:
            for seq, (start, length) in enumerate(spans):
                k2 = k_out[start : start + length, lanes]
                usable = lax.broadcasted_iota(jnp.int32, (length, 1), 0) < refs[seq]
                block = min(length, 512)
                for half in range(2):
                    for at in range(0, length, block):
                        jobs.append(dict(pair=pair, probs=probs, seq=seq, start=start, length=length, usable=usable, half=half, at=at, block=block, lanes=lanes,
                            scores=dot_t(head_lanes(k2, half), q_out[start + at : start + at + block, lanes])))
    for job in jobs:
        scores = jnp.where(job["usable"], job["scores"], -1e30)
        top = jnp.max(scores, axis=0, keepdims=True)
        powers = jnp.exp(scores - top)
        total = jnp.sum(powers, axis=0, keepdims=True)
        job["prob"] = (powers * (1.0 / total)).astype(BF)
        job["probs"][job["seq"], 2 * job["pair"] + job["half"], :, job["at"] : job["at"] + job["block"]] = job["prob"]

    flipped = {pair: flip(v_out[:, 128 * pair : 128 * pair + 128]) for pair in pairs}
    for job in jobs:
        feature = 128 * job["pair"] + HEAD_DIM * job["half"]
        v_head = flipped[job["pair"]][HEAD_DIM * job["half"] : HEAD_DIM * job["half"] + HEAD_DIM, job["start"] : job["start"] + job["length"]]
        mixed_t[feature : feature + HEAD_DIM, job["start"] + job["at"] : job["start"] + job["at"] + job["block"]] = dot(v_head, job["prob"])
    for pair in pairs:
        offset = pl.multiple_of(step * width + 128 * pair, 128)
        mixed[:, pl.ds(offset, 128)] = flip(mixed_t[128 * pair : 128 * pair + 128, :]).astype(BF)

    @pl.when(step == steps - 1)
    def _():
        first_sum = x_all[...].astype(F32) + (dot(mixed[...], wo[...]) + ob[...])
        center = first_sum - jnp.mean(first_sum, axis=-1, keepdims=True)
        spread = jnp.mean(center * center, axis=-1, keepdims=True)
        rstd = lax.rsqrt(spread + 1e-06)
        xhat = center * rstd
        xhat_out[...] = xhat
        rstd_out[...] = rstd
        first_out[...] = (xhat * gain1[...] + beta1[...]).astype(BF)
        for keep in keeps:
            keep.wait()


def attention_forward(shape, lengths, xs, weights, vectors):
    short_seqs, short_len, long_seqs, long_len = shape
    rows = short_seqs * short_len + long_seqs * long_len
    width = xs[0].shape[1]
    block = 256
    heads = block // HEAD_DIM
    steps = width // block
    whole = lambda shp: pl.BlockSpec(shp, lambda j: (0,) * len(shp))
    smem = pl.BlockSpec(memory_space=pltpu.SMEM)
    anywhere = pl.BlockSpec(memory_space=pl.ANY)
    row_block = pl.BlockSpec((1, block), lambda j: (0, j))
    out_col = pl.BlockSpec((rows, block), lambda j: (0, j))
    half_width = 3 * width // 2
    return pl.pallas_call(
        partial(attention_forward_kernel, shape, weights["slots"]),
        grid=(steps,),
        in_specs=[
            smem, smem, smem, whole(xs[0].shape), whole(xs[1].shape),
            *[anywhere] * len(weights["pieces"]), row_block, row_block, *[whole((1, width))] * 3,
        ],
        out_specs=[
            out_col, out_col, out_col,
            pl.BlockSpec((short_seqs, heads, short_len, short_len), lambda j: (0, j, 0, 0)),
            pl.BlockSpec((long_seqs, heads, long_len, long_len), lambda j: (0, j, 0, 0)),
            pl.BlockSpec((block, rows), lambda j: (j, 0)),
            whole((rows, width)), whole((rows, 1)), whole((rows, width)), anywhere, anywhere,
        ],
        out_shape=[
            jax.ShapeDtypeStruct((rows, width), BF),
            jax.ShapeDtypeStruct((rows, width), BF),
            jax.ShapeDtypeStruct((rows, width), BF),
            jax.ShapeDtypeStruct((short_seqs, HEADS, short_len, short_len), BF),
            jax.ShapeDtypeStruct((long_seqs, HEADS, long_len, long_len), BF),
            jax.ShapeDtypeStruct((width, rows), F32),
            jax.ShapeDtypeStruct((rows, width), F32),
            jax.ShapeDtypeStruct((rows, 1), F32),
            jax.ShapeDtypeStruct((rows, width), BF),
            jax.ShapeDtypeStruct((2, width, half_width), BF),
            jax.ShapeDtypeStruct((width, width), BF),
        ],
        scratch_shapes=[
            pltpu.VMEM((rows, width), BF), pltpu.VMEM((rows, width), BF),
            pltpu.VMEM((2, width, half_width), BF), pltpu.VMEM((width, width), BF),
            pltpu.SemaphoreType.DMA((3,)), pltpu.SemaphoreType.DMA((3,)),
        ],
        compiler_params=pltpu.CompilerParams(vmem_limit_bytes=VMEM_BYTES),
        cost_estimate=pl.CostEstimate(flops=36 * 10**9, bytes_accessed=40 * 10**6, transcendentals=5 * 10**6),
        name="attention_forward",
    )(
        weights["me"], *lengths, *xs, *weights["pieces"],
        vectors["query_bias"], vectors["value_bias"], vectors["output_bias"],
        vectors["first_gain"], vectors["first_beta"],
    )


def gelu_and_slope(value):
    share = 0.5 + 0.5 * lax.erf(value * 0.5 ** 0.5)
    density = jnp.exp2(value * (value * -0.7213475204444817)) * 0.3989422804014327
    return value * share, share + value * density


def inner_block(feed_w, block, turn):
    shards, _, width = feed_w.shape
    per = width // block
    return pl.BlockSpec((shards, width // shards, block), lambda j: (0, turn(j) // per, lax.rem(turn(j), per)))


def down_block(feed_w, block, turn):
    shards, tall, width = feed_w.shape
    tall = tall // 2
    return pl.BlockSpec((block // tall, tall, width), lambda j: (turn(j), 1, 0))


def norm_gradient(grad, xhat, rstd, gain):
    scaled = grad * gain
    mean = jnp.mean(scaled, axis=-1, keepdims=True)
    along = jnp.mean(scaled * xhat, axis=-1, keepdims=True)
    return rstd * (scaled - mean - xhat * along)


def fold(block):
    return jnp.sum(block.reshape(block.shape[0] // 8, 8, block.shape[1]), axis=0)


def tail_kernel(
    shape, steps, keep, rstd, first, wi, wd, inner_bias, gain1, beta1, gain2, beta2, down_bias,
    xhat_in, short_ct, long_ct, wo_in, q_in, k_in, v_in, short_p_in, long_p_in, mixed_t_in, packed_in,
    short_out, long_out, short_grad, long_grad, sums_out,
    total, low, value, slope, sums, inner_fold, xhat, ct, wo, short_p, long_p, mixed_t, packed, gm, sems, load_sems,
):
    step = pl.program_id(0)
    short_seqs, short_len, long_seqs, long_len = shape
    base = short_seqs * short_len
    rows, width = total.shape
    units = steps * value.shape[2]
    part = packed.shape[3]
    attention_steps = width // part
    heads = part // HEAD_DIM
    first_attention = 2 * steps
    turn = step - first_attention
    slot = lax.rem(jnp.maximum(turn, 0), 2)
    chunk = rows // 2
    wide = lambda ref: ref[...].reshape(width, -1)
    tall = lambda ref: ref[...].reshape(-1, width)
    short_spans, long_spans = sequences(*shape)

    early = [
        pltpu.make_async_copy(short_ct, ct.at[:base], sems.at[0]),
        pltpu.make_async_copy(long_ct, ct.at[base:], sems.at[1]),
        pltpu.make_async_copy(xhat_in, xhat, sems.at[2]),
        pltpu.make_async_copy(wo_in, wo, sems.at[3]),
    ]
    outs = [
        pltpu.make_async_copy(ct.at[:base], short_out, sems.at[4]),
        pltpu.make_async_copy(ct.at[base:], long_out, sems.at[5]),
    ]
    grads = [
        pltpu.make_async_copy(low.at[:base], short_grad, sems.at[6]),
        pltpu.make_async_copy(low.at[base:], long_grad, sems.at[7]),
    ]

    def loads(at, into):
        columns = pl.ds(pl.multiple_of(at * part, part), part)
        side = at // (attention_steps // 2)
        within = lax.rem(at, attention_steps // 2)
        third = packed_in.shape[2] // 3
        pairs = [(ref.at[:, columns], slope.at[3 - into, :, part * i : part * i + part]) for i, ref in enumerate((q_in, k_in, v_in))]
        pairs += [
            (short_p_in.at[:, pl.ds(at * heads, heads)], short_p.at[into]),
            (long_p_in.at[:, pl.ds(at * heads, heads)], long_p.at[into]),
            (mixed_t_in.at[columns], mixed_t.at[into]),
        ]
        pairs += [
            (
                packed_in.at[side, :, pl.ds(pl.multiple_of(i * third + within * part, part), part)],
                packed.at[into, i],
            )
            for i in range(3)
        ]
        return [pltpu.make_async_copy(a, b, load_sems.at[into, i]) for i, (a, b) in enumerate(pairs)]

    def first_part():
        value[lax.rem(step, 2)] = dot(first[...], wide(wi)) + inner_bias[...]

    def second_part():
        act, slp = gelu_and_slope(value[lax.rem(step + 1, 2)])
        slope[step - 1] = slp.astype(BF)
        total[...] += dot(act.astype(BF), tall(wd))

    @pl.when(step == 0)
    def _():
        for copy in early:
            copy.start()
        first_part()
        total[...] = jnp.broadcast_to(down_bias[...], total.shape)

    @pl.when((step > 0) & (step < steps))
    def _():
        first_part()
        second_part()

    chunks = [slice(at, at + chunk) for at in range(0, rows, chunk)]
    block = value.shape[2]

    def inner_place():
        return pl.ds(pl.multiple_of(3 * width + (2 * steps - 1 - step) * block, 128), block)

    @pl.when(step == steps)
    def _():
        for copy in early[:3]:
            copy.wait()
        sums[...] = jnp.zeros_like(sums)
        inner_fold[...] = jnp.zeros_like(inner_fold)
        second, grads_of = {}, {}
        for turn_of in range(len(chunks) + 2):
            if turn_of >= 2:
                back_here = chunks[turn_of - 2]
                grad_active = dot_t(low[back_here], tall(wd))
            if turn_of < len(chunks):
                ahead = chunks[turn_of]
                act, slp = gelu_and_slope(value[(steps - 1) % 2, ahead])
                slope[steps - 1, ahead] = slp.astype(BF)
                act = act.astype(BF)
            if turn_of >= 2:
                grad_inner = (grad_active * slope[steps - 1, back_here].astype(F32)).astype(BF)
                through = dot_t(grad_inner, wide(wi))
            if turn_of < len(chunks):
                down = dot(act, tall(wd))
            if 0 < turn_of <= len(chunks):
                here = chunks[turn_of - 1]
                summed = second.pop(turn_of - 1) + (xhat[here] * gain1[...] + beta1[...])
                center = summed - jnp.mean(summed, axis=-1, keepdims=True)
                spread = jnp.mean(center * center, axis=-1, keepdims=True)
                rstd2 = lax.rsqrt(spread + 1e-06)
                xhat2 = center * rstd2
                usable = keep[here]
                grad_out = ct[here].astype(F32) * usable
                ct[here] = ((xhat2 * gain2[...] + beta2[...]) * usable).astype(BF)
                grad_second = norm_gradient(grad_out, xhat2, rstd2, gain2[...])
                rounded = grad_second.astype(BF)
                low[here] = rounded
                grads_of[turn_of - 1] = grad_second
                sums[0] += fold(grad_out)
                sums[1] += fold(rounded.astype(F32))
            if turn_of >= 2:
                inner_fold[...] += fold(grad_inner.astype(F32))
                total[back_here] = grads_of.pop(turn_of - 2) + through
            if turn_of < len(chunks):
                second[turn_of] = total[ahead] + down
        for copy in outs:
            copy.start()
        sums_out[:, 5 * width + units : 6 * width + units] = jnp.sum(sums[0], axis=0, keepdims=True)
        sums_out[:, 3 * width + units : 4 * width + units] = jnp.sum(sums[1], axis=0, keepdims=True)
        sums_out[:, inner_place()] = jnp.sum(inner_fold[...], axis=0, keepdims=True)

    @pl.when((step > steps) & (step < 2 * steps - 1))
    def _():
        grad_inner = (dot_t(low[...], tall(wd)) * slope[2 * steps - 1 - step].astype(F32)).astype(BF)
        sums_out[:, inner_place()] = jnp.sum(grad_inner.astype(F32), axis=0, keepdims=True)
        total[...] += dot_t(grad_inner, wide(wi))

    @pl.when(step == 2 * steps - 2)
    def _():
        for copy in loads(0, 0):
            copy.start()

    @pl.when(step == 2 * steps - 1)
    def _():
        for copy in loads(1, 1):
            copy.start()
        early[3].wait()
        sums[...] = jnp.zeros_like(sums)
        inner_fold[...] = jnp.zeros_like(inner_fold)
        firsts = {}
        for turn_of in range(len(chunks) + 2):
            if turn_of < len(chunks):
                ahead = chunks[turn_of]
                grad_active = dot_t(low[ahead], tall(wd))
            if turn_of >= 2:
                back_here = chunks[turn_of - 2]
                mixed_grad = dot_t(low[back_here], wo[...])
            if 0 < turn_of <= len(chunks):
                here = chunks[turn_of - 1]
                grad_first = firsts.pop(turn_of - 1)
                result = norm_gradient(grad_first, xhat[here], rstd[here], gain1[...])
                total[here] = result
                branch = result.astype(BF)
                low[here] = branch
                sums[0] += fold(grad_first)
                sums[1] += fold(branch.astype(F32))
            if turn_of < len(chunks):
                grad_inner = (grad_active * slope[0, ahead].astype(F32)).astype(BF)
                firsts[turn_of] = total[ahead] + dot_t(grad_inner, wide(wi))
                inner_fold[...] += fold(grad_inner.astype(F32))
            if turn_of >= 2:
                gm[back_here] = mixed_grad.astype(BF)
        sums_out[:, 4 * width + units : 5 * width + units] = jnp.sum(sums[0], axis=0, keepdims=True)
        sums_out[:, 2 * width : 3 * width] = jnp.sum(sums[1], axis=0, keepdims=True)
        sums_out[:, inner_place()] = jnp.sum(inner_fold[...], axis=0, keepdims=True)

    @pl.when(turn >= 0)
    def _():
        for copy in loads(turn, slot):
            copy.wait()
        scale = HEAD_DIM ** (-0.5)
        own = 3 - slot
        q = lambda here, lanes: slope[own, here, lanes]
        k = lambda here, lanes: slope[own, here, slice(part + lanes.start, part + lanes.stop)]
        v = lambda here, lanes: slope[own, here, slice(2 * part + lanes.start, 2 * part + lanes.stop)]
        grad = lambda here, lanes: slope[1, here, slice(3 * part + lanes.start, 3 * part + lanes.stop)]
        slope[1, :, 3 * part : 4 * part] = gm[:, pl.ds(pl.multiple_of(turn * part, part), part)]
        everything = slice(0, rows)
        jobs = []
        for pair in range(part // 128):
            lanes = slice(128 * pair, 128 * pair + 128)
            for spans, probs in ((short_spans, short_p), (long_spans, long_p)):
                for seq, (start, length) in enumerate(spans):
                    here = slice(start, start + length)
                    for half in range(2):
                        jobs.append(dict(
                            pair=pair, here=here, lanes=lanes, half=half, probs=probs, seq=seq,
                            grad_p=dot_t(head_lanes(v(here, lanes), half), grad(here, lanes)),
                        ))
        flipped, delta = {}, {}
        for pair in range(part // 128):
            lanes = slice(128 * pair, 128 * pair + 128)
            flipped[pair] = flip(k(everything, lanes))
            product = flip(grad(everything, lanes)).astype(F32) * mixed_t[slot, lanes, :]
            for half in range(2):
                delta[pair, half] = jnp.sum(product[HEAD_DIM * half : HEAD_DIM * half + HEAD_DIM], axis=0, keepdims=True)
        for job in jobs:
            pair, half = job["pair"], job["half"]
            prob = job["probs"][slot, job["seq"], 2 * pair + half].astype(F32)
            job["grad_s"] = (prob * (job["grad_p"] - delta[pair, half][:, job["here"]])).astype(BF)
        for one, two in zip(jobs[0::2], jobs[1::2]):
            pair, here, lanes = one["pair"], one["here"], one["lanes"]
            grad_value = grad_key = None
            grad_query_t = []
            for job in (one, two):
                half = job["half"]
                prob = job["probs"][slot, job["seq"], 2 * pair + half]
                dv = dot(prob, head_lanes(grad(here, lanes), half))
                dk = dot(job["grad_s"], head_lanes(q(here, lanes), half))
                grad_value = dv if half == 0 else grad_value + dv
                grad_key = dk if half == 0 else grad_key + dk
                grad_query_t.append(dot(flipped[pair][HEAD_DIM * half : HEAD_DIM * half + HEAD_DIM, here], job["grad_s"]))
            slope[1, here, 128 * pair : 128 * pair + 128] = (flip(jnp.concatenate(grad_query_t, axis=0)) * scale).astype(BF)
            slope[1, here, part + 128 * pair : part + 128 * pair + 128] = grad_key.astype(BF)
            slope[1, here, 2 * part + 128 * pair : 2 * part + 128 * pair + 128] = grad_value.astype(BF)
        place = pl.multiple_of(turn * part, part)
        sums_out[:, pl.ds(place, part)] = jnp.sum(slope[1, :, :part].astype(F32), axis=0, keepdims=True)
        sums_out[:, pl.ds(width + place, part)] = jnp.sum(slope[1, :, 2 * part : 3 * part].astype(F32), axis=0, keepdims=True)
        total[...] += (
            dot_t(slope[1, :, :part], packed[slot, 0])
            + dot_t(slope[1, :, part : 2 * part], packed[slot, 1])
            + dot_t(slope[1, :, 2 * part : 3 * part], packed[slot, 2])
        )

    @pl.when((turn >= 0) & (turn < attention_steps - 2))
    def _():
        for copy in loads(turn + 2, slot):
            copy.start()

    @pl.when(turn == attention_steps - 1)
    def _():
        low[...] = (total[...] * keep[...]).astype(BF)
        for copy in grads:
            copy.start()
        for copy in outs + grads:
            copy.wait()


def feed_and_attention_backward(shape, keep, attention, cts, feed_w, vectors, block=FEED_BLOCK):
    q, k, v, short_p, long_p, mixed_t, xhat, rstd, first, packed_w, output_w = attention
    short_seqs, short_len, long_seqs, long_len = shape
    rows, width = xhat.shape
    base = short_seqs * short_len
    units = vectors["inner_bias"].shape[1]
    steps = units // block
    part = 256
    heads = part // HEAD_DIM
    once = pl.Buffered(1)
    whole = lambda shp: pl.BlockSpec(shp, lambda j: (0,) * len(shp), pipeline_mode=once)
    vec = whole((1, width))
    anywhere = pl.BlockSpec(memory_space=pl.ANY)
    back = lambda j: jnp.maximum(2 * steps - 1 - j, 0)
    inner_turn = lambda j: jnp.where(j < steps, j, back(j))
    down_turn = lambda j: jnp.where(j <= steps, jnp.maximum(j - 1, 0), back(j))
    total_width = 6 * width + units
    return pl.pallas_call(
        partial(tail_kernel, shape, steps),
        grid=(2 * steps + width // part,),
        in_specs=[
            whole((rows, 1)), whole((rows, 1)), whole((rows, width)),
            inner_block(feed_w, block, inner_turn), down_block(feed_w, block, down_turn),
            pl.BlockSpec((1, block), lambda j: (0, jnp.minimum(j, steps - 1))), vec, vec, vec, vec, vec,
            *[anywhere] * 11,
        ],
        out_specs=[anywhere] * 4 + [pl.BlockSpec((1, total_width), lambda j: (0, 0))],
        out_shape=[
            jax.ShapeDtypeStruct(cts[0].shape, BF), jax.ShapeDtypeStruct(cts[1].shape, BF),
            jax.ShapeDtypeStruct(cts[0].shape, BF), jax.ShapeDtypeStruct(cts[1].shape, BF),
            jax.ShapeDtypeStruct((1, total_width), F32),
        ],
        scratch_shapes=[
            pltpu.VMEM((rows, width), F32), pltpu.VMEM((rows, width), BF), pltpu.VMEM((2, rows, block), F32),
            pltpu.VMEM((steps, rows, block), BF), pltpu.VMEM((2, 8, width), F32), pltpu.VMEM((8, block), F32),
            pltpu.VMEM((rows, width), F32), pltpu.VMEM((rows, width), BF), pltpu.VMEM((width, width), BF),
            pltpu.VMEM((2, short_seqs, heads, short_len, short_len), BF),
            pltpu.VMEM((2, long_seqs, heads, long_len, long_len), BF),
            pltpu.VMEM((2, part, rows), F32), pltpu.VMEM((2, 3, width, part), BF), pltpu.VMEM((rows, width), BF),
            pltpu.SemaphoreType.DMA((8,)), pltpu.SemaphoreType.DMA((2, 9)),
        ],
        compiler_params=pltpu.CompilerParams(vmem_limit_bytes=TAIL_VMEM_BYTES),
        cost_estimate=pl.CostEstimate(flops=85 * 10**9, bytes_accessed=90 * 10**6, transcendentals=4 * 10**6),
        name="feed_and_attention_backward",
    )(
        keep, rstd, first, feed_w, feed_w, vectors["inner_bias"],
        vectors["first_gain"], vectors["first_beta"], vectors["second_gain"], vectors["second_beta"], vectors["down_bias"],
        xhat, *cts, output_w, q, k, v, short_p, long_p, mixed_t, packed_w,
    )


def local(
    short_input, short_lengths, short_cotangent, long_input, long_lengths, long_cotangent,
    packed_weight, output_weight, inner_weight, down_weight,
    first_gain, second_gain, query_bias, value_bias, output_bias, inner_bias, down_bias, first_beta, second_beta,
):
    short_seqs, short_len, width = short_input.shape
    long_seqs, long_len, _ = long_input.shape
    shape = (short_seqs, short_len, long_seqs, long_len)
    lengths = (short_lengths, long_lengths)
    vectors = dict(
        first_gain=first_gain, second_gain=second_gain, query_bias=query_bias, value_bias=value_bias,
        output_bias=output_bias, inner_bias=inner_bias, down_bias=down_bias, first_beta=first_beta, second_beta=second_beta,
    )
    vectors = {name: item.reshape(1, -1) for name, item in vectors.items()}
    xs = (short_input.reshape(-1, width), long_input.reshape(-1, width))
    cts = (short_cotangent.reshape(-1, width), long_cotangent.reshape(-1, width))
    weights = gather_weights(packed_weight, output_weight, inner_weight, down_weight)
    attention = attention_forward(shape, lengths, xs, weights, vectors)
    keep = jnp.concatenate([
        (jnp.arange(item.shape[1])[None, :] < length[:, None]).reshape(-1, 1)
        for item, length in ((short_input, short_lengths), (long_input, long_lengths))
    ], axis=0).astype(F32)
    short_out, long_out, short_grad, long_grad, sums = feed_and_attention_backward(
        shape, keep, attention, cts, weights["feed"], vectors
    )
    sums = sum_all(sums).reshape(-1)
    outs = []
    at = 0
    for size in (width, width, width, inner_bias.shape[0], width, width, width):
        outs.append(lax.slice_in_dim(sums, at, at + size))
        at += size
    return (
        short_out.reshape(short_input.shape), short_grad.reshape(short_input.shape),
        long_out.reshape(long_input.shape), long_grad.reshape(long_input.shape), *outs,
    )


def exchange(block, mask):
    count = lax.axis_size("dp")
    return lax.ppermute(block, "dp", [(i, i ^ mask(i)) for i in range(count)])


CORE, X, Y, Z_NEAR, Z_FAR = 1, 2, 4, 8, 16


def side_first(index):
    return X if index & CORE == 0 else Y


def side_second(index):
    return Y if index & CORE == 0 else X


def gather_by_exchange(shard):
    held = jnp.concatenate([shard, exchange(shard, lambda i: Z_FAR)])
    held = jnp.concatenate([held, exchange(held, side_first)])
    held = jnp.concatenate([held, exchange(held, lambda i: Z_NEAR)])
    other = exchange(held, side_second)
    return [held, other, exchange(held, lambda i: CORE), exchange(other, lambda i: CORE)]


def exchange_slots():
    def mask(core, swap, far, slot):
        owner = core ^ swap
        return (
            swap * CORE + far * side_second(owner) + Z_FAR * (slot & 1)
            + side_first(owner) * (slot >> 1 & 1) + Z_NEAR * (slot >> 2)
        )

    return [
        [(mask(0, swap, far, slot), mask(1, swap, far, slot)) for slot in range(8)]
        for swap in (0, 1) for far in (0, 1)
    ]


def pack_kernel(inner, down, out, sems):
    tall, width = inner.shape[0], down.shape[1]
    blocks = inner.shape[1] // width
    copies = [
        pltpu.make_async_copy(
            inner.at[:, pl.ds(i * width, width)], out.at[pl.ds(i * tall, tall)], sems.at[i]
        )
        for i in range(blocks)
    ]
    copies.append(pltpu.make_async_copy(down, out.at[pl.ds(blocks * tall, down.shape[0])], sems.at[blocks]))
    for copy in copies:
        copy.start()
    for copy in copies:
        copy.wait()


def pack_rows(inner, down):
    width = down.shape[1]
    blocks = inner.shape[1] // width
    anywhere = pl.BlockSpec(memory_space=pl.ANY)
    return pl.pallas_call(
        pack_kernel,
        in_specs=[anywhere, anywhere],
        out_specs=anywhere,
        out_shape=jax.ShapeDtypeStruct((blocks * inner.shape[0] + down.shape[0], width), inner.dtype),
        scratch_shapes=[pltpu.SemaphoreType.DMA((blocks + 1,))],
        name="pack_rows",
    )(inner, down)


def gather_weights(packed, output, inner, down):
    count = lax.axis_size("dp")
    width = output.shape[1]
    half = width // 2
    sides = [
        jnp.concatenate([packed[:, i * width + at : i * width + at + half] for i in range(3)], axis=1) for at in (0, half)
    ]
    parts = [*sides, output]
    tall = inner.shape[0]
    blocks = inner.shape[1] // width
    if count == 32:
        feed = lax.all_gather(pack_rows(inner, down), "dp", axis=0, tiled=False)
        gathered = [gather_by_exchange(part) for part in parts]
        return dict(
            me=lax.axis_index("dp").reshape(1).astype(jnp.int32), slots=exchange_slots(),
            pieces=[gathered[part][piece] for piece in range(4) for part in range(3)], feed=feed,
        )
    whole = [lax.all_gather(part, "dp", axis=0, tiled=True) for part in (*parts, inner, down)]
    shards = 32
    feed = jnp.concatenate(
        [
            whole[3].reshape(shards, -1, blocks, width).transpose(0, 2, 1, 3).reshape(shards, -1, width),
            whole[4].reshape(shards, -1, width),
        ],
        axis=1,
    )
    return dict(me=jnp.zeros((1,), jnp.int32), slots=[[(i, i) for i in range(shards)]], pieces=whole[:3], feed=feed)


def sum_all(vector):
    count = lax.axis_size("dp")
    if count & (count - 1):
        return lax.psum(vector, "dp")
    vector = vector + exchange(vector, lambda i: 1) if count > 1 else vector
    bit = 2
    while bit < count:
        near = exchange(vector, lambda i: bit)
        if 2 * bit < count:
            far = exchange(vector, lambda i: 2 * bit)
            both = exchange(vector, lambda i: 3 * bit)
            vector = (vector + near) + (far + both)
        else:
            vector = vector + near
        bit *= 4
    return vector


def solution(mesh):
    rows = P("dp", None, None)
    in_specs = (rows, P("dp"), rows, rows, P("dp"), rows) + (P("dp", None),) * 4 + (P(),) * 9
    out_specs = (rows,) * 4 + (P(),) * 7
    return jax.shard_map(local, mesh=mesh, in_specs=in_specs, out_specs=out_specs, check_vma=False)
```

```python
from functools import partial

import jax
import jax.numpy as jnp
from jax import lax
from jax.experimental import pallas as pl
from jax.experimental.pallas import tpu as pltpu
from jax.sharding import PartitionSpec as P

HEADS = 16
HEAD_DIM = 64
BF = jnp.bfloat16
F32 = jnp.float32
VMEM_BYTES = 60 * 1024 * 1024
FEED_BLOCK = 1024
TAIL_VMEM_BYTES = 63 * 1024 * 1024


def dot(left, right):
    return lax.dot_general(left, right, (((1,), (0,)), ((), ())), preferred_element_type=F32)


def dot_t(left, right):
    return lax.dot_general(left, right, (((1,), (1,)), ((), ())), preferred_element_type=F32)


def sequences(short_seqs, short_len, long_seqs, long_len):
    spans = [(i * short_len, short_len) for i in range(short_seqs)]
    base = short_seqs * short_len
    return spans, [(base + i * long_len, long_len) for i in range(long_seqs)]


def row_mask(short_lengths, long_lengths, shape):
    short_seqs, short_len, long_seqs, long_len = shape
    pieces = []
    for count, length, refs in (
        (short_seqs, short_len, short_lengths),
        (long_seqs, long_len, long_lengths),
    ):
        for i in range(count):
            rows = lax.broadcasted_iota(jnp.int32, (length, 1), 0)
            pieces.append(jnp.where(rows < refs[i], 1.0, 0.0).astype(F32))
    return jnp.concatenate(pieces, axis=0)


def head_lanes(block, half):
    lanes = lax.broadcasted_iota(jnp.int32, block.shape, 1)
    keep = lanes < HEAD_DIM if half == 0 else lanes >= HEAD_DIM
    return jnp.where(keep, block, jnp.zeros_like(block))


def flip(block):
    return jnp.transpose(block, (1, 0))


def attention_forward_kernel(
    shape, slots, me, short_lengths, long_lengths, short_x, long_x, *refs,
):
    pieces, refs = refs[: 3 * len(slots)], refs[3 * len(slots) :]
    (
        qb, vb, ob, gain1, beta1, q_out, k_out, v_out, short_p, long_p, mixed_t, xhat_out, rstd_out, first_out,
        packed_out, output_out,
        x_all, mixed, packed, wo, in_sems, out_sems,
    ) = refs
    step = pl.program_id(0)
    steps = pl.num_programs(0)
    short_seqs, short_len, long_seqs, long_len = shape
    base = short_seqs * short_len
    width = q_out.shape[1]
    half_width = packed.shape[2]
    short_spans, long_spans = sequences(*shape)
    targets = (packed.at[0], packed.at[1], wo)

    @pl.when(step == 0)
    def _():
        for part in range(3):
            for ref, masks in zip(pieces[part::3], slots):
                tall = ref.shape[0] // len(masks)
                for slot, mask in enumerate(masks):
                    mask = jnp.where(jnp.bitwise_and(me[0], 1) == 0, mask[0], mask[1])
                    place = pl.multiple_of(jnp.bitwise_xor(me[0], mask) * tall, tall)
                    pltpu.make_async_copy(
                        ref.at[pl.ds(slot * tall, tall)], targets[part].at[pl.ds(place, tall)], in_sems.at[part]
                    ).start()
        x_all[:base, :] = short_x[...]
        x_all[base:, :] = long_x[...]

    keeps = [
        pltpu.make_async_copy(packed.at[0], packed_out.at[0], out_sems.at[0]),
        pltpu.make_async_copy(packed.at[1], packed_out.at[1], out_sems.at[1]),
        pltpu.make_async_copy(wo, output_out, out_sems.at[2]),
    ]
    for part, first_step in enumerate((0, steps // 2, steps - 1)):
        @pl.when(step == first_step)
        def _():
            pltpu.make_async_copy(targets[part], targets[part], in_sems.at[part]).wait()
            keeps[part].start()

    x = x_all[...]
    side = step // (steps // 2)
    turn = lax.rem(step, steps // 2)
    third = half_width // 3
    weight = lambda which: packed[side, :, pl.ds(pl.multiple_of(which * third + turn * width, width), width)]
    q_out[...] = ((dot(x, weight(0)) + qb[...]).astype(BF).astype(F32) * HEAD_DIM ** (-0.5)).astype(BF)
    k_out[...] = dot(x, weight(1)).astype(BF)
    v_out[...] = (dot(x, weight(2)) + vb[...]).astype(BF)
    groups = ((short_spans, short_lengths, short_p), (long_spans, long_lengths, long_p))
    pairs = range(width // 128)
    jobs = []
    for pair in pairs:
        lanes = slice(128 * pair, 128 * pair + 128)
        for spans, refs, probs in groups:
            for seq, (start, length) in enumerate(spans):
                k2 = k_out[start : start + length, lanes]
                usable = lax.broadcasted_iota(jnp.int32, (length, 1), 0) < refs[seq]
                block = min(length, 512)
                for half in range(2):
                    for at in range(0, length, block):
                        jobs.append(dict(pair=pair, probs=probs, seq=seq, start=start, length=length, usable=usable, half=half, at=at, block=block, lanes=lanes,
                            scores=dot_t(head_lanes(k2, half), q_out[start + at : start + at + block, lanes])))
    for job in jobs:
        scores = jnp.where(job["usable"], job["scores"], -1e30)
        top = jnp.max(scores, axis=0, keepdims=True)
        powers = jnp.exp(scores - top)
        total = jnp.sum(powers, axis=0, keepdims=True)
        job["prob"] = (powers * (1.0 / total)).astype(BF)
        job["probs"][job["seq"], 2 * job["pair"] + job["half"], :, job["at"] : job["at"] + job["block"]] = job["prob"]

    flipped = {pair: flip(v_out[:, 128 * pair : 128 * pair + 128]) for pair in pairs}
    for job in jobs:
        feature = 128 * job["pair"] + HEAD_DIM * job["half"]
        v_head = flipped[job["pair"]][HEAD_DIM * job["half"] : HEAD_DIM * job["half"] + HEAD_DIM, job["start"] : job["start"] + job["length"]]
        mixed_t[feature : feature + HEAD_DIM, job["start"] + job["at"] : job["start"] + job["at"] + job["block"]] = dot(v_head, job["prob"])
    for pair in pairs:
        offset = pl.multiple_of(step * width + 128 * pair, 128)
        mixed[:, pl.ds(offset, 128)] = flip(mixed_t[128 * pair : 128 * pair + 128, :]).astype(BF)

    @pl.when(step == steps - 1)
    def _():
        first_sum = x_all[...].astype(F32) + (dot(mixed[...], wo[...]) + ob[...])
        center = first_sum - jnp.mean(first_sum, axis=-1, keepdims=True)
        spread = jnp.mean(center * center, axis=-1, keepdims=True)
        rstd = lax.rsqrt(spread + 1e-06)
        xhat = center * rstd
        xhat_out[...] = xhat
        rstd_out[...] = rstd
        first_out[...] = (xhat * gain1[...] + beta1[...]).astype(BF)
        for keep in keeps:
            keep.wait()


def attention_forward(shape, lengths, xs, weights, vectors):
    short_seqs, short_len, long_seqs, long_len = shape
    rows = short_seqs * short_len + long_seqs * long_len
    width = xs[0].shape[1]
    block = 256
    heads = block // HEAD_DIM
    steps = width // block
    whole = lambda shp: pl.BlockSpec(shp, lambda j: (0,) * len(shp))
    smem = pl.BlockSpec(memory_space=pltpu.SMEM)
    anywhere = pl.BlockSpec(memory_space=pl.ANY)
    row_block = pl.BlockSpec((1, block), lambda j: (0, j))
    out_col = pl.BlockSpec((rows, block), lambda j: (0, j))
    half_width = 3 * width // 2
    return pl.pallas_call(
        partial(attention_forward_kernel, shape, weights["slots"]),
        grid=(steps,),
        in_specs=[
            smem, smem, smem, whole(xs[0].shape), whole(xs[1].shape),
            *[anywhere] * len(weights["pieces"]), row_block, row_block, *[whole((1, width))] * 3,
        ],
        out_specs=[
            out_col, out_col, out_col,
            pl.BlockSpec((short_seqs, heads, short_len, short_len), lambda j: (0, j, 0, 0)),
            pl.BlockSpec((long_seqs, heads, long_len, long_len), lambda j: (0, j, 0, 0)),
            pl.BlockSpec((block, rows), lambda j: (j, 0)),
            whole((rows, width)), whole((rows, 1)), whole((rows, width)), anywhere, anywhere,
        ],
        out_shape=[
            jax.ShapeDtypeStruct((rows, width), BF),
            jax.ShapeDtypeStruct((rows, width), BF),
            jax.ShapeDtypeStruct((rows, width), BF),
            jax.ShapeDtypeStruct((short_seqs, HEADS, short_len, short_len), BF),
            jax.ShapeDtypeStruct((long_seqs, HEADS, long_len, long_len), BF),
            jax.ShapeDtypeStruct((width, rows), F32),
            jax.ShapeDtypeStruct((rows, width), F32),
            jax.ShapeDtypeStruct((rows, 1), F32),
            jax.ShapeDtypeStruct((rows, width), BF),
            jax.ShapeDtypeStruct((2, width, half_width), BF),
            jax.ShapeDtypeStruct((width, width), BF),
        ],
        scratch_shapes=[
            pltpu.VMEM((rows, width), BF), pltpu.VMEM((rows, width), BF),
            pltpu.VMEM((2, width, half_width), BF), pltpu.VMEM((width, width), BF),
            pltpu.SemaphoreType.DMA((3,)), pltpu.SemaphoreType.DMA((3,)),
        ],
        compiler_params=pltpu.CompilerParams(vmem_limit_bytes=VMEM_BYTES),
        cost_estimate=pl.CostEstimate(flops=36 * 10**9, bytes_accessed=40 * 10**6, transcendentals=5 * 10**6),
        name="attention_forward",
    )(
        weights["me"], *lengths, *xs, *weights["pieces"],
        vectors["query_bias"], vectors["value_bias"], vectors["output_bias"],
        vectors["first_gain"], vectors["first_beta"],
    )


def gelu_and_slope(value):
    share = 0.5 + 0.5 * lax.erf(value * 0.5 ** 0.5)
    density = jnp.exp2(value * (value * -0.7213475204444817)) * 0.3989422804014327
    return value * share, share + value * density


def inner_block(feed_w, block, turn):
    shards, _, width = feed_w.shape
    per = width // block
    return pl.BlockSpec((shards, width // shards, block), lambda j: (0, turn(j) // per, lax.rem(turn(j), per)))


def down_block(feed_w, block, turn):
    shards, tall, width = feed_w.shape
    tall = tall // 2
    return pl.BlockSpec((block // tall, tall, width), lambda j: (turn(j), 1, 0))


def norm_gradient(grad, xhat, rstd, gain):
    scaled = grad * gain
    mean = jnp.mean(scaled, axis=-1, keepdims=True)
    along = jnp.mean(scaled * xhat, axis=-1, keepdims=True)
    return rstd * (scaled - mean - xhat * along)


def fold(block):
    return jnp.sum(block.reshape(block.shape[0] // 8, 8, block.shape[1]), axis=0)


def tail_kernel(
    shape, steps, keep, rstd, first, wi, wd, inner_bias, gain1, beta1, gain2, beta2, down_bias,
    xhat_in, short_ct, long_ct, wo_in, q_in, k_in, v_in, short_p_in, long_p_in, mixed_t_in, packed_in,
    short_out, long_out, short_grad, long_grad, sums_out,
    total, low, value, slope, sums, xhat, ct, wo, short_p, long_p, mixed_t, packed, gm, sems, load_sems,
):
    step = pl.program_id(0)
    short_seqs, short_len, long_seqs, long_len = shape
    base = short_seqs * short_len
    rows, width = total.shape
    units = steps * value.shape[2]
    part = packed.shape[3]
    attention_steps = width // part
    heads = part // HEAD_DIM
    first_attention = 2 * steps + 1
    turn = step - first_attention
    slot = lax.rem(jnp.maximum(turn, 0), 2)
    chunk = 128
    wide = lambda ref: ref[...].reshape(width, -1)
    tall = lambda ref: ref[...].reshape(-1, width)
    short_spans, long_spans = sequences(*shape)

    early = [
        pltpu.make_async_copy(short_ct, ct.at[:base], sems.at[0]),
        pltpu.make_async_copy(long_ct, ct.at[base:], sems.at[1]),
        pltpu.make_async_copy(xhat_in, xhat, sems.at[2]),
        pltpu.make_async_copy(wo_in, wo, sems.at[3]),
    ]
    outs = [
        pltpu.make_async_copy(ct.at[:base], short_out, sems.at[4]),
        pltpu.make_async_copy(ct.at[base:], long_out, sems.at[5]),
    ]
    grads = [
        pltpu.make_async_copy(low.at[:base], short_grad, sems.at[6]),
        pltpu.make_async_copy(low.at[base:], long_grad, sems.at[7]),
    ]

    def loads(at, into):
        columns = pl.ds(pl.multiple_of(at * part, part), part)
        side = at // (attention_steps // 2)
        within = lax.rem(at, attention_steps // 2)
        third = packed_in.shape[2] // 3
        pairs = [(ref.at[:, columns], slope.at[3 - into, :, part * i : part * i + part]) for i, ref in enumerate((q_in, k_in, v_in))]
        pairs += [
            (short_p_in.at[:, pl.ds(at * heads, heads)], short_p.at[into]),
            (long_p_in.at[:, pl.ds(at * heads, heads)], long_p.at[into]),
            (mixed_t_in.at[columns], mixed_t.at[into]),
        ]
        pairs += [
            (
                packed_in.at[side, :, pl.ds(pl.multiple_of(i * third + within * part, part), part)],
                packed.at[into, i],
            )
            for i in range(3)
        ]
        return [pltpu.make_async_copy(a, b, load_sems.at[into, i]) for i, (a, b) in enumerate(pairs)]

    def first_part():
        value[lax.rem(step, 2)] = dot(first[...], wide(wi)) + inner_bias[...]

    def second_part():
        act, slp = gelu_and_slope(value[lax.rem(step + 1, 2)])
        slope[step - 1] = slp.astype(BF)
        total[...] += dot(act.astype(BF), tall(wd))

    @pl.when(step == 0)
    def _():
        for copy in early:
            copy.start()
        first_part()
        total[...] = jnp.broadcast_to(down_bias[...], total.shape)

    @pl.when((step > 0) & (step < steps))
    def _():
        first_part()
        second_part()

    @pl.when(step == steps)
    def _():
        for copy in early[:3]:
            copy.wait()
        second_part()
        sums[...] = jnp.zeros_like(sums)

        def body(i, _):
            here = pl.ds(pl.multiple_of(i * chunk, chunk), chunk)
            second = total[here, :] + (xhat[here, :] * gain1[...] + beta1[...])
            center = second - jnp.mean(second, axis=-1, keepdims=True)
            spread = jnp.mean(center * center, axis=-1, keepdims=True)
            rstd2 = lax.rsqrt(spread + 1e-06)
            xhat2 = center * rstd2
            usable = keep[here, :]
            grad_out = ct[here, :].astype(F32) * usable
            ct[here, :] = ((xhat2 * gain2[...] + beta2[...]) * usable).astype(BF)
            grad_second = norm_gradient(grad_out, xhat2, rstd2, gain2[...])
            rounded = grad_second.astype(BF)
            low[here, :] = rounded
            total[here, :] = grad_second
            sums[0] += fold(grad_out)
            sums[1] += fold(rounded.astype(F32))
            return 0

        lax.fori_loop(0, rows // chunk, body, 0)
        for copy in outs:
            copy.start()
        sums_out[:, 5 * width + units : 6 * width + units] = jnp.sum(sums[0], axis=0, keepdims=True)
        sums_out[:, 3 * width + units : 4 * width + units] = jnp.sum(sums[1], axis=0, keepdims=True)

    @pl.when((step > steps) & (step <= 2 * steps))
    def _():
        grad_inner = (dot_t(low[...], tall(wd)) * slope[2 * steps - step].astype(F32)).astype(BF)
        place = pl.multiple_of(3 * width + (2 * steps - step) * wd.shape[0] * wd.shape[1], 128)
        sums_out[:, pl.ds(place, value.shape[2])] = jnp.sum(grad_inner.astype(F32), axis=0, keepdims=True)
        total[...] += dot_t(grad_inner, wide(wi))

    @pl.when(step == 2 * steps - 1)
    def _():
        for copy in loads(0, 0):
            copy.start()

    @pl.when(step == 2 * steps)
    def _():
        for copy in loads(1, 1):
            copy.start()
        sums[...] = jnp.zeros_like(sums)

        def body(i, _):
            here = pl.ds(pl.multiple_of(i * chunk, chunk), chunk)
            grad_first = total[here, :]
            result = norm_gradient(grad_first, xhat[here, :], rstd[here, :], gain1[...])
            total[here, :] = result
            branch = result.astype(BF)
            low[here, :] = branch
            sums[0] += fold(grad_first)
            sums[1] += fold(branch.astype(F32))
            return 0

        lax.fori_loop(0, rows // chunk, body, 0)
        sums_out[:, 4 * width + units : 5 * width + units] = jnp.sum(sums[0], axis=0, keepdims=True)
        sums_out[:, 2 * width : 3 * width] = jnp.sum(sums[1], axis=0, keepdims=True)
        early[3].wait()
        gm[...] = dot_t(low[...], wo[...]).astype(BF)

    @pl.when(turn >= 0)
    def _():
        for copy in loads(turn, slot):
            copy.wait()
        scale = HEAD_DIM ** (-0.5)
        own = 3 - slot
        q = lambda here, lanes: slope[own, here, lanes]
        k = lambda here, lanes: slope[own, here, slice(part + lanes.start, part + lanes.stop)]
        v = lambda here, lanes: slope[own, here, slice(2 * part + lanes.start, 2 * part + lanes.stop)]
        grad = lambda here, lanes: slope[1, here, slice(3 * part + lanes.start, 3 * part + lanes.stop)]
        slope[1, :, 3 * part : 4 * part] = gm[:, pl.ds(pl.multiple_of(turn * part, part), part)]
        everything = slice(0, rows)
        jobs = []
        for pair in range(part // 128):
            lanes = slice(128 * pair, 128 * pair + 128)
            for spans, probs in ((short_spans, short_p), (long_spans, long_p)):
                for seq, (start, length) in enumerate(spans):
                    here = slice(start, start + length)
                    for half in range(2):
                        jobs.append(dict(
                            pair=pair, here=here, lanes=lanes, half=half, probs=probs, seq=seq,
                            grad_p=dot_t(head_lanes(v(here, lanes), half), grad(here, lanes)),
                        ))
        flipped, delta = {}, {}
        for pair in range(part // 128):
            lanes = slice(128 * pair, 128 * pair + 128)
            flipped[pair] = flip(k(everything, lanes))
            product = flip(grad(everything, lanes)).astype(F32) * mixed_t[slot, lanes, :]
            for half in range(2):
                delta[pair, half] = jnp.sum(product[HEAD_DIM * half : HEAD_DIM * half + HEAD_DIM], axis=0, keepdims=True)
        for job in jobs:
            pair, half = job["pair"], job["half"]
            prob = job["probs"][slot, job["seq"], 2 * pair + half].astype(F32)
            job["grad_s"] = (prob * (job["grad_p"] - delta[pair, half][:, job["here"]])).astype(BF)
        for one, two in zip(jobs[0::2], jobs[1::2]):
            pair, here, lanes = one["pair"], one["here"], one["lanes"]
            grad_value = grad_key = None
            grad_query_t = []
            for job in (one, two):
                half = job["half"]
                prob = job["probs"][slot, job["seq"], 2 * pair + half]
                dv = dot(prob, head_lanes(grad(here, lanes), half))
                dk = dot(job["grad_s"], head_lanes(q(here, lanes), half))
                grad_value = dv if half == 0 else grad_value + dv
                grad_key = dk if half == 0 else grad_key + dk
                grad_query_t.append(dot(flipped[pair][HEAD_DIM * half : HEAD_DIM * half + HEAD_DIM, here], job["grad_s"]))
            slope[1, here, 128 * pair : 128 * pair + 128] = (flip(jnp.concatenate(grad_query_t, axis=0)) * scale).astype(BF)
            slope[1, here, part + 128 * pair : part + 128 * pair + 128] = grad_key.astype(BF)
            slope[1, here, 2 * part + 128 * pair : 2 * part + 128 * pair + 128] = grad_value.astype(BF)
        place = pl.multiple_of(turn * part, part)
        sums_out[:, pl.ds(place, part)] = jnp.sum(slope[1, :, :part].astype(F32), axis=0, keepdims=True)
        sums_out[:, pl.ds(width + place, part)] = jnp.sum(slope[1, :, 2 * part : 3 * part].astype(F32), axis=0, keepdims=True)
        total[...] += (
            dot_t(slope[1, :, :part], packed[slot, 0])
            + dot_t(slope[1, :, part : 2 * part], packed[slot, 1])
            + dot_t(slope[1, :, 2 * part : 3 * part], packed[slot, 2])
        )

    @pl.when((turn >= 0) & (turn < attention_steps - 2))
    def _():
        for copy in loads(turn + 2, slot):
            copy.start()

    @pl.when(turn == attention_steps - 1)
    def _():
        low[...] = (total[...] * keep[...]).astype(BF)
        for copy in grads:
            copy.start()
        for copy in outs + grads:
            copy.wait()


def feed_and_attention_backward(shape, keep, attention, cts, feed_w, vectors, block=FEED_BLOCK):
    q, k, v, short_p, long_p, mixed_t, xhat, rstd, first, packed_w, output_w = attention
    short_seqs, short_len, long_seqs, long_len = shape
    rows, width = xhat.shape
    base = short_seqs * short_len
    units = vectors["inner_bias"].shape[1]
    steps = units // block
    part = 256
    heads = part // HEAD_DIM
    once = pl.Buffered(1)
    whole = lambda shp: pl.BlockSpec(shp, lambda j: (0,) * len(shp), pipeline_mode=once)
    vec = whole((1, width))
    anywhere = pl.BlockSpec(memory_space=pl.ANY)
    back = lambda j: jnp.maximum(2 * steps - j, 0)
    inner_turn = lambda j: jnp.where(j <= steps, jnp.minimum(j, steps - 1), back(j))
    down_turn = lambda j: jnp.where(j <= steps, jnp.maximum(j - 1, 0), back(j))
    total_width = 6 * width + units
    return pl.pallas_call(
        partial(tail_kernel, shape, steps),
        grid=(2 * steps + 1 + width // part,),
        in_specs=[
            whole((rows, 1)), whole((rows, 1)), whole((rows, width)),
            inner_block(feed_w, block, inner_turn), down_block(feed_w, block, down_turn),
            pl.BlockSpec((1, block), lambda j: (0, jnp.minimum(j, steps - 1))), vec, vec, vec, vec, vec,
            *[anywhere] * 11,
        ],
        out_specs=[anywhere] * 4 + [pl.BlockSpec((1, total_width), lambda j: (0, 0))],
        out_shape=[
            jax.ShapeDtypeStruct(cts[0].shape, BF), jax.ShapeDtypeStruct(cts[1].shape, BF),
            jax.ShapeDtypeStruct(cts[0].shape, BF), jax.ShapeDtypeStruct(cts[1].shape, BF),
            jax.ShapeDtypeStruct((1, total_width), F32),
        ],
        scratch_shapes=[
            pltpu.VMEM((rows, width), F32), pltpu.VMEM((rows, width), BF), pltpu.VMEM((2, rows, block), F32),
            pltpu.VMEM((steps, rows, block), BF), pltpu.VMEM((2, 8, width), F32),
            pltpu.VMEM((rows, width), F32), pltpu.VMEM((rows, width), BF), pltpu.VMEM((width, width), BF),
            pltpu.VMEM((2, short_seqs, heads, short_len, short_len), BF),
            pltpu.VMEM((2, long_seqs, heads, long_len, long_len), BF),
            pltpu.VMEM((2, part, rows), F32), pltpu.VMEM((2, 3, width, part), BF), pltpu.VMEM((rows, width), BF),
            pltpu.SemaphoreType.DMA((8,)), pltpu.SemaphoreType.DMA((2, 9)),
        ],
        compiler_params=pltpu.CompilerParams(vmem_limit_bytes=TAIL_VMEM_BYTES),
        cost_estimate=pl.CostEstimate(flops=85 * 10**9, bytes_accessed=90 * 10**6, transcendentals=4 * 10**6),
        name="feed_and_attention_backward",
    )(
        keep, rstd, first, feed_w, feed_w, vectors["inner_bias"],
        vectors["first_gain"], vectors["first_beta"], vectors["second_gain"], vectors["second_beta"], vectors["down_bias"],
        xhat, *cts, output_w, q, k, v, short_p, long_p, mixed_t, packed_w,
    )


def local(
    short_input, short_lengths, short_cotangent, long_input, long_lengths, long_cotangent,
    packed_weight, output_weight, inner_weight, down_weight,
    first_gain, second_gain, query_bias, value_bias, output_bias, inner_bias, down_bias, first_beta, second_beta,
):
    short_seqs, short_len, width = short_input.shape
    long_seqs, long_len, _ = long_input.shape
    shape = (short_seqs, short_len, long_seqs, long_len)
    lengths = (short_lengths, long_lengths)
    vectors = dict(
        first_gain=first_gain, second_gain=second_gain, query_bias=query_bias, value_bias=value_bias,
        output_bias=output_bias, inner_bias=inner_bias, down_bias=down_bias, first_beta=first_beta, second_beta=second_beta,
    )
    vectors = {name: item.reshape(1, -1) for name, item in vectors.items()}
    xs = (short_input.reshape(-1, width), long_input.reshape(-1, width))
    cts = (short_cotangent.reshape(-1, width), long_cotangent.reshape(-1, width))
    weights = gather_weights(packed_weight, output_weight, inner_weight, down_weight)
    attention = attention_forward(shape, lengths, xs, weights, vectors)
    keep = jnp.concatenate([
        (jnp.arange(item.shape[1])[None, :] < length[:, None]).reshape(-1, 1)
        for item, length in ((short_input, short_lengths), (long_input, long_lengths))
    ], axis=0).astype(F32)
    short_out, long_out, short_grad, long_grad, sums = feed_and_attention_backward(
        shape, keep, attention, cts, weights["feed"], vectors
    )
    sums = sum_all(sums).reshape(-1)
    outs = []
    at = 0
    for size in (width, width, width, inner_bias.shape[0], width, width, width):
        outs.append(lax.slice_in_dim(sums, at, at + size))
        at += size
    return (
        short_out.reshape(short_input.shape), short_grad.reshape(short_input.shape),
        long_out.reshape(long_input.shape), long_grad.reshape(long_input.shape), *outs,
    )


def exchange(block, mask):
    count = lax.axis_size("dp")
    return lax.ppermute(block, "dp", [(i, i ^ mask(i)) for i in range(count)])


CORE, X, Y, Z_NEAR, Z_FAR = 1, 2, 4, 8, 16


def side_first(index):
    return X if index & CORE == 0 else Y


def side_second(index):
    return Y if index & CORE == 0 else X


def gather_by_exchange(shard):
    held = jnp.concatenate([shard, exchange(shard, lambda i: Z_FAR)])
    held = jnp.concatenate([held, exchange(held, side_first)])
    held = jnp.concatenate([held, exchange(held, lambda i: Z_NEAR)])
    other = exchange(held, side_second)
    return [held, other, exchange(held, lambda i: CORE), exchange(other, lambda i: CORE)]


def exchange_slots():
    def mask(core, swap, far, slot):
        owner = core ^ swap
        return (
            swap * CORE + far * side_second(owner) + Z_FAR * (slot & 1)
            + side_first(owner) * (slot >> 1 & 1) + Z_NEAR * (slot >> 2)
        )

    return [
        [(mask(0, swap, far, slot), mask(1, swap, far, slot)) for slot in range(8)]
        for swap in (0, 1) for far in (0, 1)
    ]


def pack_kernel(inner, down, out):
    tall, width = inner.shape[0], down.shape[1]
    blocks = inner.shape[1] // width
    for i in range(blocks):
        out[i * tall : (i + 1) * tall, :] = inner[:, i * width : (i + 1) * width]
    out[blocks * tall :, :] = down[...]


def pack_rows(inner, down):
    width = down.shape[1]
    rows = inner.shape[1] // width * inner.shape[0] + down.shape[0]
    return pl.pallas_call(
        pack_kernel, out_shape=jax.ShapeDtypeStruct((rows, width), inner.dtype), name="pack_rows"
    )(inner, down)


def gather_weights(packed, output, inner, down):
    count = lax.axis_size("dp")
    width = output.shape[1]
    half = width // 2
    sides = [
        jnp.concatenate([packed[:, i * width + at : i * width + at + half] for i in range(3)], axis=1) for at in (0, half)
    ]
    parts = [*sides, output]
    tall = inner.shape[0]
    blocks = inner.shape[1] // width
    if count == 32:
        feed = lax.all_gather(pack_rows(inner, down), "dp", axis=0, tiled=False)
        gathered = [gather_by_exchange(part) for part in parts]
        return dict(
            me=lax.axis_index("dp").reshape(1).astype(jnp.int32), slots=exchange_slots(),
            pieces=[gathered[part][piece] for piece in range(4) for part in range(3)], feed=feed,
        )
    whole = [lax.all_gather(part, "dp", axis=0, tiled=True) for part in (*parts, inner, down)]
    shards = 32
    feed = jnp.concatenate(
        [
            whole[3].reshape(shards, -1, blocks, width).transpose(0, 2, 1, 3).reshape(shards, -1, width),
            whole[4].reshape(shards, -1, width),
        ],
        axis=1,
    )
    return dict(me=jnp.zeros((1,), jnp.int32), slots=[[(i, i) for i in range(shards)]], pieces=whole[:3], feed=feed)


def sum_all(vector):
    count = lax.axis_size("dp")
    if count & (count - 1):
        return lax.psum(vector, "dp")
    vector = vector + exchange(vector, lambda i: 1) if count > 1 else vector
    bit = 2
    while bit < count:
        near = exchange(vector, lambda i: bit)
        if 2 * bit < count:
            far = exchange(vector, lambda i: 2 * bit)
            both = exchange(vector, lambda i: 3 * bit)
            vector = (vector + near) + (far + both)
        else:
            vector = vector + near
        bit *= 4
    return vector


def solution(mesh):
    rows = P("dp", None, None)
    in_specs = (rows, P("dp"), rows, rows, P("dp"), rows) + (P("dp", None),) * 4 + (P(),) * 9
    out_specs = (rows,) * 4 + (P(),) * 7
    return jax.shard_map(local, mesh=mesh, in_specs=in_specs, out_specs=out_specs, check_vma=False)
```

```python
from functools import partial

import jax
import jax.numpy as jnp
from jax import lax
from jax.experimental import pallas as pl
from jax.experimental.pallas import tpu as pltpu
from jax.sharding import PartitionSpec as P

HEADS = 16
HEAD_DIM = 64
BF = jnp.bfloat16
F32 = jnp.float32
VMEM_BYTES = 60 * 1024 * 1024
FEED_BLOCK = 1024
TAIL_VMEM_BYTES = 63 * 1024 * 1024


def dot(left, right):
    return lax.dot_general(left, right, (((1,), (0,)), ((), ())), preferred_element_type=F32)


def dot_t(left, right):
    return lax.dot_general(left, right, (((1,), (1,)), ((), ())), preferred_element_type=F32)


def sequences(short_seqs, short_len, long_seqs, long_len):
    spans = [(i * short_len, short_len) for i in range(short_seqs)]
    base = short_seqs * short_len
    return spans, [(base + i * long_len, long_len) for i in range(long_seqs)]


def row_mask(short_lengths, long_lengths, shape):
    short_seqs, short_len, long_seqs, long_len = shape
    pieces = []
    for count, length, refs in (
        (short_seqs, short_len, short_lengths),
        (long_seqs, long_len, long_lengths),
    ):
        for i in range(count):
            rows = lax.broadcasted_iota(jnp.int32, (length, 1), 0)
            pieces.append(jnp.where(rows < refs[i], 1.0, 0.0).astype(F32))
    return jnp.concatenate(pieces, axis=0)


def head_lanes(block, half):
    lanes = lax.broadcasted_iota(jnp.int32, block.shape, 1)
    keep = lanes < HEAD_DIM if half == 0 else lanes >= HEAD_DIM
    return jnp.where(keep, block, jnp.zeros_like(block))


def flip(block):
    return jnp.transpose(block, (1, 0))


def attention_forward_kernel(
    shape, slots, me, short_lengths, long_lengths, short_x, long_x, *refs,
):
    pieces, refs = refs[: 3 * len(slots)], refs[3 * len(slots) :]
    (
        qb, vb, ob, gain1, beta1, q_out, k_out, v_out, short_p, long_p, mixed_t, xhat_out, rstd_out, first_out,
        packed_out, output_out,
        x_all, mixed, packed, wo, in_sems, out_sems,
    ) = refs
    step = pl.program_id(0)
    steps = pl.num_programs(0)
    short_seqs, short_len, long_seqs, long_len = shape
    base = short_seqs * short_len
    width = q_out.shape[1]
    half_width = packed.shape[2]
    short_spans, long_spans = sequences(*shape)
    targets = (packed.at[0], packed.at[1], wo)

    @pl.when(step == 0)
    def _():
        for part in range(3):
            for ref, masks in zip(pieces[part::3], slots):
                tall = ref.shape[0] // len(masks)
                for slot, mask in enumerate(masks):
                    mask = jnp.where(jnp.bitwise_and(me[0], 1) == 0, mask[0], mask[1])
                    place = pl.multiple_of(jnp.bitwise_xor(me[0], mask) * tall, tall)
                    pltpu.make_async_copy(
                        ref.at[pl.ds(slot * tall, tall)], targets[part].at[pl.ds(place, tall)], in_sems.at[part]
                    ).start()
        x_all[:base, :] = short_x[...]
        x_all[base:, :] = long_x[...]

    keeps = [
        pltpu.make_async_copy(packed.at[0], packed_out.at[0], out_sems.at[0]),
        pltpu.make_async_copy(packed.at[1], packed_out.at[1], out_sems.at[1]),
        pltpu.make_async_copy(wo, output_out, out_sems.at[2]),
    ]
    for part, first_step in enumerate((0, steps // 2, steps - 1)):
        @pl.when(step == first_step)
        def _():
            pltpu.make_async_copy(targets[part], targets[part], in_sems.at[part]).wait()
            keeps[part].start()

    x = x_all[...]
    side = step // (steps // 2)
    turn = lax.rem(step, steps // 2)
    third = half_width // 3
    weight = lambda which: packed[side, :, pl.ds(pl.multiple_of(which * third + turn * width, width), width)]
    q_out[...] = ((dot(x, weight(0)) + qb[...]).astype(BF).astype(F32) * HEAD_DIM ** (-0.5)).astype(BF)
    k_out[...] = dot(x, weight(1)).astype(BF)
    v_out[...] = (dot(x, weight(2)) + vb[...]).astype(BF)
    groups = ((short_spans, short_lengths, short_p), (long_spans, long_lengths, long_p))
    pairs = range(width // 128)
    jobs = []
    for pair in pairs:
        lanes = slice(128 * pair, 128 * pair + 128)
        for spans, refs, probs in groups:
            for seq, (start, length) in enumerate(spans):
                k2 = k_out[start : start + length, lanes]
                usable = lax.broadcasted_iota(jnp.int32, (length, 1), 0) < refs[seq]
                block = min(length, 512)
                for half in range(2):
                    for at in range(0, length, block):
                        jobs.append(dict(pair=pair, probs=probs, seq=seq, start=start, length=length, usable=usable, half=half, at=at, block=block, lanes=lanes,
                            scores=dot_t(head_lanes(k2, half), q_out[start + at : start + at + block, lanes])))
    for job in jobs:
        scores = jnp.where(job["usable"], job["scores"], -1e30)
        top = jnp.max(scores, axis=0, keepdims=True)
        powers = jnp.exp(scores - top)
        total = jnp.sum(powers, axis=0, keepdims=True)
        job["prob"] = (powers * (1.0 / total)).astype(BF)
        job["probs"][job["seq"], 2 * job["pair"] + job["half"], :, job["at"] : job["at"] + job["block"]] = job["prob"]

    flipped = {pair: flip(v_out[:, 128 * pair : 128 * pair + 128]) for pair in pairs}
    for job in jobs:
        feature = 128 * job["pair"] + HEAD_DIM * job["half"]
        v_head = flipped[job["pair"]][HEAD_DIM * job["half"] : HEAD_DIM * job["half"] + HEAD_DIM, job["start"] : job["start"] + job["length"]]
        mixed_t[feature : feature + HEAD_DIM, job["start"] + job["at"] : job["start"] + job["at"] + job["block"]] = dot(v_head, job["prob"])
    for pair in pairs:
        offset = pl.multiple_of(step * width + 128 * pair, 128)
        mixed[:, pl.ds(offset, 128)] = flip(mixed_t[128 * pair : 128 * pair + 128, :]).astype(BF)

    @pl.when(step == steps - 1)
    def _():
        first_sum = x_all[...].astype(F32) + (dot(mixed[...], wo[...]) + ob[...])
        center = first_sum - jnp.mean(first_sum, axis=-1, keepdims=True)
        spread = jnp.mean(center * center, axis=-1, keepdims=True)
        rstd = lax.rsqrt(spread + 1e-06)
        xhat = center * rstd
        xhat_out[...] = xhat
        rstd_out[...] = rstd
        first_out[...] = (xhat * gain1[...] + beta1[...]).astype(BF)
        for keep in keeps:
            keep.wait()


def attention_forward(shape, lengths, xs, weights, vectors):
    short_seqs, short_len, long_seqs, long_len = shape
    rows = short_seqs * short_len + long_seqs * long_len
    width = xs[0].shape[1]
    block = 256
    heads = block // HEAD_DIM
    steps = width // block
    whole = lambda shp: pl.BlockSpec(shp, lambda j: (0,) * len(shp))
    smem = pl.BlockSpec(memory_space=pltpu.SMEM)
    anywhere = pl.BlockSpec(memory_space=pl.ANY)
    row_block = pl.BlockSpec((1, block), lambda j: (0, j))
    out_col = pl.BlockSpec((rows, block), lambda j: (0, j))
    half_width = 3 * width // 2
    return pl.pallas_call(
        partial(attention_forward_kernel, shape, weights["slots"]),
        grid=(steps,),
        in_specs=[
            smem, smem, smem, whole(xs[0].shape), whole(xs[1].shape),
            *[anywhere] * len(weights["pieces"]), row_block, row_block, *[whole((1, width))] * 3,
        ],
        out_specs=[
            out_col, out_col, out_col,
            pl.BlockSpec((short_seqs, heads, short_len, short_len), lambda j: (0, j, 0, 0)),
            pl.BlockSpec((long_seqs, heads, long_len, long_len), lambda j: (0, j, 0, 0)),
            pl.BlockSpec((block, rows), lambda j: (j, 0)),
            whole((rows, width)), whole((rows, 1)), whole((rows, width)), anywhere, anywhere,
        ],
        out_shape=[
            jax.ShapeDtypeStruct((rows, width), BF),
            jax.ShapeDtypeStruct((rows, width), BF),
            jax.ShapeDtypeStruct((rows, width), BF),
            jax.ShapeDtypeStruct((short_seqs, HEADS, short_len, short_len), BF),
            jax.ShapeDtypeStruct((long_seqs, HEADS, long_len, long_len), BF),
            jax.ShapeDtypeStruct((width, rows), F32),
            jax.ShapeDtypeStruct((rows, width), F32),
            jax.ShapeDtypeStruct((rows, 1), F32),
            jax.ShapeDtypeStruct((rows, width), BF),
            jax.ShapeDtypeStruct((2, width, half_width), BF),
            jax.ShapeDtypeStruct((width, width), BF),
        ],
        scratch_shapes=[
            pltpu.VMEM((rows, width), BF), pltpu.VMEM((rows, width), BF),
            pltpu.VMEM((2, width, half_width), BF), pltpu.VMEM((width, width), BF),
            pltpu.SemaphoreType.DMA((3,)), pltpu.SemaphoreType.DMA((3,)),
        ],
        compiler_params=pltpu.CompilerParams(vmem_limit_bytes=VMEM_BYTES),
        cost_estimate=pl.CostEstimate(flops=36 * 10**9, bytes_accessed=40 * 10**6, transcendentals=5 * 10**6),
        name="attention_forward",
    )(
        weights["me"], *lengths, *xs, *weights["pieces"],
        vectors["query_bias"], vectors["value_bias"], vectors["output_bias"],
        vectors["first_gain"], vectors["first_beta"],
    )


def gelu_and_slope(value):
    share = 0.5 + 0.5 * lax.erf(value * 0.5 ** 0.5)
    density = jnp.exp2(value * (value * -0.7213475204444817)) * 0.3989422804014327
    return value * share, share + value * density


def inner_block(feed_w, block, turn):
    shards, _, width = feed_w.shape
    per = width // block
    return pl.BlockSpec((shards, width // shards, block), lambda j: (0, turn(j) // per, lax.rem(turn(j), per)))


def down_block(feed_w, block, turn):
    shards, tall, width = feed_w.shape
    tall = tall // 2
    return pl.BlockSpec((block // tall, tall, width), lambda j: (turn(j), 1, 0))


def norm_gradient(grad, xhat, rstd, gain):
    scaled = grad * gain
    mean = jnp.mean(scaled, axis=-1, keepdims=True)
    along = jnp.mean(scaled * xhat, axis=-1, keepdims=True)
    return rstd * (scaled - mean - xhat * along)


def fold(block):
    return jnp.sum(block.reshape(block.shape[0] // 8, 8, block.shape[1]), axis=0)


def tail_kernel(
    shape, steps, keep, rstd, first, wi, wd, inner_bias, gain1, beta1, gain2, beta2, down_bias,
    xhat_in, short_ct, long_ct, wo_in, q_in, k_in, v_in, short_p_in, long_p_in, mixed_t_in, packed_in,
    short_out, long_out, short_grad, long_grad, sums_out,
    total, low, value, slope, sums, inner_fold, xhat, ct, wo, short_p, long_p, mixed_t, packed, gm, sems, load_sems,
):
    step = pl.program_id(0)
    short_seqs, short_len, long_seqs, long_len = shape
    base = short_seqs * short_len
    rows, width = total.shape
    units = steps * value.shape[2]
    part = packed.shape[3]
    attention_steps = width // part
    heads = part // HEAD_DIM
    first_attention = 2 * steps + 1
    turn = step - first_attention
    slot = lax.rem(jnp.maximum(turn, 0), 2)
    chunk = 128
    wide = lambda ref: ref[...].reshape(width, -1)
    tall = lambda ref: ref[...].reshape(-1, width)
    short_spans, long_spans = sequences(*shape)

    early = [
        pltpu.make_async_copy(short_ct, ct.at[:base], sems.at[0]),
        pltpu.make_async_copy(long_ct, ct.at[base:], sems.at[1]),
        pltpu.make_async_copy(xhat_in, xhat, sems.at[2]),
        pltpu.make_async_copy(wo_in, wo, sems.at[3]),
    ]
    outs = [
        pltpu.make_async_copy(ct.at[:base], short_out, sems.at[4]),
        pltpu.make_async_copy(ct.at[base:], long_out, sems.at[5]),
    ]
    grads = [
        pltpu.make_async_copy(low.at[:base], short_grad, sems.at[6]),
        pltpu.make_async_copy(low.at[base:], long_grad, sems.at[7]),
    ]

    def loads(at, into):
        columns = pl.ds(pl.multiple_of(at * part, part), part)
        side = at // (attention_steps // 2)
        within = lax.rem(at, attention_steps // 2)
        third = packed_in.shape[2] // 3
        pairs = [(ref.at[:, columns], slope.at[3 - into, :, part * i : part * i + part]) for i, ref in enumerate((q_in, k_in, v_in))]
        pairs += [
            (short_p_in.at[:, pl.ds(at * heads, heads)], short_p.at[into]),
            (long_p_in.at[:, pl.ds(at * heads, heads)], long_p.at[into]),
            (mixed_t_in.at[columns], mixed_t.at[into]),
        ]
        pairs += [
            (
                packed_in.at[side, :, pl.ds(pl.multiple_of(i * third + within * part, part), part)],
                packed.at[into, i],
            )
            for i in range(3)
        ]
        return [pltpu.make_async_copy(a, b, load_sems.at[into, i]) for i, (a, b) in enumerate(pairs)]

    def first_part():
        value[lax.rem(step, 2)] = dot(first[...], wide(wi)) + inner_bias[...]

    def second_part():
        act, slp = gelu_and_slope(value[lax.rem(step + 1, 2)])
        slope[step - 1] = slp.astype(BF)
        total[...] += dot(act.astype(BF), tall(wd))

    @pl.when(step == 0)
    def _():
        for copy in early:
            copy.start()
        first_part()
        total[...] = jnp.broadcast_to(down_bias[...], total.shape)

    @pl.when((step > 0) & (step < steps))
    def _():
        first_part()
        second_part()

    @pl.when(step == steps)
    def _():
        for copy in early[:3]:
            copy.wait()
        second_part()
        sums[...] = jnp.zeros_like(sums)

        def body(i, _):
            here = pl.ds(pl.multiple_of(i * chunk, chunk), chunk)
            second = total[here, :] + (xhat[here, :] * gain1[...] + beta1[...])
            center = second - jnp.mean(second, axis=-1, keepdims=True)
            spread = jnp.mean(center * center, axis=-1, keepdims=True)
            rstd2 = lax.rsqrt(spread + 1e-06)
            xhat2 = center * rstd2
            usable = keep[here, :]
            grad_out = ct[here, :].astype(F32) * usable
            ct[here, :] = ((xhat2 * gain2[...] + beta2[...]) * usable).astype(BF)
            grad_second = norm_gradient(grad_out, xhat2, rstd2, gain2[...])
            rounded = grad_second.astype(BF)
            low[here, :] = rounded
            total[here, :] = grad_second
            sums[0] += fold(grad_out)
            sums[1] += fold(rounded.astype(F32))
            return 0

        lax.fori_loop(0, rows // chunk, body, 0)
        for copy in outs:
            copy.start()
        sums_out[:, 5 * width + units : 6 * width + units] = jnp.sum(sums[0], axis=0, keepdims=True)
        sums_out[:, 3 * width + units : 4 * width + units] = jnp.sum(sums[1], axis=0, keepdims=True)

    @pl.when((step > steps) & (step < 2 * steps))
    def _():
        grad_inner = (dot_t(low[...], tall(wd)) * slope[2 * steps - step].astype(F32)).astype(BF)
        place = pl.multiple_of(3 * width + (2 * steps - step) * wd.shape[0] * wd.shape[1], 128)
        sums_out[:, pl.ds(place, value.shape[2])] = jnp.sum(grad_inner.astype(F32), axis=0, keepdims=True)
        total[...] += dot_t(grad_inner, wide(wi))

    @pl.when(step == 2 * steps - 1)
    def _():
        for copy in loads(0, 0):
            copy.start()

    @pl.when(step == 2 * steps)
    def _():
        for copy in loads(1, 1):
            copy.start()
        early[3].wait()
        sums[...] = jnp.zeros_like(sums)
        inner_fold[...] = jnp.zeros_like(inner_fold)
        chunks = [slice(at, at + rows // 2) for at in range(0, rows, rows // 2)]
        firsts = {}
        for turn_of in range(len(chunks) + 2):
            if turn_of < len(chunks):
                ahead = chunks[turn_of]
                grad_active = dot_t(low[ahead], tall(wd))
            if turn_of >= 2:
                back_here = chunks[turn_of - 2]
                mixed_grad = dot_t(low[back_here], wo[...])
            if 0 < turn_of <= len(chunks):
                here = chunks[turn_of - 1]
                grad_first = firsts.pop(turn_of - 1)
                result = norm_gradient(grad_first, xhat[here], rstd[here], gain1[...])
                total[here] = result
                branch = result.astype(BF)
                low[here] = branch
                sums[0] += fold(grad_first)
                sums[1] += fold(branch.astype(F32))
            if turn_of < len(chunks):
                grad_inner = (grad_active * slope[0, ahead].astype(F32)).astype(BF)
                firsts[turn_of] = total[ahead] + dot_t(grad_inner, wide(wi))
                inner_fold[...] += fold(grad_inner.astype(F32))
            if turn_of >= 2:
                gm[back_here] = mixed_grad.astype(BF)
        sums_out[:, 4 * width + units : 5 * width + units] = jnp.sum(sums[0], axis=0, keepdims=True)
        sums_out[:, 2 * width : 3 * width] = jnp.sum(sums[1], axis=0, keepdims=True)
        sums_out[:, 3 * width : 3 * width + value.shape[2]] = jnp.sum(inner_fold[...], axis=0, keepdims=True)

    @pl.when(turn >= 0)
    def _():
        for copy in loads(turn, slot):
            copy.wait()
        scale = HEAD_DIM ** (-0.5)
        own = 3 - slot
        q = lambda here, lanes: slope[own, here, lanes]
        k = lambda here, lanes: slope[own, here, slice(part + lanes.start, part + lanes.stop)]
        v = lambda here, lanes: slope[own, here, slice(2 * part + lanes.start, 2 * part + lanes.stop)]
        grad = lambda here, lanes: slope[1, here, slice(3 * part + lanes.start, 3 * part + lanes.stop)]
        slope[1, :, 3 * part : 4 * part] = gm[:, pl.ds(pl.multiple_of(turn * part, part), part)]
        everything = slice(0, rows)
        jobs = []
        for pair in range(part // 128):
            lanes = slice(128 * pair, 128 * pair + 128)
            for spans, probs in ((short_spans, short_p), (long_spans, long_p)):
                for seq, (start, length) in enumerate(spans):
                    here = slice(start, start + length)
                    for half in range(2):
                        jobs.append(dict(
                            pair=pair, here=here, lanes=lanes, half=half, probs=probs, seq=seq,
                            grad_p=dot_t(head_lanes(v(here, lanes), half), grad(here, lanes)),
                        ))
        flipped, delta = {}, {}
        for pair in range(part // 128):
            lanes = slice(128 * pair, 128 * pair + 128)
            flipped[pair] = flip(k(everything, lanes))
            product = flip(grad(everything, lanes)).astype(F32) * mixed_t[slot, lanes, :]
            for half in range(2):
                delta[pair, half] = jnp.sum(product[HEAD_DIM * half : HEAD_DIM * half + HEAD_DIM], axis=0, keepdims=True)
        for job in jobs:
            pair, half = job["pair"], job["half"]
            prob = job["probs"][slot, job["seq"], 2 * pair + half].astype(F32)
            job["grad_s"] = (prob * (job["grad_p"] - delta[pair, half][:, job["here"]])).astype(BF)
        for one, two in zip(jobs[0::2], jobs[1::2]):
            pair, here, lanes = one["pair"], one["here"], one["lanes"]
            probs2 = [job["probs"][slot, job["seq"], 2 * pair + job["half"]] for job in (one, two)]
            grad_value = dot(
                jnp.concatenate(probs2, axis=1),
                jnp.concatenate([head_lanes(grad(here, lanes), half) for half in range(2)], axis=0),
            )
            grad_key = dot(
                jnp.concatenate([one["grad_s"], two["grad_s"]], axis=1),
                jnp.concatenate([head_lanes(q(here, lanes), half) for half in range(2)], axis=0),
            )
            k_t = flipped[pair][:, here]
            first_head = lax.broadcasted_iota(jnp.int32, k_t.shape, 0) < HEAD_DIM
            zero = jnp.zeros_like(k_t)
            grad_query_t = dot(
                jnp.concatenate([jnp.where(first_head, k_t, zero), jnp.where(first_head, zero, k_t)], axis=1),
                jnp.concatenate([one["grad_s"], two["grad_s"]], axis=0),
            )
            slope[1, here, 128 * pair : 128 * pair + 128] = (flip(grad_query_t) * scale).astype(BF)
            slope[1, here, part + 128 * pair : part + 128 * pair + 128] = grad_key.astype(BF)
            slope[1, here, 2 * part + 128 * pair : 2 * part + 128 * pair + 128] = grad_value.astype(BF)
        place = pl.multiple_of(turn * part, part)
        sums_out[:, pl.ds(place, part)] = jnp.sum(slope[1, :, :part].astype(F32), axis=0, keepdims=True)
        sums_out[:, pl.ds(width + place, part)] = jnp.sum(slope[1, :, 2 * part : 3 * part].astype(F32), axis=0, keepdims=True)
        total[...] += (
            dot_t(slope[1, :, :part], packed[slot, 0])
            + dot_t(slope[1, :, part : 2 * part], packed[slot, 1])
            + dot_t(slope[1, :, 2 * part : 3 * part], packed[slot, 2])
        )

    @pl.when((turn >= 0) & (turn < attention_steps - 2))
    def _():
        for copy in loads(turn + 2, slot):
            copy.start()

    @pl.when(turn == attention_steps - 1)
    def _():
        low[...] = (total[...] * keep[...]).astype(BF)
        for copy in grads:
            copy.start()
        for copy in outs + grads:
            copy.wait()


def feed_and_attention_backward(shape, keep, attention, cts, feed_w, vectors, block=FEED_BLOCK):
    q, k, v, short_p, long_p, mixed_t, xhat, rstd, first, packed_w, output_w = attention
    short_seqs, short_len, long_seqs, long_len = shape
    rows, width = xhat.shape
    base = short_seqs * short_len
    units = vectors["inner_bias"].shape[1]
    steps = units // block
    part = 256
    heads = part // HEAD_DIM
    once = pl.Buffered(1)
    whole = lambda shp: pl.BlockSpec(shp, lambda j: (0,) * len(shp), pipeline_mode=once)
    vec = whole((1, width))
    anywhere = pl.BlockSpec(memory_space=pl.ANY)
    back = lambda j: jnp.maximum(2 * steps - j, 0)
    inner_turn = lambda j: jnp.where(j <= steps, jnp.minimum(j, steps - 1), back(j))
    down_turn = lambda j: jnp.where(j <= steps, jnp.maximum(j - 1, 0), back(j))
    total_width = 6 * width + units
    return pl.pallas_call(
        partial(tail_kernel, shape, steps),
        grid=(2 * steps + 1 + width // part,),
        in_specs=[
            whole((rows, 1)), whole((rows, 1)), whole((rows, width)),
            inner_block(feed_w, block, inner_turn), down_block(feed_w, block, down_turn),
            pl.BlockSpec((1, block), lambda j: (0, jnp.minimum(j, steps - 1))), vec, vec, vec, vec, vec,
            *[anywhere] * 11,
        ],
        out_specs=[anywhere] * 4 + [pl.BlockSpec((1, total_width), lambda j: (0, 0))],
        out_shape=[
            jax.ShapeDtypeStruct(cts[0].shape, BF), jax.ShapeDtypeStruct(cts[1].shape, BF),
            jax.ShapeDtypeStruct(cts[0].shape, BF), jax.ShapeDtypeStruct(cts[1].shape, BF),
            jax.ShapeDtypeStruct((1, total_width), F32),
        ],
        scratch_shapes=[
            pltpu.VMEM((rows, width), F32), pltpu.VMEM((rows, width), BF), pltpu.VMEM((2, rows, block), F32),
            pltpu.VMEM((steps, rows, block), BF), pltpu.VMEM((2, 8, width), F32), pltpu.VMEM((8, block), F32),
            pltpu.VMEM((rows, width), F32), pltpu.VMEM((rows, width), BF), pltpu.VMEM((width, width), BF),
            pltpu.VMEM((2, short_seqs, heads, short_len, short_len), BF),
            pltpu.VMEM((2, long_seqs, heads, long_len, long_len), BF),
            pltpu.VMEM((2, part, rows), F32), pltpu.VMEM((2, 3, width, part), BF), pltpu.VMEM((rows, width), BF),
            pltpu.SemaphoreType.DMA((8,)), pltpu.SemaphoreType.DMA((2, 9)),
        ],
        compiler_params=pltpu.CompilerParams(vmem_limit_bytes=TAIL_VMEM_BYTES),
        cost_estimate=pl.CostEstimate(flops=85 * 10**9, bytes_accessed=90 * 10**6, transcendentals=4 * 10**6),
        name="feed_and_attention_backward",
    )(
        keep, rstd, first, feed_w, feed_w, vectors["inner_bias"],
        vectors["first_gain"], vectors["first_beta"], vectors["second_gain"], vectors["second_beta"], vectors["down_bias"],
        xhat, *cts, output_w, q, k, v, short_p, long_p, mixed_t, packed_w,
    )


def local(
    short_input, short_lengths, short_cotangent, long_input, long_lengths, long_cotangent,
    packed_weight, output_weight, inner_weight, down_weight,
    first_gain, second_gain, query_bias, value_bias, output_bias, inner_bias, down_bias, first_beta, second_beta,
):
    short_seqs, short_len, width = short_input.shape
    long_seqs, long_len, _ = long_input.shape
    shape = (short_seqs, short_len, long_seqs, long_len)
    lengths = (short_lengths, long_lengths)
    vectors = dict(
        first_gain=first_gain, second_gain=second_gain, query_bias=query_bias, value_bias=value_bias,
        output_bias=output_bias, inner_bias=inner_bias, down_bias=down_bias, first_beta=first_beta, second_beta=second_beta,
    )
    vectors = {name: item.reshape(1, -1) for name, item in vectors.items()}
    xs = (short_input.reshape(-1, width), long_input.reshape(-1, width))
    cts = (short_cotangent.reshape(-1, width), long_cotangent.reshape(-1, width))
    weights = gather_weights(packed_weight, output_weight, inner_weight, down_weight)
    attention = attention_forward(shape, lengths, xs, weights, vectors)
    keep = jnp.concatenate([
        (jnp.arange(item.shape[1])[None, :] < length[:, None]).reshape(-1, 1)
        for item, length in ((short_input, short_lengths), (long_input, long_lengths))
    ], axis=0).astype(F32)
    short_out, long_out, short_grad, long_grad, sums = feed_and_attention_backward(
        shape, keep, attention, cts, weights["feed"], vectors
    )
    sums = sum_all(sums).reshape(-1)
    outs = []
    at = 0
    for size in (width, width, width, inner_bias.shape[0], width, width, width):
        outs.append(lax.slice_in_dim(sums, at, at + size))
        at += size
    return (
        short_out.reshape(short_input.shape), short_grad.reshape(short_input.shape),
        long_out.reshape(long_input.shape), long_grad.reshape(long_input.shape), *outs,
    )


def exchange(block, mask):
    count = lax.axis_size("dp")
    return lax.ppermute(block, "dp", [(i, i ^ mask(i)) for i in range(count)])


CORE, X, Y, Z_NEAR, Z_FAR = 1, 2, 4, 8, 16


def side_first(index):
    return X if index & CORE == 0 else Y


def side_second(index):
    return Y if index & CORE == 0 else X


def gather_by_exchange(shard):
    held = jnp.concatenate([shard, exchange(shard, lambda i: Z_FAR)])
    held = jnp.concatenate([held, exchange(held, side_first)])
    held = jnp.concatenate([held, exchange(held, lambda i: Z_NEAR)])
    other = exchange(held, side_second)
    return [held, other, exchange(held, lambda i: CORE), exchange(other, lambda i: CORE)]


def exchange_slots():
    def mask(core, swap, far, slot):
        owner = core ^ swap
        return (
            swap * CORE + far * side_second(owner) + Z_FAR * (slot & 1)
            + side_first(owner) * (slot >> 1 & 1) + Z_NEAR * (slot >> 2)
        )

    return [
        [(mask(0, swap, far, slot), mask(1, swap, far, slot)) for slot in range(8)]
        for swap in (0, 1) for far in (0, 1)
    ]


def pack_kernel(inner, down, out):
    tall, width = inner.shape[0], down.shape[1]
    blocks = inner.shape[1] // width
    for i in range(blocks):
        out[i * tall : (i + 1) * tall, :] = inner[:, i * width : (i + 1) * width]
    out[blocks * tall :, :] = down[...]


def pack_rows(inner, down):
    width = down.shape[1]
    rows = inner.shape[1] // width * inner.shape[0] + down.shape[0]
    return pl.pallas_call(
        pack_kernel, out_shape=jax.ShapeDtypeStruct((rows, width), inner.dtype), name="pack_rows"
    )(inner, down)


def gather_weights(packed, output, inner, down):
    count = lax.axis_size("dp")
    width = output.shape[1]
    half = width // 2
    sides = [
        jnp.concatenate([packed[:, i * width + at : i * width + at + half] for i in range(3)], axis=1) for at in (0, half)
    ]
    parts = [*sides, output]
    tall = inner.shape[0]
    blocks = inner.shape[1] // width
    if count == 32:
        feed = lax.all_gather(pack_rows(inner, down), "dp", axis=0, tiled=False)
        gathered = [gather_by_exchange(part) for part in parts]
        return dict(
            me=lax.axis_index("dp").reshape(1).astype(jnp.int32), slots=exchange_slots(),
            pieces=[gathered[part][piece] for piece in range(4) for part in range(3)], feed=feed,
        )
    whole = [lax.all_gather(part, "dp", axis=0, tiled=True) for part in (*parts, inner, down)]
    shards = 32
    feed = jnp.concatenate(
        [
            whole[3].reshape(shards, -1, blocks, width).transpose(0, 2, 1, 3).reshape(shards, -1, width),
            whole[4].reshape(shards, -1, width),
        ],
        axis=1,
    )
    return dict(me=jnp.zeros((1,), jnp.int32), slots=[[(i, i) for i in range(shards)]], pieces=whole[:3], feed=feed)


def sum_all(vector):
    count = lax.axis_size("dp")
    if count & (count - 1):
        return lax.psum(vector, "dp")
    vector = vector + exchange(vector, lambda i: 1) if count > 1 else vector
    bit = 2
    while bit < count:
        near = exchange(vector, lambda i: bit)
        if 2 * bit < count:
            far = exchange(vector, lambda i: 2 * bit)
            both = exchange(vector, lambda i: 3 * bit)
            vector = (vector + near) + (far + both)
        else:
            vector = vector + near
        bit *= 4
    return vector


def solution(mesh):
    rows = P("dp", None, None)
    in_specs = (rows, P("dp"), rows, rows, P("dp"), rows) + (P("dp", None),) * 4 + (P(),) * 9
    out_specs = (rows,) * 4 + (P(),) * 7
    return jax.shard_map(local, mesh=mesh, in_specs=in_specs, out_specs=out_specs, check_vma=False)
```

```python
from functools import partial

import jax
import jax.numpy as jnp
from jax import lax
from jax.experimental import pallas as pl
from jax.experimental.pallas import tpu as pltpu
from jax.sharding import PartitionSpec as P

HEADS = 16
HEAD_DIM = 64
BF = jnp.bfloat16
F32 = jnp.float32
VMEM_BYTES = 60 * 1024 * 1024
FEED_BLOCK = 1024
TAIL_VMEM_BYTES = 63 * 1024 * 1024


def dot(left, right):
    return lax.dot_general(left, right, (((1,), (0,)), ((), ())), preferred_element_type=F32)


def dot_t(left, right):
    return lax.dot_general(left, right, (((1,), (1,)), ((), ())), preferred_element_type=F32)


def sequences(short_seqs, short_len, long_seqs, long_len):
    spans = [(i * short_len, short_len) for i in range(short_seqs)]
    base = short_seqs * short_len
    return spans, [(base + i * long_len, long_len) for i in range(long_seqs)]


def row_mask(short_lengths, long_lengths, shape):
    short_seqs, short_len, long_seqs, long_len = shape
    pieces = []
    for count, length, refs in (
        (short_seqs, short_len, short_lengths),
        (long_seqs, long_len, long_lengths),
    ):
        for i in range(count):
            rows = lax.broadcasted_iota(jnp.int32, (length, 1), 0)
            pieces.append(jnp.where(rows < refs[i], 1.0, 0.0).astype(F32))
    return jnp.concatenate(pieces, axis=0)


def head_lanes(block, half):
    lanes = lax.broadcasted_iota(jnp.int32, block.shape, 1)
    keep = lanes < HEAD_DIM if half == 0 else lanes >= HEAD_DIM
    return jnp.where(keep, block, jnp.zeros_like(block))


def flip(block):
    return jnp.transpose(block, (1, 0))


def attention_forward_kernel(
    shape, slots, me, short_lengths, long_lengths, short_x, long_x, *refs,
):
    pieces, refs = refs[: 3 * len(slots)], refs[3 * len(slots) :]
    (
        qb, vb, ob, gain1, beta1, q_out, k_out, v_out, short_p, long_p, mixed_t, xhat_out, rstd_out, first_out,
        packed_out, output_out,
        x_all, mixed, packed, wo, in_sems, out_sems,
    ) = refs
    step = pl.program_id(0)
    steps = pl.num_programs(0)
    short_seqs, short_len, long_seqs, long_len = shape
    base = short_seqs * short_len
    width = q_out.shape[1]
    half_width = packed.shape[2]
    short_spans, long_spans = sequences(*shape)
    targets = (packed.at[0], packed.at[1], wo)

    @pl.when(step == 0)
    def _():
        for part in range(3):
            for ref, masks in zip(pieces[part::3], slots):
                tall = ref.shape[0] // len(masks)
                for slot, mask in enumerate(masks):
                    mask = jnp.where(jnp.bitwise_and(me[0], 1) == 0, mask[0], mask[1])
                    place = pl.multiple_of(jnp.bitwise_xor(me[0], mask) * tall, tall)
                    pltpu.make_async_copy(
                        ref.at[pl.ds(slot * tall, tall)], targets[part].at[pl.ds(place, tall)], in_sems.at[part]
                    ).start()
        x_all[:base, :] = short_x[...]
        x_all[base:, :] = long_x[...]

    keeps = [
        pltpu.make_async_copy(packed.at[0], packed_out.at[0], out_sems.at[0]),
        pltpu.make_async_copy(packed.at[1], packed_out.at[1], out_sems.at[1]),
        pltpu.make_async_copy(wo, output_out, out_sems.at[2]),
    ]
    for part, first_step in enumerate((0, steps // 2, steps - 1)):
        @pl.when(step == first_step)
        def _():
            pltpu.make_async_copy(targets[part], targets[part], in_sems.at[part]).wait()
            keeps[part].start()

    x = x_all[...]
    side = step // (steps // 2)
    turn = lax.rem(step, steps // 2)
    third = half_width // 3
    weight = lambda which: packed[side, :, pl.ds(pl.multiple_of(which * third + turn * width, width), width)]
    q_out[...] = ((dot(x, weight(0)) + qb[...]).astype(BF).astype(F32) * HEAD_DIM ** (-0.5)).astype(BF)
    k_out[...] = dot(x, weight(1)).astype(BF)
    v_out[...] = (dot(x, weight(2)) + vb[...]).astype(BF)
    groups = ((short_spans, short_lengths, short_p), (long_spans, long_lengths, long_p))
    pairs = range(width // 128)
    jobs = []
    for pair in pairs:
        lanes = slice(128 * pair, 128 * pair + 128)
        for spans, refs, probs in groups:
            for seq, (start, length) in enumerate(spans):
                k2 = k_out[start : start + length, lanes]
                usable = lax.broadcasted_iota(jnp.int32, (length, 1), 0) < refs[seq]
                block = min(length, 512)
                for half in range(2):
                    for at in range(0, length, block):
                        jobs.append(dict(pair=pair, probs=probs, seq=seq, start=start, length=length, usable=usable, half=half, at=at, block=block, lanes=lanes,
                            scores=dot_t(head_lanes(k2, half), q_out[start + at : start + at + block, lanes])))
    for job in jobs:
        scores = jnp.where(job["usable"], job["scores"], -1e30)
        top = jnp.max(scores, axis=0, keepdims=True)
        powers = jnp.exp(scores - top)
        total = jnp.sum(powers, axis=0, keepdims=True)
        job["prob"] = (powers * (1.0 / total)).astype(BF)
        job["probs"][job["seq"], 2 * job["pair"] + job["half"], :, job["at"] : job["at"] + job["block"]] = job["prob"]

    flipped = {pair: flip(v_out[:, 128 * pair : 128 * pair + 128]) for pair in pairs}
    for job in jobs:
        feature = 128 * job["pair"] + HEAD_DIM * job["half"]
        v_head = flipped[job["pair"]][HEAD_DIM * job["half"] : HEAD_DIM * job["half"] + HEAD_DIM, job["start"] : job["start"] + job["length"]]
        mixed_t[feature : feature + HEAD_DIM, job["start"] + job["at"] : job["start"] + job["at"] + job["block"]] = dot(v_head, job["prob"])
    for pair in pairs:
        offset = pl.multiple_of(step * width + 128 * pair, 128)
        mixed[:, pl.ds(offset, 128)] = flip(mixed_t[128 * pair : 128 * pair + 128, :]).astype(BF)

    @pl.when(step == steps - 1)
    def _():
        first_sum = x_all[...].astype(F32) + (dot(mixed[...], wo[...]) + ob[...])
        center = first_sum - jnp.mean(first_sum, axis=-1, keepdims=True)
        spread = jnp.mean(center * center, axis=-1, keepdims=True)
        rstd = lax.rsqrt(spread + 1e-06)
        xhat = center * rstd
        xhat_out[...] = xhat
        rstd_out[...] = rstd
        first_out[...] = (xhat * gain1[...] + beta1[...]).astype(BF)
        for keep in keeps:
            keep.wait()


def attention_forward(shape, lengths, xs, weights, vectors):
    short_seqs, short_len, long_seqs, long_len = shape
    rows = short_seqs * short_len + long_seqs * long_len
    width = xs[0].shape[1]
    block = 256
    heads = block // HEAD_DIM
    steps = width // block
    whole = lambda shp: pl.BlockSpec(shp, lambda j: (0,) * len(shp))
    smem = pl.BlockSpec(memory_space=pltpu.SMEM)
    anywhere = pl.BlockSpec(memory_space=pl.ANY)
    row_block = pl.BlockSpec((1, block), lambda j: (0, j))
    out_col = pl.BlockSpec((rows, block), lambda j: (0, j))
    half_width = 3 * width // 2
    return pl.pallas_call(
        partial(attention_forward_kernel, shape, weights["slots"]),
        grid=(steps,),
        in_specs=[
            smem, smem, smem, whole(xs[0].shape), whole(xs[1].shape),
            *[anywhere] * len(weights["pieces"]), row_block, row_block, *[whole((1, width))] * 3,
        ],
        out_specs=[
            out_col, out_col, out_col,
            pl.BlockSpec((short_seqs, heads, short_len, short_len), lambda j: (0, j, 0, 0)),
            pl.BlockSpec((long_seqs, heads, long_len, long_len), lambda j: (0, j, 0, 0)),
            pl.BlockSpec((block, rows), lambda j: (j, 0)),
            whole((rows, width)), whole((rows, 1)), whole((rows, width)), anywhere, anywhere,
        ],
        out_shape=[
            jax.ShapeDtypeStruct((rows, width), BF),
            jax.ShapeDtypeStruct((rows, width), BF),
            jax.ShapeDtypeStruct((rows, width), BF),
            jax.ShapeDtypeStruct((short_seqs, HEADS, short_len, short_len), BF),
            jax.ShapeDtypeStruct((long_seqs, HEADS, long_len, long_len), BF),
            jax.ShapeDtypeStruct((width, rows), F32),
            jax.ShapeDtypeStruct((rows, width), F32),
            jax.ShapeDtypeStruct((rows, 1), F32),
            jax.ShapeDtypeStruct((rows, width), BF),
            jax.ShapeDtypeStruct((2, width, half_width), BF),
            jax.ShapeDtypeStruct((width, width), BF),
        ],
        scratch_shapes=[
            pltpu.VMEM((rows, width), BF), pltpu.VMEM((rows, width), BF),
            pltpu.VMEM((2, width, half_width), BF), pltpu.VMEM((width, width), BF),
            pltpu.SemaphoreType.DMA((3,)), pltpu.SemaphoreType.DMA((3,)),
        ],
        compiler_params=pltpu.CompilerParams(vmem_limit_bytes=VMEM_BYTES),
        cost_estimate=pl.CostEstimate(flops=36 * 10**9, bytes_accessed=40 * 10**6, transcendentals=5 * 10**6),
        name="attention_forward",
    )(
        weights["me"], *lengths, *xs, *weights["pieces"],
        vectors["query_bias"], vectors["value_bias"], vectors["output_bias"],
        vectors["first_gain"], vectors["first_beta"],
    )


def gelu_and_slope(value):
    share = 0.5 + 0.5 * lax.erf(value * 0.5 ** 0.5)
    density = jnp.exp2(value * (value * -0.7213475204444817)) * 0.3989422804014327
    return value * share, share + value * density


def inner_block(feed_w, block, turn):
    shards, _, width = feed_w.shape
    per = width // block
    return pl.BlockSpec((shards, width // shards, block), lambda j: (0, turn(j) // per, lax.rem(turn(j), per)))


def down_block(feed_w, block, turn):
    shards, tall, width = feed_w.shape
    tall = tall // 2
    return pl.BlockSpec((block // tall, tall, width), lambda j: (turn(j), 1, 0))


def norm_gradient(grad, xhat, rstd, gain):
    scaled = grad * gain
    mean = jnp.mean(scaled, axis=-1, keepdims=True)
    along = jnp.mean(scaled * xhat, axis=-1, keepdims=True)
    return rstd * (scaled - mean - xhat * along)


def fold(block):
    return jnp.sum(block.reshape(block.shape[0] // 8, 8, block.shape[1]), axis=0)


def tail_kernel(
    shape, steps, keep, rstd, first, wi, wd, inner_bias, gain1, beta1, gain2, beta2, down_bias,
    xhat_in, short_ct, long_ct, wo_in, q_in, k_in, v_in, short_p_in, long_p_in, mixed_t_in, packed_in,
    short_out, long_out, short_grad, long_grad, sums_out,
    total, low, value, slope, sums, inner_fold, xhat, ct, wo, short_p, long_p, mixed_t, packed, gm, sems, load_sems,
):
    step = pl.program_id(0)
    short_seqs, short_len, long_seqs, long_len = shape
    base = short_seqs * short_len
    rows, width = total.shape
    units = steps * value.shape[2]
    part = packed.shape[2] // 3
    attention_steps = width // part
    heads = part // HEAD_DIM
    first_attention = 2 * steps + 1
    turn = step - first_attention
    slot = lax.rem(jnp.maximum(turn, 0), 2)
    chunk = 224 if rows % 224 == 0 else 128
    wide = lambda ref: ref[...].reshape(width, -1)
    tall = lambda ref: ref[...].reshape(-1, width)
    short_spans, long_spans = sequences(*shape)

    early = [
        pltpu.make_async_copy(short_ct, ct.at[:base], sems.at[0]),
        pltpu.make_async_copy(long_ct, ct.at[base:], sems.at[1]),
        pltpu.make_async_copy(xhat_in, xhat, sems.at[2]),
        pltpu.make_async_copy(wo_in, wo, sems.at[3]),
    ]
    outs = [
        pltpu.make_async_copy(ct.at[:base], short_out, sems.at[4]),
        pltpu.make_async_copy(ct.at[base:], long_out, sems.at[5]),
    ]
    grads = [
        pltpu.make_async_copy(low.at[:base], short_grad, sems.at[6]),
        pltpu.make_async_copy(low.at[base:], long_grad, sems.at[7]),
    ]

    def loads(at, into):
        columns = pl.ds(pl.multiple_of(at * part, part), part)
        side = at // (attention_steps // 2)
        within = lax.rem(at, attention_steps // 2)
        third = packed_in.shape[2] // 3
        pairs = [(ref.at[:, columns], slope.at[3 - into, :, part * i : part * i + part]) for i, ref in enumerate((q_in, k_in, v_in))]
        pairs += [
            (short_p_in.at[:, pl.ds(at * heads, heads)], short_p.at[into]),
            (long_p_in.at[:, pl.ds(at * heads, heads)], long_p.at[into]),
            (mixed_t_in.at[columns], mixed_t.at[into]),
        ]
        pairs += [
            (
                packed_in.at[side, :, pl.ds(pl.multiple_of(i * third + within * part, part), part)],
                packed.at[into, :, part * i : part * i + part],
            )
            for i in range(3)
        ]
        return [pltpu.make_async_copy(a, b, load_sems.at[into, i]) for i, (a, b) in enumerate(pairs)]

    def first_part():
        value[lax.rem(step, 2)] = dot(first[...], wide(wi)) + inner_bias[...]

    def second_part():
        act, slp = gelu_and_slope(value[lax.rem(step + 1, 2)])
        slope[step - 1] = slp.astype(BF)
        total[...] += dot(act.astype(BF), tall(wd))

    @pl.when(step == 0)
    def _():
        for copy in early:
            copy.start()
        first_part()
        total[...] = jnp.broadcast_to(down_bias[...], total.shape)

    @pl.when((step > 0) & (step < steps))
    def _():
        first_part()
        second_part()

    @pl.when(step == steps)
    def _():
        for copy in early[:3]:
            copy.wait()
        second_part()
        sums[...] = jnp.zeros_like(sums)

        def body(i, _):
            here = pl.ds(pl.multiple_of(i * chunk, chunk), chunk)
            second = total[here, :] + (xhat[here, :] * gain1[...] + beta1[...])
            center = second - jnp.mean(second, axis=-1, keepdims=True)
            spread = jnp.mean(center * center, axis=-1, keepdims=True)
            rstd2 = lax.rsqrt(spread + 1e-06)
            xhat2 = center * rstd2
            usable = keep[here, :]
            grad_out = ct[here, :].astype(F32) * usable
            ct[here, :] = ((xhat2 * gain2[...] + beta2[...]) * usable).astype(BF)
            grad_second = norm_gradient(grad_out, xhat2, rstd2, gain2[...])
            rounded = grad_second.astype(BF)
            low[here, :] = rounded
            total[here, :] = grad_second
            sums[0] += fold(grad_out)
            sums[1] += fold(rounded.astype(F32))
            return 0

        lax.fori_loop(0, rows // chunk, body, 0)
        for copy in outs:
            copy.start()
        sums_out[:, 5 * width + units : 6 * width + units] = jnp.sum(sums[0], axis=0, keepdims=True)
        sums_out[:, 3 * width + units : 4 * width + units] = jnp.sum(sums[1], axis=0, keepdims=True)

    @pl.when((step > steps) & (step < 2 * steps))
    def _():
        grad_inner = (dot_t(low[...], tall(wd)) * slope[2 * steps - step].astype(F32)).astype(BF)
        place = pl.multiple_of(3 * width + (2 * steps - step) * wd.shape[0] * wd.shape[1], 128)
        sums_out[:, pl.ds(place, value.shape[2])] = jnp.sum(grad_inner.astype(F32), axis=0, keepdims=True)
        total[...] += dot_t(grad_inner, wide(wi))

    @pl.when(step == 2 * steps - 1)
    def _():
        for copy in loads(0, 0):
            copy.start()

    @pl.when(step == 2 * steps)
    def _():
        for copy in loads(1, 1):
            copy.start()
        early[3].wait()
        sums[...] = jnp.zeros_like(sums)
        inner_fold[...] = jnp.zeros_like(inner_fold)
        chunks = [slice(at, at + rows // 2) for at in range(0, rows, rows // 2)]
        firsts = {}
        for turn_of in range(len(chunks) + 2):
            if turn_of < len(chunks):
                ahead = chunks[turn_of]
                grad_active = dot_t(low[ahead], tall(wd))
            if turn_of >= 2:
                back_here = chunks[turn_of - 2]
                mixed_grad = dot_t(low[back_here], wo[...])
            if 0 < turn_of <= len(chunks):
                here = chunks[turn_of - 1]
                grad_first = firsts.pop(turn_of - 1)
                result = norm_gradient(grad_first, xhat[here], rstd[here], gain1[...])
                total[here] = result
                branch = result.astype(BF)
                low[here] = branch
                sums[0] += fold(grad_first)
                sums[1] += fold(branch.astype(F32))
            if turn_of < len(chunks):
                grad_inner = (grad_active * slope[0, ahead].astype(F32)).astype(BF)
                firsts[turn_of] = total[ahead] + dot_t(grad_inner, wide(wi))
                inner_fold[...] += fold(grad_inner.astype(F32))
            if turn_of >= 2:
                gm[back_here] = mixed_grad.astype(BF)
        sums_out[:, 4 * width + units : 5 * width + units] = jnp.sum(sums[0], axis=0, keepdims=True)
        sums_out[:, 2 * width : 3 * width] = jnp.sum(sums[1], axis=0, keepdims=True)
        sums_out[:, 3 * width : 3 * width + value.shape[2]] = jnp.sum(inner_fold[...], axis=0, keepdims=True)

    @pl.when(turn >= 0)
    def _():
        for copy in loads(turn, slot):
            copy.wait()
        scale = HEAD_DIM ** (-0.5)
        own = 3 - slot
        q = lambda here, lanes: slope[own, here, lanes]
        k = lambda here, lanes: slope[own, here, slice(part + lanes.start, part + lanes.stop)]
        v = lambda here, lanes: slope[own, here, slice(2 * part + lanes.start, 2 * part + lanes.stop)]
        grad = lambda here, lanes: slope[1, here, slice(3 * part + lanes.start, 3 * part + lanes.stop)]
        slope[1, :, 3 * part : 4 * part] = gm[:, pl.ds(pl.multiple_of(turn * part, part), part)]
        everything = slice(0, rows)
        jobs = []
        for pair in range(part // 128):
            lanes = slice(128 * pair, 128 * pair + 128)
            for spans, probs in ((short_spans, short_p), (long_spans, long_p)):
                for seq, (start, length) in enumerate(spans):
                    here = slice(start, start + length)
                    for half in range(2):
                        jobs.append(dict(
                            pair=pair, here=here, lanes=lanes, half=half, probs=probs, seq=seq,
                            grad_p=dot_t(head_lanes(v(here, lanes), half), grad(here, lanes)),
                        ))
        flipped, delta = {}, {}
        for pair in range(part // 128):
            lanes = slice(128 * pair, 128 * pair + 128)
            flipped[pair] = flip(k(everything, lanes))
            product = flip(grad(everything, lanes)).astype(F32) * mixed_t[slot, lanes, :]
            for half in range(2):
                delta[pair, half] = jnp.sum(product[HEAD_DIM * half : HEAD_DIM * half + HEAD_DIM], axis=0, keepdims=True)
        for job in jobs:
            pair, half = job["pair"], job["half"]
            prob = job["probs"][slot, job["seq"], 2 * pair + half].astype(F32)
            job["grad_s"] = (prob * (job["grad_p"] - delta[pair, half][:, job["here"]])).astype(BF)
        for one, two in zip(jobs[0::2], jobs[1::2]):
            pair, here, lanes = one["pair"], one["here"], one["lanes"]
            probs2 = [job["probs"][slot, job["seq"], 2 * pair + job["half"]] for job in (one, two)]
            grad_value = dot(
                jnp.concatenate(probs2, axis=1),
                jnp.concatenate([head_lanes(grad(here, lanes), half) for half in range(2)], axis=0),
            )
            grad_key = dot(
                jnp.concatenate([one["grad_s"], two["grad_s"]], axis=1),
                jnp.concatenate([head_lanes(q(here, lanes), half) for half in range(2)], axis=0),
            )
            k_t = flipped[pair][:, here]
            first_head = lax.broadcasted_iota(jnp.int32, k_t.shape, 0) < HEAD_DIM
            zero = jnp.zeros_like(k_t)
            grad_query_t = dot(
                jnp.concatenate([jnp.where(first_head, k_t, zero), jnp.where(first_head, zero, k_t)], axis=1),
                jnp.concatenate([one["grad_s"], two["grad_s"]], axis=0),
            )
            slope[1, here, 128 * pair : 128 * pair + 128] = (flip(grad_query_t) * scale).astype(BF)
            slope[1, here, part + 128 * pair : part + 128 * pair + 128] = grad_key.astype(BF)
            slope[1, here, 2 * part + 128 * pair : 2 * part + 128 * pair + 128] = grad_value.astype(BF)
        place = pl.multiple_of(turn * part, part)
        sums_out[:, pl.ds(place, part)] = jnp.sum(slope[1, :, :part].astype(F32), axis=0, keepdims=True)
        sums_out[:, pl.ds(width + place, part)] = jnp.sum(slope[1, :, 2 * part : 3 * part].astype(F32), axis=0, keepdims=True)
        total[...] += dot_t(slope[1, :, : 3 * part], packed[slot])

    @pl.when((turn >= 0) & (turn < attention_steps - 2))
    def _():
        for copy in loads(turn + 2, slot):
            copy.start()

    @pl.when(turn == attention_steps - 1)
    def _():
        low[...] = (total[...] * keep[...]).astype(BF)
        for copy in grads:
            copy.start()
        for copy in outs + grads:
            copy.wait()


def feed_and_attention_backward(shape, keep, attention, cts, feed_w, vectors, block=FEED_BLOCK):
    q, k, v, short_p, long_p, mixed_t, xhat, rstd, first, packed_w, output_w = attention
    short_seqs, short_len, long_seqs, long_len = shape
    rows, width = xhat.shape
    base = short_seqs * short_len
    units = vectors["inner_bias"].shape[1]
    steps = units // block
    part = 256
    heads = part // HEAD_DIM
    once = pl.Buffered(1)
    whole = lambda shp: pl.BlockSpec(shp, lambda j: (0,) * len(shp), pipeline_mode=once)
    vec = whole((1, width))
    anywhere = pl.BlockSpec(memory_space=pl.ANY)
    back = lambda j: jnp.maximum(2 * steps - j, 0)
    inner_turn = lambda j: jnp.where(j <= steps, jnp.minimum(j, steps - 1), back(j))
    down_turn = lambda j: jnp.where(j <= steps, jnp.maximum(j - 1, 0), back(j))
    total_width = 6 * width + units
    return pl.pallas_call(
        partial(tail_kernel, shape, steps),
        grid=(2 * steps + 1 + width // part,),
        in_specs=[
            whole((rows, 1)), whole((rows, 1)), whole((rows, width)),
            inner_block(feed_w, block, inner_turn), down_block(feed_w, block, down_turn),
            pl.BlockSpec((1, block), lambda j: (0, jnp.minimum(j, steps - 1))), vec, vec, vec, vec, vec,
            *[anywhere] * 11,
        ],
        out_specs=[anywhere] * 4 + [pl.BlockSpec((1, total_width), lambda j: (0, 0))],
        out_shape=[
            jax.ShapeDtypeStruct(cts[0].shape, BF), jax.ShapeDtypeStruct(cts[1].shape, BF),
            jax.ShapeDtypeStruct(cts[0].shape, BF), jax.ShapeDtypeStruct(cts[1].shape, BF),
            jax.ShapeDtypeStruct((1, total_width), F32),
        ],
        scratch_shapes=[
            pltpu.VMEM((rows, width), F32), pltpu.VMEM((rows, width), BF), pltpu.VMEM((2, rows, block), F32),
            pltpu.VMEM((steps, rows, block), BF), pltpu.VMEM((2, 8, width), F32), pltpu.VMEM((8, block), F32),
            pltpu.VMEM((rows, width), F32), pltpu.VMEM((rows, width), BF), pltpu.VMEM((width, width), BF),
            pltpu.VMEM((2, short_seqs, heads, short_len, short_len), BF),
            pltpu.VMEM((2, long_seqs, heads, long_len, long_len), BF),
            pltpu.VMEM((2, part, rows), F32), pltpu.VMEM((2, width, 3 * part), BF), pltpu.VMEM((rows, width), BF),
            pltpu.SemaphoreType.DMA((8,)), pltpu.SemaphoreType.DMA((2, 9)),
        ],
        compiler_params=pltpu.CompilerParams(vmem_limit_bytes=TAIL_VMEM_BYTES),
        cost_estimate=pl.CostEstimate(flops=85 * 10**9, bytes_accessed=90 * 10**6, transcendentals=4 * 10**6),
        name="feed_and_attention_backward",
    )(
        keep, rstd, first, feed_w, feed_w, vectors["inner_bias"],
        vectors["first_gain"], vectors["first_beta"], vectors["second_gain"], vectors["second_beta"], vectors["down_bias"],
        xhat, *cts, output_w, q, k, v, short_p, long_p, mixed_t, packed_w,
    )


def local(
    short_input, short_lengths, short_cotangent, long_input, long_lengths, long_cotangent,
    packed_weight, output_weight, inner_weight, down_weight,
    first_gain, second_gain, query_bias, value_bias, output_bias, inner_bias, down_bias, first_beta, second_beta,
):
    short_seqs, short_len, width = short_input.shape
    long_seqs, long_len, _ = long_input.shape
    shape = (short_seqs, short_len, long_seqs, long_len)
    lengths = (short_lengths, long_lengths)
    vectors = dict(
        first_gain=first_gain, second_gain=second_gain, query_bias=query_bias, value_bias=value_bias,
        output_bias=output_bias, inner_bias=inner_bias, down_bias=down_bias, first_beta=first_beta, second_beta=second_beta,
    )
    vectors = {name: item.reshape(1, -1) for name, item in vectors.items()}
    xs = (short_input.reshape(-1, width), long_input.reshape(-1, width))
    cts = (short_cotangent.reshape(-1, width), long_cotangent.reshape(-1, width))
    weights = gather_weights(packed_weight, output_weight, inner_weight, down_weight)
    attention = attention_forward(shape, lengths, xs, weights, vectors)
    keep = jnp.concatenate([
        (jnp.arange(item.shape[1])[None, :] < length[:, None]).reshape(-1, 1)
        for item, length in ((short_input, short_lengths), (long_input, long_lengths))
    ], axis=0).astype(F32)
    short_out, long_out, short_grad, long_grad, sums = feed_and_attention_backward(
        shape, keep, attention, cts, weights["feed"], vectors
    )
    sums = sum_all(sums).reshape(-1)
    outs = []
    at = 0
    for size in (width, width, width, inner_bias.shape[0], width, width, width):
        outs.append(lax.slice_in_dim(sums, at, at + size))
        at += size
    return (
        short_out.reshape(short_input.shape), short_grad.reshape(short_input.shape),
        long_out.reshape(long_input.shape), long_grad.reshape(long_input.shape), *outs,
    )


def exchange(block, mask):
    count = lax.axis_size("dp")
    return lax.ppermute(block, "dp", [(i, i ^ mask(i)) for i in range(count)])


CORE, X, Y, Z_NEAR, Z_FAR = 1, 2, 4, 8, 16


def side_first(index):
    return X if index & CORE == 0 else Y


def side_second(index):
    return Y if index & CORE == 0 else X


def gather_by_exchange(shard):
    held = jnp.concatenate([shard, exchange(shard, lambda i: Z_FAR)])
    held = jnp.concatenate([held, exchange(held, side_first)])
    held = jnp.concatenate([held, exchange(held, lambda i: Z_NEAR)])
    other = exchange(held, side_second)
    return [held, other, exchange(held, lambda i: CORE), exchange(other, lambda i: CORE)]


def exchange_slots():
    def mask(core, swap, far, slot):
        owner = core ^ swap
        return (
            swap * CORE + far * side_second(owner) + Z_FAR * (slot & 1)
            + side_first(owner) * (slot >> 1 & 1) + Z_NEAR * (slot >> 2)
        )

    return [
        [(mask(0, swap, far, slot), mask(1, swap, far, slot)) for slot in range(8)]
        for swap in (0, 1) for far in (0, 1)
    ]


def pack_kernel(inner, down, out):
    tall, width = inner.shape[0], down.shape[1]
    blocks = inner.shape[1] // width
    for i in range(blocks):
        out[i * tall : (i + 1) * tall, :] = inner[:, i * width : (i + 1) * width]
    out[blocks * tall :, :] = down[...]


def pack_rows(inner, down):
    width = down.shape[1]
    rows = inner.shape[1] // width * inner.shape[0] + down.shape[0]
    return pl.pallas_call(
        pack_kernel, out_shape=jax.ShapeDtypeStruct((rows, width), inner.dtype), name="pack_rows"
    )(inner, down)


def gather_weights(packed, output, inner, down):
    count = lax.axis_size("dp")
    width = output.shape[1]
    half = width // 2
    sides = [
        jnp.concatenate([packed[:, i * width + at : i * width + at + half] for i in range(3)], axis=1) for at in (0, half)
    ]
    parts = [*sides, output]
    tall = inner.shape[0]
    blocks = inner.shape[1] // width
    if count == 32:
        feed = lax.all_gather(pack_rows(inner, down), "dp", axis=0, tiled=False)
        gathered = [gather_by_exchange(part) for part in parts]
        return dict(
            me=lax.axis_index("dp").reshape(1).astype(jnp.int32), slots=exchange_slots(),
            pieces=[gathered[part][piece] for piece in range(4) for part in range(3)], feed=feed,
        )
    whole = [lax.all_gather(part, "dp", axis=0, tiled=True) for part in (*parts, inner, down)]
    shards = 32
    feed = jnp.concatenate(
        [
            whole[3].reshape(shards, -1, blocks, width).transpose(0, 2, 1, 3).reshape(shards, -1, width),
            whole[4].reshape(shards, -1, width),
        ],
        axis=1,
    )
    return dict(me=jnp.zeros((1,), jnp.int32), slots=[[(i, i) for i in range(shards)]], pieces=whole[:3], feed=feed)


def sum_all(vector):
    count = lax.axis_size("dp")
    if count & (count - 1):
        return lax.psum(vector, "dp")
    vector = vector + exchange(vector, lambda i: 1) if count > 1 else vector
    bit = 2
    while bit < count:
        near = exchange(vector, lambda i: bit)
        if 2 * bit < count:
            far = exchange(vector, lambda i: 2 * bit)
            both = exchange(vector, lambda i: 3 * bit)
            vector = (vector + near) + (far + both)
        else:
            vector = vector + near
        bit *= 4
    return vector


def solution(mesh):
    rows = P("dp", None, None)
    in_specs = (rows, P("dp"), rows, rows, P("dp"), rows) + (P("dp", None),) * 4 + (P(),) * 9
    out_specs = (rows,) * 4 + (P(),) * 7
    return jax.shard_map(local, mesh=mesh, in_specs=in_specs, out_specs=out_specs, check_vma=False)
```

```python
from functools import partial

import jax
import jax.numpy as jnp
from jax import lax
from jax.experimental import pallas as pl
from jax.experimental.pallas import tpu as pltpu
from jax.sharding import PartitionSpec as P

HEADS = 16
HEAD_DIM = 64
BF = jnp.bfloat16
F32 = jnp.float32
VMEM_BYTES = 60 * 1024 * 1024
FEED_BLOCK = 1024
TAIL_VMEM_BYTES = 63 * 1024 * 1024


def dot(left, right):
    return lax.dot_general(left, right, (((1,), (0,)), ((), ())), preferred_element_type=F32)


def dot_t(left, right):
    return lax.dot_general(left, right, (((1,), (1,)), ((), ())), preferred_element_type=F32)


def sequences(short_seqs, short_len, long_seqs, long_len):
    spans = [(i * short_len, short_len) for i in range(short_seqs)]
    base = short_seqs * short_len
    return spans, [(base + i * long_len, long_len) for i in range(long_seqs)]


def row_mask(short_lengths, long_lengths, shape):
    short_seqs, short_len, long_seqs, long_len = shape
    pieces = []
    for count, length, refs in (
        (short_seqs, short_len, short_lengths),
        (long_seqs, long_len, long_lengths),
    ):
        for i in range(count):
            rows = lax.broadcasted_iota(jnp.int32, (length, 1), 0)
            pieces.append(jnp.where(rows < refs[i], 1.0, 0.0).astype(F32))
    return jnp.concatenate(pieces, axis=0)


def head_lanes(block, half):
    lanes = lax.broadcasted_iota(jnp.int32, block.shape, 1)
    keep = lanes < HEAD_DIM if half == 0 else lanes >= HEAD_DIM
    return jnp.where(keep, block, jnp.zeros_like(block))


def flip(block):
    return jnp.transpose(block, (1, 0))


def attention_forward_kernel(
    shape, slots, me, short_lengths, long_lengths, short_x, long_x, *refs,
):
    pieces, refs = refs[: 3 * len(slots)], refs[3 * len(slots) :]
    (
        qb, vb, ob, gain1, beta1, q_out, k_out, v_out, short_p, long_p, mixed_t, xhat_out, rstd_out, first_out,
        packed_out, output_out,
        x_all, mixed, packed, wo, in_sems, out_sems,
    ) = refs
    step = pl.program_id(0)
    steps = pl.num_programs(0)
    short_seqs, short_len, long_seqs, long_len = shape
    base = short_seqs * short_len
    width = q_out.shape[1]
    half_width = packed.shape[2]
    short_spans, long_spans = sequences(*shape)
    targets = (packed.at[0], packed.at[1], wo)

    @pl.when(step == 0)
    def _():
        for part in range(3):
            for ref, masks in zip(pieces[part::3], slots):
                tall = ref.shape[0] // len(masks)
                for slot, mask in enumerate(masks):
                    mask = jnp.where(jnp.bitwise_and(me[0], 1) == 0, mask[0], mask[1])
                    place = pl.multiple_of(jnp.bitwise_xor(me[0], mask) * tall, tall)
                    pltpu.make_async_copy(
                        ref.at[pl.ds(slot * tall, tall)], targets[part].at[pl.ds(place, tall)], in_sems.at[part]
                    ).start()
        x_all[:base, :] = short_x[...]
        x_all[base:, :] = long_x[...]

    keeps = [
        pltpu.make_async_copy(packed.at[0], packed_out.at[0], out_sems.at[0]),
        pltpu.make_async_copy(packed.at[1], packed_out.at[1], out_sems.at[1]),
        pltpu.make_async_copy(wo, output_out, out_sems.at[2]),
    ]
    for part, first_step in enumerate((0, steps // 2, steps - 1)):
        @pl.when(step == first_step)
        def _():
            pltpu.make_async_copy(targets[part], targets[part], in_sems.at[part]).wait()
            keeps[part].start()

    x = x_all[...]
    side = step // (steps // 2)
    turn = lax.rem(step, steps // 2)
    third = half_width // 3
    weight = lambda which: packed[side, :, pl.ds(pl.multiple_of(which * third + turn * width, width), width)]
    q_out[...] = ((dot(x, weight(0)) + qb[...]).astype(BF).astype(F32) * HEAD_DIM ** (-0.5)).astype(BF)
    k_out[...] = dot(x, weight(1)).astype(BF)
    v_out[...] = (dot(x, weight(2)) + vb[...]).astype(BF)
    groups = ((short_spans, short_lengths, short_p), (long_spans, long_lengths, long_p))
    pairs = range(width // 128)
    jobs = []
    for pair in pairs:
        lanes = slice(128 * pair, 128 * pair + 128)
        for spans, refs, probs in groups:
            for seq, (start, length) in enumerate(spans):
                k2 = k_out[start : start + length, lanes]
                usable = lax.broadcasted_iota(jnp.int32, (length, 1), 0) < refs[seq]
                block = min(length, 512)
                for half in range(2):
                    for at in range(0, length, block):
                        jobs.append(dict(pair=pair, probs=probs, seq=seq, start=start, length=length, usable=usable, half=half, at=at, block=block, lanes=lanes,
                            scores=dot_t(head_lanes(k2, half), q_out[start + at : start + at + block, lanes])))
    for job in jobs:
        scores = jnp.where(job["usable"], job["scores"], -1e30)
        top = jnp.max(scores, axis=0, keepdims=True)
        powers = jnp.exp(scores - top)
        total = jnp.sum(powers, axis=0, keepdims=True)
        job["prob"] = (powers * (1.0 / total)).astype(BF)
        job["probs"][job["seq"], 2 * job["pair"] + job["half"], :, job["at"] : job["at"] + job["block"]] = job["prob"]

    flipped = {pair: flip(v_out[:, 128 * pair : 128 * pair + 128]) for pair in pairs}
    for job in jobs:
        feature = 128 * job["pair"] + HEAD_DIM * job["half"]
        v_head = flipped[job["pair"]][HEAD_DIM * job["half"] : HEAD_DIM * job["half"] + HEAD_DIM, job["start"] : job["start"] + job["length"]]
        mixed_t[feature : feature + HEAD_DIM, job["start"] + job["at"] : job["start"] + job["at"] + job["block"]] = dot(v_head, job["prob"])
    for pair in pairs:
        offset = pl.multiple_of(step * width + 128 * pair, 128)
        mixed[:, pl.ds(offset, 128)] = flip(mixed_t[128 * pair : 128 * pair + 128, :]).astype(BF)

    @pl.when(step == steps - 1)
    def _():
        first_sum = x_all[...].astype(F32) + (dot(mixed[...], wo[...]) + ob[...])
        center = first_sum - jnp.mean(first_sum, axis=-1, keepdims=True)
        spread = jnp.mean(center * center, axis=-1, keepdims=True)
        rstd = lax.rsqrt(spread + 1e-06)
        xhat = center * rstd
        xhat_out[...] = xhat
        rstd_out[...] = rstd
        first_out[...] = (xhat * gain1[...] + beta1[...]).astype(BF)
        for keep in keeps:
            keep.wait()


def attention_forward(shape, lengths, xs, weights, vectors):
    short_seqs, short_len, long_seqs, long_len = shape
    rows = short_seqs * short_len + long_seqs * long_len
    width = xs[0].shape[1]
    block = 256
    heads = block // HEAD_DIM
    steps = width // block
    whole = lambda shp: pl.BlockSpec(shp, lambda j: (0,) * len(shp))
    smem = pl.BlockSpec(memory_space=pltpu.SMEM)
    anywhere = pl.BlockSpec(memory_space=pl.ANY)
    row_block = pl.BlockSpec((1, block), lambda j: (0, j))
    out_col = pl.BlockSpec((rows, block), lambda j: (0, j))
    half_width = 3 * width // 2
    return pl.pallas_call(
        partial(attention_forward_kernel, shape, weights["slots"]),
        grid=(steps,),
        in_specs=[
            smem, smem, smem, whole(xs[0].shape), whole(xs[1].shape),
            *[anywhere] * len(weights["pieces"]), row_block, row_block, *[whole((1, width))] * 3,
        ],
        out_specs=[
            out_col, out_col, out_col,
            pl.BlockSpec((short_seqs, heads, short_len, short_len), lambda j: (0, j, 0, 0)),
            pl.BlockSpec((long_seqs, heads, long_len, long_len), lambda j: (0, j, 0, 0)),
            pl.BlockSpec((block, rows), lambda j: (j, 0)),
            whole((rows, width)), whole((rows, 1)), whole((rows, width)), anywhere, anywhere,
        ],
        out_shape=[
            jax.ShapeDtypeStruct((rows, width), BF),
            jax.ShapeDtypeStruct((rows, width), BF),
            jax.ShapeDtypeStruct((rows, width), BF),
            jax.ShapeDtypeStruct((short_seqs, HEADS, short_len, short_len), BF),
            jax.ShapeDtypeStruct((long_seqs, HEADS, long_len, long_len), BF),
            jax.ShapeDtypeStruct((width, rows), F32),
            jax.ShapeDtypeStruct((rows, width), F32),
            jax.ShapeDtypeStruct((rows, 1), F32),
            jax.ShapeDtypeStruct((rows, width), BF),
            jax.ShapeDtypeStruct((2, width, half_width), BF),
            jax.ShapeDtypeStruct((width, width), BF),
        ],
        scratch_shapes=[
            pltpu.VMEM((rows, width), BF), pltpu.VMEM((rows, width), BF),
            pltpu.VMEM((2, width, half_width), BF), pltpu.VMEM((width, width), BF),
            pltpu.SemaphoreType.DMA((3,)), pltpu.SemaphoreType.DMA((3,)),
        ],
        compiler_params=pltpu.CompilerParams(vmem_limit_bytes=VMEM_BYTES),
        cost_estimate=pl.CostEstimate(flops=36 * 10**9, bytes_accessed=40 * 10**6, transcendentals=5 * 10**6),
        name="attention_forward",
    )(
        weights["me"], *lengths, *xs, *weights["pieces"],
        vectors["query_bias"], vectors["value_bias"], vectors["output_bias"],
        vectors["first_gain"], vectors["first_beta"],
    )


def gelu_and_slope(value):
    share = 0.5 + 0.5 * lax.erf(value * 0.5 ** 0.5)
    density = jnp.exp2(value * (value * -0.7213475204444817)) * 0.3989422804014327
    return value * share, share + value * density


def inner_block(feed_w, block, turn):
    shards, _, width = feed_w.shape
    per = width // block
    return pl.BlockSpec((shards, width // shards, block), lambda j: (0, turn(j) // per, lax.rem(turn(j), per)))


def down_block(feed_w, block, turn):
    shards, tall, width = feed_w.shape
    tall = tall // 2
    return pl.BlockSpec((block // tall, tall, width), lambda j: (turn(j), 1, 0))


def norm_gradient(grad, xhat, rstd, gain):
    scaled = grad * gain
    mean = jnp.mean(scaled, axis=-1, keepdims=True)
    along = jnp.mean(scaled * xhat, axis=-1, keepdims=True)
    return rstd * (scaled - mean - xhat * along)


def fold(block):
    return jnp.sum(block.reshape(block.shape[0] // 8, 8, block.shape[1]), axis=0)


def tail_kernel(
    shape, steps, keep, rstd, first, wi, wd, inner_bias, gain1, beta1, gain2, beta2, down_bias,
    xhat_in, short_ct, long_ct, wo_in, q_in, k_in, v_in, short_p_in, long_p_in, mixed_t_in, packed_in,
    short_out, long_out, short_grad, long_grad, sums_out,
    total, low, value, slope, sums, inner_fold, xhat, ct, wo, short_p, long_p, mixed_t, packed, gm, sems, load_sems,
):
    step = pl.program_id(0)
    short_seqs, short_len, long_seqs, long_len = shape
    base = short_seqs * short_len
    rows, width = total.shape
    units = steps * value.shape[2]
    part = packed.shape[2] // 3
    attention_steps = width // part
    heads = part // HEAD_DIM
    first_attention = 2 * steps + 1
    turn = step - first_attention
    slot = lax.rem(jnp.maximum(turn, 0), 2)
    chunk = 224 if rows % 224 == 0 else 128
    wide = lambda ref: ref[...].reshape(width, -1)
    tall = lambda ref: ref[...].reshape(-1, width)
    short_spans, long_spans = sequences(*shape)

    early = [
        pltpu.make_async_copy(short_ct, ct.at[:base], sems.at[0]),
        pltpu.make_async_copy(long_ct, ct.at[base:], sems.at[1]),
        pltpu.make_async_copy(xhat_in, xhat, sems.at[2]),
        pltpu.make_async_copy(wo_in, wo, sems.at[3]),
    ]
    outs = [
        pltpu.make_async_copy(ct.at[:base], short_out, sems.at[4]),
        pltpu.make_async_copy(ct.at[base:], long_out, sems.at[5]),
    ]
    grads = [
        pltpu.make_async_copy(low.at[:base], short_grad, sems.at[6]),
        pltpu.make_async_copy(low.at[base:], long_grad, sems.at[7]),
    ]

    def loads(at, into):
        columns = pl.ds(pl.multiple_of(at * part, part), part)
        side = at // (attention_steps // 2)
        within = lax.rem(at, attention_steps // 2)
        third = packed_in.shape[2] // 3
        pairs = [(ref.at[:, columns], slope.at[3 - into, :, part * i : part * i + part]) for i, ref in enumerate((q_in, k_in, v_in))]
        pairs += [
            (short_p_in.at[:, pl.ds(at * heads, heads)], short_p.at[into]),
            (long_p_in.at[:, pl.ds(at * heads, heads)], long_p.at[into]),
            (mixed_t_in.at[columns], mixed_t.at[into]),
        ]
        pairs += [
            (
                packed_in.at[side, :, pl.ds(pl.multiple_of(i * third + within * part, part), part)],
                packed.at[into, :, part * i : part * i + part],
            )
            for i in range(3)
        ]
        return [pltpu.make_async_copy(a, b, load_sems.at[into, i]) for i, (a, b) in enumerate(pairs)]

    def first_part():
        value[lax.rem(step, 2)] = dot(first[...], wide(wi)) + inner_bias[...]

    def second_part():
        act, slp = gelu_and_slope(value[lax.rem(step + 1, 2)])
        slope[step - 1] = slp.astype(BF)
        total[...] += dot(act.astype(BF), tall(wd))

    @pl.when(step == 0)
    def _():
        for copy in early:
            copy.start()
        first_part()
        total[...] = jnp.broadcast_to(down_bias[...], total.shape)

    @pl.when((step > 0) & (step < steps))
    def _():
        first_part()
        second_part()

    @pl.when(step == steps)
    def _():
        for copy in early[:3]:
            copy.wait()
        second_part()
        sums[...] = jnp.zeros_like(sums)

        def body(i, _):
            here = pl.ds(pl.multiple_of(i * chunk, chunk), chunk)
            second = total[here, :] + (xhat[here, :] * gain1[...] + beta1[...])
            center = second - jnp.mean(second, axis=-1, keepdims=True)
            spread = jnp.mean(center * center, axis=-1, keepdims=True)
            rstd2 = lax.rsqrt(spread + 1e-06)
            xhat2 = center * rstd2
            usable = keep[here, :]
            grad_out = ct[here, :].astype(F32) * usable
            ct[here, :] = ((xhat2 * gain2[...] + beta2[...]) * usable).astype(BF)
            grad_second = norm_gradient(grad_out, xhat2, rstd2, gain2[...])
            rounded = grad_second.astype(BF)
            low[here, :] = rounded
            total[here, :] = grad_second
            sums[0] += fold(grad_out)
            sums[1] += fold(rounded.astype(F32))
            return 0

        lax.fori_loop(0, rows // chunk, body, 0)
        for copy in outs:
            copy.start()
        sums_out[:, 5 * width + units : 6 * width + units] = jnp.sum(sums[0], axis=0, keepdims=True)
        sums_out[:, 3 * width + units : 4 * width + units] = jnp.sum(sums[1], axis=0, keepdims=True)

    @pl.when((step > steps) & (step < 2 * steps))
    def _():
        grad_inner = (dot_t(low[...], tall(wd)) * slope[2 * steps - step].astype(F32)).astype(BF)
        place = pl.multiple_of(3 * width + (2 * steps - step) * wd.shape[0] * wd.shape[1], 128)
        sums_out[:, pl.ds(place, value.shape[2])] = jnp.sum(grad_inner.astype(F32), axis=0, keepdims=True)
        total[...] += dot_t(grad_inner, wide(wi))

    @pl.when(step == 2 * steps - 1)
    def _():
        for copy in loads(0, 0):
            copy.start()

    @pl.when(step == 2 * steps)
    def _():
        for copy in loads(1, 1):
            copy.start()
        early[3].wait()
        sums[...] = jnp.zeros_like(sums)
        inner_fold[...] = jnp.zeros_like(inner_fold)
        chunks = [slice(at, at + rows // 2) for at in range(0, rows, rows // 2)]
        firsts = {}
        for turn_of in range(len(chunks) + 2):
            if turn_of < len(chunks):
                ahead = chunks[turn_of]
                grad_active = dot_t(low[ahead], tall(wd))
            if turn_of >= 2:
                back_here = chunks[turn_of - 2]
                mixed_grad = dot_t(low[back_here], wo[...])
            if 0 < turn_of <= len(chunks):
                here = chunks[turn_of - 1]
                grad_first = firsts.pop(turn_of - 1)
                result = norm_gradient(grad_first, xhat[here], rstd[here], gain1[...])
                total[here] = result
                branch = result.astype(BF)
                low[here] = branch
                sums[0] += fold(grad_first)
                sums[1] += fold(branch.astype(F32))
            if turn_of < len(chunks):
                grad_inner = (grad_active * slope[0, ahead].astype(F32)).astype(BF)
                firsts[turn_of] = total[ahead] + dot_t(grad_inner, wide(wi))
                inner_fold[...] += fold(grad_inner.astype(F32))
            if turn_of >= 2:
                gm[back_here] = mixed_grad.astype(BF)
        sums_out[:, 4 * width + units : 5 * width + units] = jnp.sum(sums[0], axis=0, keepdims=True)
        sums_out[:, 2 * width : 3 * width] = jnp.sum(sums[1], axis=0, keepdims=True)
        sums_out[:, 3 * width : 3 * width + value.shape[2]] = jnp.sum(inner_fold[...], axis=0, keepdims=True)

    @pl.when(turn >= 0)
    def _():
        for copy in loads(turn, slot):
            copy.wait()
        scale = HEAD_DIM ** (-0.5)
        own = 3 - slot
        q = lambda here, lanes: slope[own, here, lanes]
        k = lambda here, lanes: slope[own, here, slice(part + lanes.start, part + lanes.stop)]
        v = lambda here, lanes: slope[own, here, slice(2 * part + lanes.start, 2 * part + lanes.stop)]
        grad = lambda here, lanes: slope[1, here, slice(3 * part + lanes.start, 3 * part + lanes.stop)]
        slope[1, :, 3 * part : 4 * part] = gm[:, pl.ds(pl.multiple_of(turn * part, part), part)]
        everything = slice(0, rows)
        jobs = []
        for pair in range(part // 128):
            lanes = slice(128 * pair, 128 * pair + 128)
            for spans, probs in ((short_spans, short_p), (long_spans, long_p)):
                for seq, (start, length) in enumerate(spans):
                    here = slice(start, start + length)
                    for half in range(2):
                        jobs.append(dict(
                            pair=pair, here=here, lanes=lanes, half=half, probs=probs, seq=seq,
                            grad_p=dot_t(head_lanes(v(here, lanes), half), grad(here, lanes)),
                        ))
        flipped, delta = {}, {}
        for pair in range(part // 128):
            lanes = slice(128 * pair, 128 * pair + 128)
            flipped[pair] = flip(k(everything, lanes))
            product = flip(grad(everything, lanes)).astype(F32) * mixed_t[slot, lanes, :]
            for half in range(2):
                delta[pair, half] = jnp.sum(product[HEAD_DIM * half : HEAD_DIM * half + HEAD_DIM], axis=0, keepdims=True)
        for job in jobs:
            pair, half = job["pair"], job["half"]
            prob = job["probs"][slot, job["seq"], 2 * pair + half].astype(F32)
            job["grad_s"] = (prob * (job["grad_p"] - delta[pair, half][:, job["here"]])).astype(BF)
        for one, two in zip(jobs[0::2], jobs[1::2]):
            pair, here, lanes = one["pair"], one["here"], one["lanes"]
            probs2 = [job["probs"][slot, job["seq"], 2 * pair + job["half"]] for job in (one, two)]
            grad_value = dot(
                jnp.concatenate(probs2, axis=1),
                jnp.concatenate([head_lanes(grad(here, lanes), half) for half in range(2)], axis=0),
            )
            grad_key = dot(
                jnp.concatenate([one["grad_s"], two["grad_s"]], axis=1),
                jnp.concatenate([head_lanes(q(here, lanes), half) for half in range(2)], axis=0),
            )
            k_t = flipped[pair][:, here]
            first_head = lax.broadcasted_iota(jnp.int32, k_t.shape, 0) < HEAD_DIM
            zero = jnp.zeros_like(k_t)
            grad_query_t = dot(
                jnp.concatenate([jnp.where(first_head, k_t, zero), jnp.where(first_head, zero, k_t)], axis=1),
                jnp.concatenate([one["grad_s"], two["grad_s"]], axis=0),
            )
            slope[1, here, 128 * pair : 128 * pair + 128] = (flip(grad_query_t) * scale).astype(BF)
            slope[1, here, part + 128 * pair : part + 128 * pair + 128] = grad_key.astype(BF)
            slope[1, here, 2 * part + 128 * pair : 2 * part + 128 * pair + 128] = grad_value.astype(BF)
        place = pl.multiple_of(turn * part, part)
        sums_out[:, pl.ds(place, part)] = jnp.sum(slope[1, :, :part].astype(F32), axis=0, keepdims=True)
        sums_out[:, pl.ds(width + place, part)] = jnp.sum(slope[1, :, 2 * part : 3 * part].astype(F32), axis=0, keepdims=True)
        total[...] += dot_t(slope[1, :, : 3 * part], packed[slot])

    @pl.when((turn >= 0) & (turn < attention_steps - 2))
    def _():
        for copy in loads(turn + 2, slot):
            copy.start()

    @pl.when(turn == attention_steps - 1)
    def _():
        low[...] = (total[...] * keep[...]).astype(BF)
        for copy in grads:
            copy.start()
        for copy in outs + grads:
            copy.wait()


def feed_and_attention_backward(shape, keep, attention, cts, feed_w, vectors, block=FEED_BLOCK):
    q, k, v, short_p, long_p, mixed_t, xhat, rstd, first, packed_w, output_w = attention
    short_seqs, short_len, long_seqs, long_len = shape
    rows, width = xhat.shape
    base = short_seqs * short_len
    units = vectors["inner_bias"].shape[1]
    steps = units // block
    part = 256
    heads = part // HEAD_DIM
    once = pl.Buffered(1)
    whole = lambda shp: pl.BlockSpec(shp, lambda j: (0,) * len(shp), pipeline_mode=once)
    vec = whole((1, width))
    anywhere = pl.BlockSpec(memory_space=pl.ANY)
    back = lambda j: jnp.maximum(2 * steps - j, 0)
    inner_turn = lambda j: jnp.where(j <= steps, jnp.minimum(j, steps - 1), back(j))
    down_turn = lambda j: jnp.where(j <= steps, jnp.maximum(j - 1, 0), back(j))
    total_width = 6 * width + units
    return pl.pallas_call(
        partial(tail_kernel, shape, steps),
        grid=(2 * steps + 1 + width // part,),
        in_specs=[
            whole((rows, 1)), whole((rows, 1)), whole((rows, width)),
            inner_block(feed_w, block, inner_turn), down_block(feed_w, block, down_turn),
            pl.BlockSpec((1, block), lambda j: (0, jnp.minimum(j, steps - 1))), vec, vec, vec, vec, vec,
            *[anywhere] * 11,
        ],
        out_specs=[anywhere] * 4 + [pl.BlockSpec((1, total_width), lambda j: (0, 0))],
        out_shape=[
            jax.ShapeDtypeStruct(cts[0].shape, BF), jax.ShapeDtypeStruct(cts[1].shape, BF),
            jax.ShapeDtypeStruct(cts[0].shape, BF), jax.ShapeDtypeStruct(cts[1].shape, BF),
            jax.ShapeDtypeStruct((1, total_width), F32),
        ],
        scratch_shapes=[
            pltpu.VMEM((rows, width), F32), pltpu.VMEM((rows, width), BF), pltpu.VMEM((2, rows, block), F32),
            pltpu.VMEM((steps, rows, block), BF), pltpu.VMEM((2, 8, width), F32), pltpu.VMEM((8, block), F32),
            pltpu.VMEM((rows, width), F32), pltpu.VMEM((rows, width), BF), pltpu.VMEM((width, width), BF),
            pltpu.VMEM((2, short_seqs, heads, short_len, short_len), BF),
            pltpu.VMEM((2, long_seqs, heads, long_len, long_len), BF),
            pltpu.VMEM((2, part, rows), F32), pltpu.VMEM((2, width, 3 * part), BF), pltpu.VMEM((rows, width), BF),
            pltpu.SemaphoreType.DMA((8,)), pltpu.SemaphoreType.DMA((2, 9)),
        ],
        compiler_params=pltpu.CompilerParams(vmem_limit_bytes=TAIL_VMEM_BYTES),
        cost_estimate=pl.CostEstimate(flops=85 * 10**9, bytes_accessed=90 * 10**6, transcendentals=4 * 10**6),
        name="feed_and_attention_backward",
    )(
        keep, rstd, first, feed_w, feed_w, vectors["inner_bias"],
        vectors["first_gain"], vectors["first_beta"], vectors["second_gain"], vectors["second_beta"], vectors["down_bias"],
        xhat, *cts, output_w, q, k, v, short_p, long_p, mixed_t, packed_w,
    )


def local(
    short_input, short_lengths, short_cotangent, long_input, long_lengths, long_cotangent,
    packed_weight, output_weight, inner_weight, down_weight,
    first_gain, second_gain, query_bias, value_bias, output_bias, inner_bias, down_bias, first_beta, second_beta,
):
    short_seqs, short_len, width = short_input.shape
    long_seqs, long_len, _ = long_input.shape
    shape = (short_seqs, short_len, long_seqs, long_len)
    lengths = (short_lengths, long_lengths)
    vectors = dict(
        first_gain=first_gain, second_gain=second_gain, query_bias=query_bias, value_bias=value_bias,
        output_bias=output_bias, inner_bias=inner_bias, down_bias=down_bias, first_beta=first_beta, second_beta=second_beta,
    )
    vectors = {name: item.reshape(1, -1) for name, item in vectors.items()}
    xs = (short_input.reshape(-1, width), long_input.reshape(-1, width))
    cts = (short_cotangent.reshape(-1, width), long_cotangent.reshape(-1, width))
    weights = gather_weights(packed_weight, output_weight, inner_weight, down_weight)
    attention = attention_forward(shape, lengths, xs, weights, vectors)
    keep = jnp.concatenate([
        (jnp.arange(item.shape[1])[None, :] < length[:, None]).reshape(-1, 1)
        for item, length in ((short_input, short_lengths), (long_input, long_lengths))
    ], axis=0).astype(F32)
    short_out, long_out, short_grad, long_grad, sums = feed_and_attention_backward(
        shape, keep, attention, cts, weights["feed"], vectors
    )
    sums = sum_all(sums.reshape(-1))
    outs = []
    at = 0
    for size in (width, width, width, inner_bias.shape[0], width, width, width):
        outs.append(lax.slice_in_dim(sums, at, at + size))
        at += size
    return (
        short_out.reshape(short_input.shape), short_grad.reshape(short_input.shape),
        long_out.reshape(long_input.shape), long_grad.reshape(long_input.shape), *outs,
    )


def exchange(block, mask):
    count = lax.axis_size("dp")
    return lax.ppermute(block, "dp", [(i, i ^ mask(i)) for i in range(count)])


CORE, X, Y, Z_NEAR, Z_FAR = 1, 2, 4, 8, 16


def side_first(index):
    return X if index & CORE == 0 else Y


def side_second(index):
    return Y if index & CORE == 0 else X


def gather_by_exchange(shard):
    held = jnp.concatenate([shard, exchange(shard, lambda i: Z_FAR)])
    held = jnp.concatenate([held, exchange(held, side_first)])
    held = jnp.concatenate([held, exchange(held, lambda i: Z_NEAR)])
    other = exchange(held, side_second)
    return [held, other, exchange(held, lambda i: CORE), exchange(other, lambda i: CORE)]


def exchange_slots():
    def mask(core, swap, far, slot):
        owner = core ^ swap
        return (
            swap * CORE + far * side_second(owner) + Z_FAR * (slot & 1)
            + side_first(owner) * (slot >> 1 & 1) + Z_NEAR * (slot >> 2)
        )

    return [
        [(mask(0, swap, far, slot), mask(1, swap, far, slot)) for slot in range(8)]
        for swap in (0, 1) for far in (0, 1)
    ]


def pack_kernel(inner, down, out):
    tall, width = inner.shape[0], down.shape[1]
    blocks = inner.shape[1] // width
    for i in range(blocks):
        out[i * tall : (i + 1) * tall, :] = inner[:, i * width : (i + 1) * width]
    out[blocks * tall :, :] = down[...]


def pack_rows(inner, down):
    width = down.shape[1]
    rows = inner.shape[1] // width * inner.shape[0] + down.shape[0]
    return pl.pallas_call(
        pack_kernel, out_shape=jax.ShapeDtypeStruct((rows, width), inner.dtype), name="pack_rows"
    )(inner, down)


def gather_weights(packed, output, inner, down):
    count = lax.axis_size("dp")
    width = output.shape[1]
    half = width // 2
    sides = [
        jnp.concatenate([packed[:, i * width + at : i * width + at + half] for i in range(3)], axis=1) for at in (0, half)
    ]
    parts = [*sides, output]
    tall = inner.shape[0]
    blocks = inner.shape[1] // width
    if count == 32:
        feed = lax.all_gather(pack_rows(inner, down), "dp", axis=0, tiled=False)
        gathered = [gather_by_exchange(part) for part in parts]
        return dict(
            me=lax.axis_index("dp").reshape(1).astype(jnp.int32), slots=exchange_slots(),
            pieces=[gathered[part][piece] for piece in range(4) for part in range(3)], feed=feed,
        )
    whole = [lax.all_gather(part, "dp", axis=0, tiled=True) for part in (*parts, inner, down)]
    shards = 32
    feed = jnp.concatenate(
        [
            whole[3].reshape(shards, -1, blocks, width).transpose(0, 2, 1, 3).reshape(shards, -1, width),
            whole[4].reshape(shards, -1, width),
        ],
        axis=1,
    )
    return dict(me=jnp.zeros((1,), jnp.int32), slots=[[(i, i) for i in range(shards)]], pieces=whole[:3], feed=feed)


def sum_all(vector):
    count = lax.axis_size("dp")
    if count & (count - 1):
        return lax.psum(vector, "dp")
    vector = vector + exchange(vector, lambda i: 1) if count > 1 else vector
    bit = 2
    while bit < count:
        near = exchange(vector, lambda i: bit)
        if 2 * bit < count:
            far = exchange(vector, lambda i: 2 * bit)
            both = exchange(vector, lambda i: 3 * bit)
            vector = (vector + near) + (far + both)
        else:
            vector = vector + near
        bit *= 4
    return vector


def solution(mesh):
    rows = P("dp", None, None)
    in_specs = (rows, P("dp"), rows, rows, P("dp"), rows) + (P("dp", None),) * 4 + (P(),) * 9
    out_specs = (rows,) * 4 + (P(),) * 7
    return jax.shard_map(local, mesh=mesh, in_specs=in_specs, out_specs=out_specs, check_vma=False)
```
